32 devices in a mesh: contact: 8 (over y, x, core), body: 4 (over z).
Axes of the slice: x: 2, y: 2, z: 4, core: 2. Of those that a mesh axis runs over, the one named last changes fastest.
Arguments:
- jacobian: bfloat16 [512, 2, 384, 384], P(('contact', 'body')), may hold values from -0.21875 to 0.21875
- tile_block: int32 [512, 2], P(('contact', 'body')), may hold values from 0 to 31
- tile_count: int32 [32], P(('contact', 'body')), may hold values from 8 to 16, as said below
- vel_free: float32 [128, 384], P('body'), may hold values from -6 to 6
- inv_mass: float32 [128, 384], P('body'), may hold values from 0.25 to 2
- bias: float32 [512, 384], P(('contact', 'body')), may hold values from -6 to 6
- step_scale: float32 [512, 384], P(('contact', 'body')), may hold values from 0.05 to 0.5
- friction: float32 [512, 128], P(('contact', 'body')), may hold values from 0.2 to 1
- impulse_start: float32 [512, 384], P(('contact', 'body')), may hold values from -6 to 6
Outputs:
- impulse: float32 [512, 384], P(('contact', 'body'))
- velocity: float32 [128, 384], P('body')
The draws below stay inside these ranges and needn't reach their ends.
Inputs may be any that keep to these rules, and one draw needn't show every extreme that they name: `tile_count`: some device has all 16 tile slots live in every draw.
All inputs are finite; a program needn't handle non-finite values.
Results may differ from the reference program's by a relative error of at most 0.0062.
Values may be sent and summed in bfloat16 or wider, within the bound.
No kernel may reach another device: no remote copies, remote signals or barrier semaphores. Data moves between devices by JAX's collectives and lax.ppermute only.
A program may use at most 64 MiB of HBM per device.

```python
import math
import jax
import jax.numpy as jnp
from jax import lax

TC = 128
TILES_DEV = 16
SLAB_BLK = 32
ITERS = 2
CROW = 384
BDOF = 384
NDEV = 32
TILES = 512
NBLK = 128
N_BODY = 4


def draw_tile_count(key, part):
    devices = TILES // TILES_DEV
    first_key, second_key = jax.random.split(jax.random.fold_in(key, 17))
    counts = jax.random.randint(first_key, (devices,), TILES_DEV // 2, TILES_DEV + 1)
    fullest = jax.random.randint(second_key, (), 0, devices)
    return jnp.where(jnp.arange(devices) == fullest, TILES_DEV, counts).astype(jnp.int32)


def touch_ends(drawn, rng, low, high):
    place = [jax.random.randint(jax.random.fold_in(rng, axis), (), 0, length) for axis, length in enumerate(drawn.shape)]
    widest = drawn.shape.index(max(drawn.shape))
    beside = place[:widest] + [(place[widest] + 1) % drawn.shape[widest]] + place[widest + 1:]
    return drawn.at[tuple(place)].set(low).at[tuple(beside)].set(high)


def steps_of(stream_key, extent, cuts, least, top_value):
    level, own = 1.0, jax.random.fold_in(stream_key, 6)
    for position, blocks in cuts:
        steps = jnp.exp(jax.random.uniform(jax.random.fold_in(own, position), (blocks,), jnp.float32, least / len(cuts), top_value / len(cuts)))
        level = level * jnp.repeat(steps, extent[position] // blocks).reshape([-1 if axis == position else 1 for axis in range(len(extent))])
    return level


def noise(rng, extent, deviation, bound, shards=(), kind=jnp.bfloat16):
    entries = deviation * jax.random.normal(rng, extent, jnp.float32)
    if shards:
        entries = entries * steps_of(rng, extent, shards, -0.22, 0.18)
    return jnp.clip(entries, -bound, bound).astype(kind)


def setup_inputs(seed: int = 0) -> dict:
    splits = jax.random.split(jax.random.key(seed), 10)
    return {
        "jacobian": noise(splits[0], (TILES, 2, BDOF, CROW), (2 * BDOF) ** -0.5, 0.21875, ((0, 32),)),
        "tile_block": touch_ends(jax.random.randint(splits[1], (TILES, 2), 0, SLAB_BLK), jax.random.fold_in(splits[1], 1), 0, SLAB_BLK - 1).astype(jnp.int32),
        "tile_count": draw_tile_count(jax.random.fold_in(splits[9], 71), 0),
        "vel_free": noise(splits[3], (NBLK, BDOF), 1.0, 6.0, ((0, 4),), jnp.float32),
        "inv_mass": jnp.clip(jnp.exp(math.log(2.0) - 2.0794415 * jax.random.uniform(splits[4], (NBLK, BDOF), jnp.float32) ** steps_of(splits[4], (NBLK, BDOF), ((0, 4),), -0.2, 0.2)), 0.25, 2.0),
        "bias": noise(splits[5], (TILES, CROW), 1.0, 6.0, ((0, 32),), jnp.float32),
        "step_scale": jnp.clip(jnp.exp(math.log(0.5) - 2.3025851 * jax.random.uniform(splits[6], (TILES, CROW), jnp.float32) ** steps_of(splits[6], (TILES, CROW), ((0, 32),), -0.2, 0.2)), 0.05, 0.5),
        "friction": jnp.clip(0.2 + 0.8 * jax.random.uniform(splits[7], (TILES, TC), jnp.float32) ** steps_of(splits[7], (TILES, TC), ((0, 32),), -0.2, 0.2), 0.2, 1.0),
        "impulse_start": noise(splits[8], (TILES, CROW), 1.0, 6.0, ((0, 32),), jnp.float32),
    }


def project(trial, friction):
    normal = trial[:, :TC]
    first = trial[:, TC:2 * TC]
    second = trial[:, 2 * TC:]
    tangent = jnp.sqrt(first * first + second * second)
    inside = tangent <= friction * normal
    below = friction * tangent <= -normal
    moved = (normal + friction * tangent) / (1.0 + friction * friction)
    safe = jnp.where(inside | below, 1.0, tangent)
    factor = jnp.where(inside, 1.0, jnp.where(below, 0.0, friction * moved / safe))
    new_normal = jnp.where(inside, normal, jnp.where(below, 0.0, moved))
    return jnp.concatenate([new_normal, first * factor, second * factor], axis=1)

def reference(jacobian, tile_block, tile_count, vel_free, inv_mass, bias, step_scale, friction, impulse_start):
    tile_ids = jnp.arange(TILES, dtype=jnp.int32)
    group = tile_ids // TILES_DEV
    live = tile_ids % TILES_DEV < tile_count[group]
    mask = live.astype(jnp.float32)[:, None]
    slab = group % N_BODY
    block_own = (slab * SLAB_BLK + tile_block[:, 0]).astype(jnp.int32)
    block_next = ((slab + 1) % N_BODY * SLAB_BLK + tile_block[:, 1]).astype(jnp.int32)
    jac_groups = jacobian.reshape(NDEV, TILES_DEV, 2, BDOF, CROW)

    def velocities(lam):
        lamb = lam.astype(jnp.bfloat16).reshape(NDEV, TILES_DEV, CROW)
        push = lax.map(lambda pair: jnp.einsum('tkbc,tc->tkb', pair[0].astype(jnp.float32), pair[1].astype(jnp.float32), precision=lax.Precision.HIGHEST), (jac_groups, lamb))
        push = push.reshape(TILES, 2, BDOF)
        total = jax.ops.segment_sum(push[:, 0], block_own, NBLK) + jax.ops.segment_sum(push[:, 1], block_next, NBLK)
        return vel_free + inv_mass * total

    def relative(vel):
        velb = vel.astype(jnp.bfloat16)
        rows = jnp.stack([velb[block_own], velb[block_next]], axis=1).reshape(NDEV, TILES_DEV, 2, BDOF)
        rel = lax.map(lambda pair: jnp.einsum('tkbc,tkb->tc', pair[0].astype(jnp.float32), pair[1].astype(jnp.float32), precision=lax.Precision.HIGHEST), (jac_groups, rows))
        return rel.reshape(TILES, CROW) + bias
    lam = impulse_start * mask
    for sweep in range(ITERS):
        vel = velocities(lam)
        rel = relative(vel)
        lam = project(lam - step_scale * rel, friction) * mask
    return (lam, velocities(lam))
```

```python
import jax
import jax.numpy as jnp
from jax import lax
from jax.sharding import PartitionSpec as P

ITERS = 2


def shifted(value, axis, steps):
    count = lax.axis_size(axis)
    pairs = [(source, (source + steps) % count) for source in range(count)]
    return lax.ppermute(value, axis, pairs)


def summed(value, axis):
    count = lax.axis_size(axis)
    if count & (count - 1):
        return lax.psum(value, axis)
    bit = 1
    while bit < count:
        pairs = [(source, source ^ bit) for source in range(count)]
        value = value + lax.ppermute(value, axis, pairs)
        bit *= 2
    return value


def project(trial, friction, contacts):
    normal = trial[:, :contacts]
    first = trial[:, contacts : 2 * contacts]
    second = trial[:, 2 * contacts :]
    tangent = jnp.sqrt(first * first + second * second)
    inside = tangent <= friction * normal
    below = friction * tangent <= -normal
    moved = (normal + friction * tangent) / (1.0 + friction * friction)
    safe = jnp.where(inside | below, 1.0, tangent)
    factor = jnp.where(inside, 1.0, jnp.where(below, 0.0, friction * moved / safe))
    new_normal = jnp.where(inside, normal, jnp.where(below, 0.0, moved))
    return jnp.concatenate([new_normal, first * factor, second * factor], axis=1)


def per_device(
    jacobian, tile_block, tile_count, vel_free, inv_mass, bias, step_scale, friction, impulse_start
):
    tiles_here = jacobian.shape[0]
    slab_blocks = vel_free.shape[0]
    contacts = friction.shape[1]
    order = jnp.arange(tiles_here, dtype=jnp.int32)
    mask = (order < tile_count[0]).astype(jnp.float32)[:, None]
    span = jnp.arange(slab_blocks, dtype=jnp.int32)
    pick_own = (tile_block[:, 0:1] == span[None, :]).astype(jnp.float32)
    pick_next = (tile_block[:, 1:2] == span[None, :]).astype(jnp.float32)
    pick_own_b = pick_own.astype(jnp.bfloat16)
    pick_next_b = pick_next.astype(jnp.bfloat16)
    free_pair = jnp.concatenate([vel_free, shifted(vel_free, "body", -1)])
    mass_pair = jnp.concatenate([inv_mass, shifted(inv_mass, "body", -1)])

    def partials(lam):
        lamb = lam.astype(jnp.bfloat16)
        push = jnp.einsum("tkbc,tc->tkb", jacobian, lamb, preferred_element_type=jnp.float32)
        own = jnp.einsum("ts,tb->sb", pick_own, push[:, 0], precision=lax.Precision.HIGHEST)
        later = jnp.einsum("ts,tb->sb", pick_next, push[:, 1], precision=lax.Precision.HIGHEST)
        return own, later

    lam = impulse_start * mask
    for sweep in range(ITERS):
        own, later = partials(lam)
        both = jnp.concatenate(
            [own + shifted(later, "body", 1), later + shifted(own, "body", -1)]
        )
        total = summed(both, "contact")
        velb = (free_pair + mass_pair * total).astype(jnp.bfloat16)
        rows_own = jnp.dot(
            pick_own_b, velb[:slab_blocks], preferred_element_type=jnp.float32
        ).astype(jnp.bfloat16)
        rows_next = jnp.dot(
            pick_next_b, velb[slab_blocks:], preferred_element_type=jnp.float32
        ).astype(jnp.bfloat16)
        rows = jnp.stack([rows_own, rows_next], axis=1)
        rel = jnp.einsum("tkbc,tkb->tc", jacobian, rows, preferred_element_type=jnp.float32) + bias
        lam = project(lam - step_scale * rel, friction, contacts) * mask
    own, later = partials(lam)
    total = summed(own + shifted(later, "body", 1), "contact")
    velocity = vel_free + inv_mass * total
    return (lam, velocity)


def solution(mesh):
    placed = (
        P(("contact", "body"), None, None, None),
        P(("contact", "body"), None),
        P(("contact", "body")),
        P("body", None),
        P("body", None),
        P(("contact", "body"), None),
        P(("contact", "body"), None),
        P(("contact", "body"), None),
        P(("contact", "body"), None),
    )
    return jax.shard_map(
        per_device,
        mesh=mesh,
        in_specs=placed,
        out_specs=(P(("contact", "body"), None), P("body", None)),
        check_vma=False,
    )
```

```python
import jax
import jax.numpy as jnp
from jax import lax
from jax.sharding import PartitionSpec as P

ITERS = 2


def shifted(value, axis, steps):
    count = lax.axis_size(axis)
    pairs = [(source, (source + steps) % count) for source in range(count)]
    return lax.ppermute(value, axis, pairs)


def rounded(value):
    return value.astype(jnp.bfloat16)


def partners(value, axis, stride, radix):
    count = lax.axis_size(axis)
    got = [value]
    for digit in range(1, radix):
        pairs = [(source, source ^ (digit * stride)) for source in range(count)]
        got.append(lax.ppermute(value, axis, pairs))
    return got


def tree(values):
    while len(values) > 1:
        values = [left + right for left, right in zip(values[::2], values[1::2])]
    return values[0]


def summed(value, axis):
    count = lax.axis_size(axis)
    if count & (count - 1):
        return lax.psum(value, axis)
    stride = min(count, 2)
    value = tree(partners(value, axis, 1, stride))
    while stride < count:
        radix = min(count // stride, 4)
        value = tree([part.astype(jnp.float32) for part in partners(rounded(value), axis, stride, radix)])
        stride *= radix
    return value


def project(trial, friction, contacts):
    normal = trial[:, :contacts]
    first = trial[:, contacts : 2 * contacts]
    second = trial[:, 2 * contacts :]
    tangent = jnp.sqrt(first * first + second * second)
    inside = tangent <= friction * normal
    below = friction * tangent <= -normal
    moved = (normal + friction * tangent) / (1.0 + friction * friction)
    safe = jnp.where(inside | below, 1.0, tangent)
    factor = jnp.where(inside, 1.0, jnp.where(below, 0.0, friction * moved / safe))
    new_normal = jnp.where(inside, normal, jnp.where(below, 0.0, moved))
    return jnp.concatenate([new_normal, first * factor, second * factor], axis=1)


def per_device(
    jacobian, tile_block, tile_count, vel_free, inv_mass, bias, step_scale, friction, impulse_start
):
    tiles_here = jacobian.shape[0]
    slab_blocks = vel_free.shape[0]
    contacts = friction.shape[1]
    order = jnp.arange(tiles_here, dtype=jnp.int32)
    mask = (order < tile_count[0]).astype(jnp.float32)[:, None]
    span = jnp.arange(slab_blocks, dtype=jnp.int32)
    pick_own = (tile_block[:, 0:1] == span[None, :]).astype(jnp.float32)
    pick_next = (tile_block[:, 1:2] == span[None, :]).astype(jnp.float32)
    pick_own_b = pick_own.astype(jnp.bfloat16)
    pick_next_b = pick_next.astype(jnp.bfloat16)
    free_pair = jnp.concatenate([vel_free, shifted(vel_free, "body", -1)])
    mass_pair = jnp.concatenate([inv_mass, shifted(inv_mass, "body", -1)])

    def partials(lam):
        lamb = lam.astype(jnp.bfloat16)
        push = jnp.einsum("tkbc,tc->tkb", jacobian, lamb, preferred_element_type=jnp.float32)
        own = jnp.einsum("ts,tb->sb", pick_own, push[:, 0], precision=lax.Precision.HIGHEST)
        later = jnp.einsum("ts,tb->sb", pick_next, push[:, 1], precision=lax.Precision.HIGHEST)
        return own, later

    lam = impulse_start * mask
    for sweep in range(ITERS):
        own, later = partials(lam)
        own_b, later_b = lax.optimization_barrier((rounded(own), rounded(later)))
        from_last, from_next = shifted(later_b, "body", 1), shifted(own_b, "body", -1)
        both = jnp.concatenate([own + from_last, later + from_next])
        total = summed(both, "contact")
        velb = (free_pair + mass_pair * total).astype(jnp.bfloat16)
        rows_own = jnp.dot(
            pick_own_b, velb[:slab_blocks], preferred_element_type=jnp.float32
        ).astype(jnp.bfloat16)
        rows_next = jnp.dot(
            pick_next_b, velb[slab_blocks:], preferred_element_type=jnp.float32
        ).astype(jnp.bfloat16)
        rows = jnp.stack([rows_own, rows_next], axis=1)
        rel = jnp.einsum("tkbc,tkb->tc", jacobian, rows, preferred_element_type=jnp.float32) + bias
        lam = project(lam - step_scale * rel, friction, contacts) * mask
    own, later = partials(lam)
    total = summed(own + shifted(rounded(later), "body", 1), "contact")
    velocity = vel_free + inv_mass * total
    return (lam, velocity)


def solution(mesh):
    placed = (
        P(("contact", "body"), None, None, None),
        P(("contact", "body"), None),
        P(("contact", "body")),
        P("body", None),
        P("body", None),
        P(("contact", "body"), None),
        P(("contact", "body"), None),
        P(("contact", "body"), None),
        P(("contact", "body"), None),
    )
    return jax.shard_map(
        per_device,
        mesh=mesh,
        in_specs=placed,
        out_specs=(P(("contact", "body"), None), P("body", None)),
        check_vma=False,
    )
```

```python
import functools

import jax
import jax.numpy as jnp
from jax import lax
from jax.experimental import pallas as pl
from jax.experimental.pallas import tpu as pltpu
from jax.sharding import PartitionSpec as P

ITERS = 2


def shifted(value, axis, steps):
    count = lax.axis_size(axis)
    pairs = [(source, (source + steps) % count) for source in range(count)]
    return lax.ppermute(value, axis, pairs)


def rounded(value):
    return value.astype(jnp.bfloat16)


def partners(value, axis, stride, radix):
    count = lax.axis_size(axis)
    got = [value]
    for digit in range(1, radix):
        pairs = [(source, source ^ (digit * stride)) for source in range(count)]
        got.append(lax.ppermute(value, axis, pairs))
    return got


def tree(values):
    while len(values) > 1:
        values = [left + right for left, right in zip(values[::2], values[1::2])]
    return values[0]


def near_sum(value, axis):
    count = lax.axis_size(axis)
    if count & (count - 1):
        return lax.psum(value, axis)
    stride = min(count, 2)
    value = tree(partners(value, axis, 1, stride))
    while count // stride > 4:
        parts = partners(rounded(value), axis, stride, 4)
        value = tree([part.astype(jnp.float32) for part in parts])
        stride *= 4
    return value


def far_parts(value, axis):
    count = lax.axis_size(axis)
    if count & (count - 1):
        return [value]
    stride = min(count, 2)
    while count // stride > 4:
        stride *= 4
    return partners(rounded(value), axis, stride, count // stride)


def project(trial, friction, contacts):
    normal = trial[:, :contacts]
    first = trial[:, contacts : 2 * contacts]
    second = trial[:, 2 * contacts :]
    tangent = jnp.sqrt(first * first + second * second)
    inside = tangent <= friction * normal
    below = friction * tangent <= -normal
    moved = (normal + friction * tangent) / (1.0 + friction * friction)
    safe = jnp.where(inside | below, 1.0, tangent)
    factor = jnp.where(inside, 1.0, jnp.where(below, 0.0, friction * moved / safe))
    new_normal = jnp.where(inside, normal, jnp.where(below, 0.0, moved))
    return jnp.concatenate([new_normal, first * factor, second * factor], axis=1)


def live(shape, count_ref):
    return lax.broadcasted_iota(jnp.int32, shape, 0) < count_ref[0]


def push_tile(tile, lam_ref, rows_of, block_ref, own_ref, later_ref):
    dofs = own_ref.shape[1]
    row = jnp.broadcast_to(lam_ref[pl.ds(tile, 1), :], (16, lam_ref.shape[1]))
    push = lax.dot_general(
        row.astype(jnp.bfloat16),
        rows_of(tile),
        (((1,), (1,)), ((), ())),
        preferred_element_type=jnp.float32,
    )
    own_ref[pl.ds(block_ref[tile, 0], 1), :] += push[:1, :dofs]
    later_ref[pl.ds(block_ref[tile, 1], 1), :] += push[:1, dofs:]


def rounded_sums(own_ref, later_ref, own_b_ref, later_b_ref):
    own_b_ref[...] = own_ref[...].astype(jnp.bfloat16)
    later_b_ref[...] = later_ref[...].astype(jnp.bfloat16)


def first_kernel(
    count_ref, block_ref, jac_ref, start_ref,
    kept_ref, lam_ref, own_ref, later_ref, own_b_ref, later_b_ref, sems,
):
    tiles = start_ref.shape[0]
    copies = [
        pltpu.make_async_copy(jac_ref.at[tile], kept_ref.at[tile], sems.at[tile])
        for tile in range(tiles)
    ]
    for copy in copies:
        copy.start()
    lam_ref[...] = jnp.where(live(start_ref.shape, count_ref), start_ref[...], 0.0)
    own_ref[...] = jnp.zeros_like(own_ref)
    later_ref[...] = jnp.zeros_like(later_ref)
    for tile in range(tiles):
        copies[tile].wait()
        push_tile(tile, lam_ref, lambda t: kept_ref[t], block_ref, own_ref, later_ref)
    rounded_sums(own_ref, later_ref, own_b_ref, later_b_ref)


def sweep_kernel(
    parts, count_ref, block_ref, jac_ref, free_ref, mass_ref, beside_ref,
    bias_ref, step_ref, friction_ref, old_ref, *refs,
):
    part_refs, refs = refs[:parts], refs[parts:]
    lam_ref, own_ref, later_ref, own_b_ref, later_b_ref, vel_ref, rel_ref = refs
    tiles = old_ref.shape[0]
    blocks, dofs = free_ref.shape
    total = tree([ref[...].astype(jnp.float32) for ref in part_refs])
    own_vel = free_ref[...] + mass_ref[...] * total[:blocks]
    next_vel = beside_ref[:blocks] + beside_ref[blocks:] * total[blocks:]
    vel_ref[:, :dofs] = own_vel
    vel_ref[:, dofs:] = next_vel
    own_ref[...] = jnp.zeros_like(own_ref)
    later_ref[...] = jnp.zeros_like(later_ref)
    for tile in range(tiles):
        own_row = vel_ref[pl.ds(block_ref[tile, 0], 1), :dofs]
        next_row = vel_ref[pl.ds(block_ref[tile, 1], 1), dofs:]
        row = jnp.broadcast_to(jnp.concatenate([own_row, next_row], axis=1), (16, 2 * dofs))
        rel = jnp.dot(row.astype(jnp.bfloat16), jac_ref[tile], preferred_element_type=jnp.float32)
        rel_ref[pl.ds(tile, 1), :] = rel[:1]
    trial = old_ref[...] - step_ref[...] * (rel_ref[...] + bias_ref[...])
    lam = project(trial, friction_ref[...], friction_ref.shape[1])
    lam_ref[...] = jnp.where(live(lam.shape, count_ref), lam, 0.0)
    for tile in range(tiles):
        push_tile(tile, lam_ref, lambda t: jac_ref[t], block_ref, own_ref, later_ref)
    rounded_sums(own_ref, later_ref, own_b_ref, later_b_ref)


LIMIT = 24 * 1024 * 1024
SMEM = pl.BlockSpec(memory_space=pltpu.SMEM)
VMEM = pl.BlockSpec(memory_space=pltpu.VMEM)


def sums_shape(lam, blocks, dofs):
    whole, half = (
        jax.ShapeDtypeStruct((blocks, dofs), kind) for kind in (jnp.float32, jnp.bfloat16)
    )
    return [jax.ShapeDtypeStruct(lam.shape, jnp.float32), whole, whole, half, half]


def first_push(jacobian, tile_block, tile_count, start, blocks):
    tiles, rows, cols = jacobian.shape
    return pl.pallas_call(
        first_kernel,
        out_shape=[pltpu.VMEM(jacobian.shape, jacobian.dtype)] + sums_shape(start, blocks, rows // 2),
        in_specs=[SMEM, SMEM, pl.BlockSpec(memory_space=pl.ANY), VMEM],
        out_specs=[VMEM] * 6,
        scratch_shapes=[pltpu.SemaphoreType.DMA((tiles,))],
        compiler_params=pltpu.CompilerParams(vmem_limit_bytes=LIMIT),
        name="first_push",
    )(tile_count, tile_block, jacobian, start)


def sweep_step(kept, tile_block, tile_count, free, mass, beside, bias, step, friction, lam, parts):
    blocks, dofs = free.shape
    kept = pltpu.with_memory_space_constraint(kept, pltpu.VMEM)
    return pl.pallas_call(
        functools.partial(sweep_kernel, len(parts)),
        out_shape=sums_shape(lam, blocks, dofs),
        in_specs=[SMEM, SMEM] + [VMEM] * (8 + len(parts)),
        out_specs=[VMEM] * 5,
        scratch_shapes=[
            pltpu.VMEM((blocks, 2 * dofs), jnp.float32),
            pltpu.VMEM(lam.shape, jnp.float32),
        ],
        compiler_params=pltpu.CompilerParams(vmem_limit_bytes=LIMIT),
        name="sweep_step",
    )(tile_count, tile_block, kept, free, mass, beside, bias, step, friction, lam, *parts)


def per_device(
    jacobian, tile_block, tile_count, vel_free, inv_mass, bias, step_scale, friction, impulse_start
):
    tiles, sides, dofs, rows = jacobian.shape
    blocks = vel_free.shape[0]
    flat = jacobian.reshape(tiles, sides * dofs, rows)
    kept, lam, own, later, own_b, later_b = first_push(
        flat, tile_block, tile_count, impulse_start, blocks
    )
    beside = None
    for sweep in range(ITERS):
        from_last, from_next = shifted(later_b, "body", 1), shifted(own_b, "body", -1)
        both = jnp.concatenate([own + from_last, later + from_next])
        near = near_sum(both, "contact")
        if beside is None:
            mine, near = lax.optimization_barrier((jnp.concatenate([vel_free, inv_mass]), near))
        parts = far_parts(near, "contact")
        if beside is None:
            beside = shifted(mine, "body", -1)
        lam, own, later, own_b, later_b = sweep_step(
            kept, tile_block, tile_count, vel_free, inv_mass, beside,
            bias, step_scale, friction, lam, parts,
        )
    total = near_sum(own + shifted(later_b, "body", 1), "contact")
    total = tree([part.astype(jnp.float32) for part in far_parts(total, "contact")])
    velocity = vel_free + inv_mass * total
    return (lam, velocity)


def solution(mesh):
    placed = (
        P(("contact", "body"), None, None, None),
        P(("contact", "body"), None),
        P(("contact", "body")),
        P("body", None),
        P("body", None),
        P(("contact", "body"), None),
        P(("contact", "body"), None),
        P(("contact", "body"), None),
        P(("contact", "body"), None),
    )
    return jax.shard_map(
        per_device,
        mesh=mesh,
        in_specs=placed,
        out_specs=(P(("contact", "body"), None), P("body", None)),
        check_vma=False,
    )
```

```python
import functools

import jax
import jax.numpy as jnp
from jax import lax
from jax.experimental import pallas as pl
from jax.experimental.pallas import tpu as pltpu
from jax.sharding import PartitionSpec as P

ITERS = 2


def shifted(value, axis, steps):
    count = lax.axis_size(axis)
    pairs = [(source, (source + steps) % count) for source in range(count)]
    return lax.ppermute(value, axis, pairs)


def traded(ahead, back, axis):
    count = lax.axis_size(axis)
    if count % 2:
        return shifted(ahead, axis, 1), shifted(back, axis, -1)
    even = (lax.axis_index(axis) & 1) == 0
    wide = [(place, (place + (-1 if place % 2 == 0 else 1)) % count) for place in range(count)]
    near = [(place, place ^ 1) for place in range(count)]
    got_wide = lax.ppermute(jnp.where(even, back, ahead), axis, wide)
    got_near = lax.ppermute(jnp.where(even, ahead, back), axis, near)
    return jnp.where(even, got_wide, got_near), jnp.where(even, got_near, got_wide)


def rounded(value):
    return value.astype(jnp.bfloat16)


def partners(value, axis, stride, radix):
    count = lax.axis_size(axis)
    got = [value]
    for digit in range(1, radix):
        pairs = [(source, source ^ (digit * stride)) for source in range(count)]
        got.append(lax.ppermute(value, axis, pairs))
    return got


def tree(values):
    while len(values) > 1:
        values = [left + right for left, right in zip(values[::2], values[1::2])]
    return values[0]


def near_sum(value, axis):
    count = lax.axis_size(axis)
    if count & (count - 1):
        return lax.psum(value, axis)
    stride = min(count, 2)
    value = tree(partners(value, axis, 1, stride))
    while count // stride > 4:
        parts = partners(rounded(value), axis, stride, 4)
        value = tree([part.astype(jnp.float32) for part in parts])
        stride *= 4
    return value


def far_parts(value, axis):
    count = lax.axis_size(axis)
    if count & (count - 1):
        return [value]
    stride = min(count, 2)
    while count // stride > 4:
        stride *= 4
    return partners(rounded(value), axis, stride, count // stride)


def project(trial, friction, contacts):
    normal = trial[:, :contacts]
    first = trial[:, contacts : 2 * contacts]
    second = trial[:, 2 * contacts :]
    tangent = jnp.sqrt(first * first + second * second)
    inside = tangent <= friction * normal
    below = friction * tangent <= -normal
    moved = (normal + friction * tangent) / (1.0 + friction * friction)
    safe = jnp.where(inside | below, 1.0, tangent)
    factor = jnp.where(inside, 1.0, jnp.where(below, 0.0, friction * moved / safe))
    new_normal = jnp.where(inside, normal, jnp.where(below, 0.0, moved))
    return jnp.concatenate([new_normal, first * factor, second * factor], axis=1)


def live(shape, count_ref):
    return lax.broadcasted_iota(jnp.int32, shape, 0) < count_ref[0]


def push_tile(tile, lam_ref, rows_of, block_ref, own_ref, later_ref):
    dofs = own_ref.shape[1]
    row = jnp.broadcast_to(lam_ref[pl.ds(tile, 1), :], (16, lam_ref.shape[1]))
    push = lax.dot_general(
        row.astype(jnp.bfloat16),
        rows_of(tile),
        (((1,), (1,)), ((), ())),
        preferred_element_type=jnp.float32,
    )
    own_ref[pl.ds(block_ref[0, tile], 1), :] += push[:1, :dofs]
    later_ref[pl.ds(block_ref[1, tile], 1), :] += push[:1, dofs:]


def rounded_sums(own_ref, later_ref, own_b_ref, later_b_ref):
    own_b_ref[...] = own_ref[...].astype(jnp.bfloat16)
    later_b_ref[...] = later_ref[...].astype(jnp.bfloat16)


def first_kernel(
    count_ref, block_ref, jac_ref, start_ref,
    kept_ref, lam_ref, own_ref, later_ref, own_b_ref, later_b_ref, sems,
):
    tiles = start_ref.shape[0]
    copies = [
        pltpu.make_async_copy(jac_ref.at[tile], kept_ref.at[tile], sems.at[tile])
        for tile in range(tiles)
    ]
    for copy in copies:
        copy.start()
    lam_ref[...] = jnp.where(live(start_ref.shape, count_ref), start_ref[...], 0.0)
    own_ref[...] = jnp.zeros_like(own_ref)
    later_ref[...] = jnp.zeros_like(later_ref)
    for tile in range(tiles):
        copies[tile].wait()
        push_tile(tile, lam_ref, lambda t: kept_ref[t], block_ref, own_ref, later_ref)
    rounded_sums(own_ref, later_ref, own_b_ref, later_b_ref)


def sweep_kernel(
    parts, count_ref, block_ref, jac_ref, free_ref, mass_ref, beside_ref,
    bias_ref, step_ref, friction_ref, old_ref, *refs,
):
    part_refs, refs = refs[:parts], refs[parts:]
    lam_ref, own_ref, later_ref, own_b_ref, later_b_ref, vel_ref, rel_ref = refs
    tiles = old_ref.shape[0]
    blocks, dofs = free_ref.shape
    total = tree([ref[...].astype(jnp.float32) for ref in part_refs])
    own_vel = free_ref[...] + mass_ref[...] * total[:blocks]
    next_vel = beside_ref[:blocks] + beside_ref[blocks:] * total[blocks:]
    vel_ref[:, :dofs] = own_vel
    vel_ref[:, dofs:] = next_vel
    own_ref[...] = jnp.zeros_like(own_ref)
    later_ref[...] = jnp.zeros_like(later_ref)
    for tile in range(tiles):
        own_row = vel_ref[pl.ds(block_ref[0, tile], 1), :dofs]
        next_row = vel_ref[pl.ds(block_ref[1, tile], 1), dofs:]
        row = jnp.broadcast_to(jnp.concatenate([own_row, next_row], axis=1), (16, 2 * dofs))
        rel = jnp.dot(row.astype(jnp.bfloat16), jac_ref[tile], preferred_element_type=jnp.float32)
        rel_ref[pl.ds(tile, 1), :] = rel[:1]
    trial = old_ref[...] - step_ref[...] * (rel_ref[...] + bias_ref[...])
    lam = project(trial, friction_ref[...], friction_ref.shape[1])
    lam_ref[...] = jnp.where(live(lam.shape, count_ref), lam, 0.0)
    for tile in range(tiles):
        push_tile(tile, lam_ref, lambda t: jac_ref[t], block_ref, own_ref, later_ref)
    rounded_sums(own_ref, later_ref, own_b_ref, later_b_ref)


LIMIT = 24 * 1024 * 1024
SMEM = pl.BlockSpec(memory_space=pltpu.SMEM)
VMEM = pl.BlockSpec(memory_space=pltpu.VMEM)


def sums_shape(lam, blocks, dofs):
    whole, half = (
        jax.ShapeDtypeStruct((blocks, dofs), kind) for kind in (jnp.float32, jnp.bfloat16)
    )
    return [jax.ShapeDtypeStruct(lam.shape, jnp.float32), whole, whole, half, half]


def first_push(jacobian, tile_block, tile_count, start, blocks):
    tiles, rows, cols = jacobian.shape
    return pl.pallas_call(
        first_kernel,
        out_shape=[pltpu.VMEM(jacobian.shape, jacobian.dtype)] + sums_shape(start, blocks, rows // 2),
        in_specs=[SMEM, SMEM, pl.BlockSpec(memory_space=pltpu.HBM), VMEM],
        out_specs=[VMEM] * 6,
        scratch_shapes=[pltpu.SemaphoreType.DMA((tiles,))],
        compiler_params=pltpu.CompilerParams(vmem_limit_bytes=LIMIT),
        name="first_push",
    )(tile_count, tile_block, pltpu.with_memory_space_constraint(jacobian, pltpu.HBM), start)


def sweep_step(kept, tile_block, tile_count, free, mass, beside, bias, step, friction, lam, parts):
    blocks, dofs = free.shape
    kept = pltpu.with_memory_space_constraint(kept, pltpu.VMEM)
    return pl.pallas_call(
        functools.partial(sweep_kernel, len(parts)),
        out_shape=sums_shape(lam, blocks, dofs),
        in_specs=[SMEM, SMEM] + [VMEM] * (8 + len(parts)),
        out_specs=[VMEM] * 5,
        scratch_shapes=[
            pltpu.VMEM((blocks, 2 * dofs), jnp.float32),
            pltpu.VMEM(lam.shape, jnp.float32),
        ],
        compiler_params=pltpu.CompilerParams(vmem_limit_bytes=LIMIT),
        name="sweep_step",
    )(tile_count, tile_block, kept, free, mass, beside, bias, step, friction, lam, *parts)


def per_device(
    jacobian, tile_block, tile_count, vel_free, inv_mass, bias, step_scale, friction, impulse_start
):
    tiles, sides, dofs, rows = jacobian.shape
    blocks = vel_free.shape[0]
    flat = jacobian.reshape(tiles, sides * dofs, rows)
    tile_block = tile_block.T
    kept, lam, own, later, own_b, later_b = first_push(
        flat, tile_block, tile_count, impulse_start, blocks
    )
    beside = None
    mine = jnp.concatenate([vel_free, inv_mass])
    for sweep in range(ITERS):
        from_last, from_next = traded(later_b, own_b, "body")
        if beside is None:
            mine, later_b, own_b = lax.optimization_barrier((mine, later_b, own_b))
            beside = shifted(mine, "body", -1)
        near = near_sum(jnp.concatenate([own + from_last, later + from_next]), "contact")
        lam, own, later, own_b, later_b = sweep_step(
            kept, tile_block, tile_count, vel_free, inv_mass, beside,
            bias, step_scale, friction, lam, far_parts(near, "contact"),
        )
    total = near_sum(own + shifted(later_b, "body", 1), "contact")
    total = tree([part.astype(jnp.float32) for part in far_parts(total, "contact")])
    velocity = vel_free + inv_mass * total
    return (lam, velocity)


def solution(mesh):
    placed = (
        P(("contact", "body"), None, None, None),
        P(("contact", "body"), None),
        P(("contact", "body")),
        P("body", None),
        P("body", None),
        P(("contact", "body"), None),
        P(("contact", "body"), None),
        P(("contact", "body"), None),
        P(("contact", "body"), None),
    )
    return jax.shard_map(
        per_device,
        mesh=mesh,
        in_specs=placed,
        out_specs=(P(("contact", "body"), None), P("body", None)),
        check_vma=False,
    )
```

```python
import functools

import jax
import jax.numpy as jnp
from jax import lax
from jax.experimental import pallas as pl
from jax.experimental.pallas import tpu as pltpu
from jax.sharding import PartitionSpec as P

ITERS = 2


def shifted(value, axis, steps):
    count = lax.axis_size(axis)
    pairs = [(source, (source + steps) % count) for source in range(count)]
    return lax.ppermute(value, axis, pairs)


def traded(ahead, back, axis):
    count = lax.axis_size(axis)
    if count % 2:
        return shifted(ahead, axis, 1), shifted(back, axis, -1)
    even = (lax.axis_index(axis) & 1) == 0
    wide = [(place, (place + (-1 if place % 2 == 0 else 1)) % count) for place in range(count)]
    near = [(place, place ^ 1) for place in range(count)]
    got_wide = lax.ppermute(jnp.where(even, back, ahead), axis, wide)
    got_near = lax.ppermute(jnp.where(even, ahead, back), axis, near)
    return jnp.where(even, got_wide, got_near), jnp.where(even, got_near, got_wide)


def rounded(value):
    return value.astype(jnp.bfloat16)


def partners(value, axis, stride, radix):
    count = lax.axis_size(axis)
    got = [value]
    for digit in range(1, radix):
        pairs = [(source, source ^ (digit * stride)) for source in range(count)]
        got.append(lax.ppermute(value, axis, pairs))
    return got


def tree(values):
    while len(values) > 1:
        values = [left + right for left, right in zip(values[::2], values[1::2])]
    return values[0]


def near_sum(value, axis):
    count = lax.axis_size(axis)
    if count & (count - 1):
        return lax.psum(value, axis)
    stride = min(count, 2)
    value = tree(partners(value, axis, 1, stride))
    while count // stride > 4:
        parts = partners(rounded(value), axis, stride, 4)
        value = tree([part.astype(jnp.float32) for part in parts])
        stride *= 4
    return value


def far_parts(value, axis):
    count = lax.axis_size(axis)
    if count & (count - 1):
        return [value]
    stride = min(count, 2)
    while count // stride > 4:
        stride *= 4
    return partners(rounded(value), axis, stride, count // stride)


def project(trial, friction, contacts):
    normal = trial[:, :contacts]
    first = trial[:, contacts : 2 * contacts]
    second = trial[:, 2 * contacts :]
    tangent = jnp.sqrt(first * first + second * second)
    inside = tangent <= friction * normal
    below = friction * tangent <= -normal
    moved = (normal + friction * tangent) / (1.0 + friction * friction)
    safe = jnp.where(inside | below, 1.0, tangent)
    factor = jnp.where(inside, 1.0, jnp.where(below, 0.0, friction * moved / safe))
    new_normal = jnp.where(inside, normal, jnp.where(below, 0.0, moved))
    return jnp.concatenate([new_normal, first * factor, second * factor], axis=1)


def live(shape, count_ref):
    return lax.broadcasted_iota(jnp.int32, shape, 0) < count_ref[0]


def push_tile(tile, lam_ref, rows_of, block_ref, own_ref, later_ref):
    dofs = own_ref.shape[1]
    row = jnp.broadcast_to(lam_ref[pl.ds(tile, 1), :], (16, lam_ref.shape[1]))
    push = lax.dot_general(
        row.astype(jnp.bfloat16),
        rows_of(tile),
        (((1,), (1,)), ((), ())),
        preferred_element_type=jnp.float32,
    )
    own_ref[pl.ds(block_ref[0, tile], 1), :] += push[:1, :dofs]
    later_ref[pl.ds(block_ref[1, tile], 1), :] += push[:1, dofs:]


def rounded_sums(own_ref, later_ref, own_b_ref, later_b_ref):
    own_b_ref[...] = own_ref[...].astype(jnp.bfloat16)
    later_b_ref[...] = later_ref[...].astype(jnp.bfloat16)


def first_kernel(
    count_ref, block_ref, jac_ref, start_ref,
    kept_ref, lam_ref, own_ref, later_ref, own_b_ref, later_b_ref, sems,
):
    tiles = start_ref.shape[0]
    copies = [
        pltpu.make_async_copy(jac_ref.at[tile], kept_ref.at[tile], sems.at[tile])
        for tile in range(tiles)
    ]
    for copy in copies[:DEEP]:
        copy.start()
    lam_ref[...] = jnp.where(live(start_ref.shape, count_ref), start_ref[...], 0.0)
    own_ref[...] = jnp.zeros_like(own_ref)
    later_ref[...] = jnp.zeros_like(later_ref)
    for tile in range(tiles):
        copies[tile].wait()
        if tile + DEEP < tiles:
            copies[tile + DEEP].start()
        push_tile(tile, lam_ref, lambda t: kept_ref[t], block_ref, own_ref, later_ref)
    rounded_sums(own_ref, later_ref, own_b_ref, later_b_ref)


def sweep_kernel(
    parts, count_ref, block_ref, jac_ref, free_ref, mass_ref, beside_ref,
    bias_ref, step_ref, friction_ref, old_ref, *refs,
):
    part_refs, refs = refs[:parts], refs[parts:]
    lam_ref, own_ref, later_ref, own_b_ref, later_b_ref, vel_ref, rel_ref = refs
    tiles = old_ref.shape[0]
    blocks, dofs = free_ref.shape
    parts = part_refs[0].shape[0]
    total = tree([part_refs[0][part].astype(jnp.float32) for part in range(parts)])
    own_vel = free_ref[...] + mass_ref[...] * total[:blocks]
    next_vel = beside_ref[:blocks] + beside_ref[blocks:] * total[blocks:]
    vel_ref[:, :dofs] = own_vel
    vel_ref[:, dofs:] = next_vel
    own_ref[...] = jnp.zeros_like(own_ref)
    later_ref[...] = jnp.zeros_like(later_ref)
    for tile in range(tiles):
        own_row = vel_ref[pl.ds(block_ref[0, tile], 1), :dofs]
        next_row = vel_ref[pl.ds(block_ref[1, tile], 1), dofs:]
        row = jnp.broadcast_to(jnp.concatenate([own_row, next_row], axis=1), (16, 2 * dofs))
        rel = jnp.dot(row.astype(jnp.bfloat16), jac_ref[tile], preferred_element_type=jnp.float32)
        rel_ref[pl.ds(tile, 1), :] = rel[:1]
    trial = old_ref[...] - step_ref[...] * (rel_ref[...] + bias_ref[...])
    lam = project(trial, friction_ref[...], friction_ref.shape[1])
    lam_ref[...] = jnp.where(live(lam.shape, count_ref), lam, 0.0)
    for tile in range(tiles):
        push_tile(tile, lam_ref, lambda t: jac_ref[t], block_ref, own_ref, later_ref)
    rounded_sums(own_ref, later_ref, own_b_ref, later_b_ref)


DEEP = 3
LIMIT = 24 * 1024 * 1024
SMEM = pl.BlockSpec(memory_space=pltpu.SMEM)
VMEM = pl.BlockSpec(memory_space=pltpu.VMEM)


def sums_shape(lam, blocks, dofs):
    whole, half = (
        jax.ShapeDtypeStruct((blocks, dofs), kind) for kind in (jnp.float32, jnp.bfloat16)
    )
    return [jax.ShapeDtypeStruct(lam.shape, jnp.float32), whole, whole, half, half]


def first_push(jacobian, tile_block, tile_count, start, blocks):
    tiles, rows, cols = jacobian.shape
    return pl.pallas_call(
        first_kernel,
        out_shape=[pltpu.VMEM(jacobian.shape, jacobian.dtype)] + sums_shape(start, blocks, rows // 2),
        in_specs=[SMEM, SMEM, pl.BlockSpec(memory_space=pltpu.HBM), VMEM],
        out_specs=[VMEM] * 6,
        scratch_shapes=[pltpu.SemaphoreType.DMA((tiles,))],
        compiler_params=pltpu.CompilerParams(vmem_limit_bytes=LIMIT),
        name="first_push",
    )(tile_count, tile_block, pltpu.with_memory_space_constraint(jacobian, pltpu.HBM), start)


def sweep_step(kept, tile_block, tile_count, free, mass, beside, bias, step, friction, lam, parts):
    blocks, dofs = free.shape
    kept = pltpu.with_memory_space_constraint(kept, pltpu.VMEM)
    return pl.pallas_call(
        functools.partial(sweep_kernel, len(parts)),
        out_shape=sums_shape(lam, blocks, dofs),
        in_specs=[SMEM, SMEM] + [VMEM] * (8 + len(parts)),
        out_specs=[VMEM] * 5,
        scratch_shapes=[
            pltpu.VMEM((blocks, 2 * dofs), jnp.float32),
            pltpu.VMEM(lam.shape, jnp.float32),
        ],
        compiler_params=pltpu.CompilerParams(vmem_limit_bytes=LIMIT),
        name="sweep_step",
    )(tile_count, tile_block, kept, free, mass, beside, bias, step, friction, lam, *parts)


def per_device(
    jacobian, tile_block, tile_count, vel_free, inv_mass, bias, step_scale, friction, impulse_start
):
    tiles, sides, dofs, rows = jacobian.shape
    blocks = vel_free.shape[0]
    flat = jacobian.reshape(tiles, sides * dofs, rows)
    tile_block = tile_block.T
    kept, lam, own, later, own_b, later_b = first_push(
        flat, tile_block, tile_count, impulse_start, blocks
    )
    slabs = lax.all_gather(jnp.concatenate([vel_free, inv_mass]), "body")
    after = (lax.axis_index("body") + 1) % lax.axis_size("body")
    beside = lax.dynamic_index_in_dim(slabs, after, 0, keepdims=False)
    for sweep in range(ITERS):
        from_last, from_next = traded(later_b, own_b, "body")
        pair = jnp.concatenate([own + from_last, later + from_next]).astype(jnp.bfloat16)
        parts = lax.all_gather(pair, "contact")
        lam, own, later, own_b, later_b = sweep_step(
            kept, tile_block, tile_count, vel_free, inv_mass, beside,
            bias, step_scale, friction, lam, [parts],
        )
    total = near_sum(own + shifted(later_b, "body", 1), "contact")
    total = tree([part.astype(jnp.float32) for part in far_parts(total, "contact")])
    velocity = vel_free + inv_mass * total
    return (lam, velocity)


def solution(mesh):
    placed = (
        P(("contact", "body"), None, None, None),
        P(("contact", "body"), None),
        P(("contact", "body")),
        P("body", None),
        P("body", None),
        P(("contact", "body"), None),
        P(("contact", "body"), None),
        P(("contact", "body"), None),
        P(("contact", "body"), None),
    )
    return jax.shard_map(
        per_device,
        mesh=mesh,
        in_specs=placed,
        out_specs=(P(("contact", "body"), None), P("body", None)),
        check_vma=False,
    )
```

```python
import jax
import jax.numpy as jnp
from jax import lax
from jax.experimental import pallas as pl
from jax.experimental.pallas import tpu as pltpu
from jax.sharding import PartitionSpec as P

ITERS = 2


def shifted(value, axis, steps):
    count = lax.axis_size(axis)
    pairs = [(source, (source + steps) % count) for source in range(count)]
    return lax.ppermute(value, axis, pairs)


def sent(value, target):
    count = lax.axis_size("body")
    pairs = [
        (group * count + place, group * count + target(place) % count)
        for group in range(lax.axis_size("contact") - 1, -1, -2)
        for place in range(count)
    ]
    return lax.ppermute(value, ("contact", "body"), pairs)


def ahead_of(place):
    return place + 1


def traded(ahead, back):
    if lax.axis_size("body") % 2:
        return sent(ahead, ahead_of), sent(back, lambda place: place - 1)
    even = (lax.axis_index("body") & 1) == 0
    wide = sent(jnp.where(even, back, ahead), lambda place: place + 2 * (place % 2) - 1)
    near = sent(jnp.where(even, ahead, back), lambda place: place ^ 1)
    return jnp.where(even, wide, near), jnp.where(even, near, wide)


def rounded(value):
    return value.astype(jnp.bfloat16)


def tree(values):
    while len(values) > 1:
        values = [left + right for left, right in zip(values[::2], values[1::2])]
    return values[0]


def to_speaker(value):
    count = lax.axis_size("contact")
    if count == 1:
        return value
    return value + lax.ppermute(value, "contact", [(place - 1, place) for place in range(1, count, 2)])


def over_speakers(value):
    count = lax.axis_size("contact")
    if count & (count - 1):
        return lax.psum(jnp.where((lax.axis_index("contact") & 1) == 1, value, 0.0), "contact")
    stride = 2
    while stride < count:
        radix = min(count // stride, 4)
        parts = [rounded(value)]
        for digit in range(1, radix):
            pairs = [(place, place ^ (digit * stride)) for place in range(1, count, 2)]
            parts.append(lax.ppermute(rounded(value), "contact", pairs))
        value = tree([part.astype(jnp.float32) for part in parts])
        stride *= radix
    return value


def from_speaker(value):
    count = lax.axis_size("contact")
    if count == 1:
        return value
    got = lax.ppermute(value, "contact", [(place, place - 1) for place in range(1, count, 2)])
    return jnp.where((lax.axis_index("contact") & 1) == 1, value, got)


def project(trial, friction, contacts):
    normal = trial[:, :contacts]
    first = trial[:, contacts : 2 * contacts]
    second = trial[:, 2 * contacts :]
    tangent = jnp.sqrt(first * first + second * second)
    inside = tangent <= friction * normal
    below = friction * tangent <= -normal
    moved = (normal + friction * tangent) / (1.0 + friction * friction)
    safe = jnp.where(inside | below, 1.0, tangent)
    factor = jnp.where(inside, 1.0, jnp.where(below, 0.0, friction * moved / safe))
    new_normal = jnp.where(inside, normal, jnp.where(below, 0.0, moved))
    return jnp.concatenate([new_normal, first * factor, second * factor], axis=1)


def live(shape, count_ref):
    return lax.broadcasted_iota(jnp.int32, shape, 0) < count_ref[0]


def push_tile(tile, lam_ref, rows_of, block_ref, sums_ref):
    blocks, dofs = sums_ref.shape[0] // 2, sums_ref.shape[1]
    row = jnp.broadcast_to(lam_ref[pl.ds(tile, 1), :], (16, lam_ref.shape[1]))
    push = lax.dot_general(
        row.astype(jnp.bfloat16),
        rows_of(tile),
        (((1,), (1,)), ((), ())),
        preferred_element_type=jnp.float32,
    )
    sums_ref[pl.ds(block_ref[0, tile], 1), :] += push[:1, :dofs]
    sums_ref[pl.ds(blocks + block_ref[1, tile], 1), :] += push[:1, dofs:]


def first_kernel(
    count_ref, block_ref, jac_ref, start_ref,
    kept_ref, lam_ref, sums_ref, sems,
):
    tiles = start_ref.shape[0]
    half = jac_ref.shape[1] // 2
    copies = [
        [
            pltpu.make_async_copy(
                jac_ref.at[tile, pl.ds(side * half, half)],
                kept_ref.at[tile, pl.ds(side * half, half)],
                sems.at[tile, side],
            )
            for side in range(2)
        ]
        for tile in range(tiles)
    ]
    for pair in copies[:DEEP]:
        for copy in pair:
            copy.start()
    lam_ref[...] = jnp.where(live(start_ref.shape, count_ref), start_ref[...], 0.0)
    sums_ref[...] = jnp.zeros_like(sums_ref)
    for tile in range(tiles):
        for copy in copies[tile]:
            copy.wait()
        for pair in copies[tile + DEEP : tile + DEEP + 1]:
            for copy in pair:
                copy.start()
        push_tile(tile, lam_ref, lambda t: kept_ref[t], block_ref, sums_ref)


def sweep_kernel(
    count_ref, block_ref, jac_ref, free_ref, mass_ref, beside_ref,
    bias_ref, step_ref, friction_ref, old_ref, total_ref,
    lam_ref, sums_ref, vel_ref, rel_ref,
):
    tiles = old_ref.shape[0]
    blocks, dofs = free_ref.shape
    total = total_ref[...]
    own_vel = free_ref[...] + mass_ref[...] * total[:blocks]
    next_vel = beside_ref[:blocks] + beside_ref[blocks:] * total[blocks:]
    vel_ref[:, :dofs] = own_vel
    vel_ref[:, dofs:] = next_vel
    sums_ref[...] = jnp.zeros_like(sums_ref)
    for tile in range(tiles):
        own_row = vel_ref[pl.ds(block_ref[0, tile], 1), :dofs]
        next_row = vel_ref[pl.ds(block_ref[1, tile], 1), dofs:]
        row = jnp.broadcast_to(jnp.concatenate([own_row, next_row], axis=1), (16, 2 * dofs))
        rel = jnp.dot(row.astype(jnp.bfloat16), jac_ref[tile], preferred_element_type=jnp.float32)
        rel_ref[pl.ds(tile, 1), :] = rel[:1]
    trial = old_ref[...] - step_ref[...] * (rel_ref[...] + bias_ref[...])
    lam = project(trial, friction_ref[...], friction_ref.shape[1])
    lam_ref[...] = jnp.where(live(lam.shape, count_ref), lam, 0.0)
    for tile in range(tiles):
        push_tile(tile, lam_ref, lambda t: jac_ref[t], block_ref, sums_ref)


DEEP = 8
LIMIT = 24 * 1024 * 1024
SMEM = pl.BlockSpec(memory_space=pltpu.SMEM)
VMEM = pl.BlockSpec(memory_space=pltpu.VMEM)


def sums_shape(lam, blocks, dofs):
    return [
        jax.ShapeDtypeStruct(lam.shape, jnp.float32),
        jax.ShapeDtypeStruct((2 * blocks, dofs), jnp.float32),
    ]


def first_push(jacobian, tile_block, tile_count, start, blocks):
    tiles, rows, cols = jacobian.shape
    return pl.pallas_call(
        first_kernel,
        out_shape=[pltpu.VMEM(jacobian.shape, jacobian.dtype)] + sums_shape(start, blocks, rows // 2),
        in_specs=[SMEM, SMEM, pl.BlockSpec(memory_space=pltpu.HBM), VMEM],
        out_specs=[VMEM] * 3,
        scratch_shapes=[pltpu.SemaphoreType.DMA((tiles, 2))],
        compiler_params=pltpu.CompilerParams(vmem_limit_bytes=LIMIT),
        name="first_push",
    )(tile_count, tile_block, pltpu.with_memory_space_constraint(jacobian, pltpu.HBM), start)


def sweep_step(kept, tile_block, tile_count, free, mass, beside, bias, step, friction, lam, total):
    blocks, dofs = free.shape
    kept = pltpu.with_memory_space_constraint(kept, pltpu.VMEM)
    return pl.pallas_call(
        sweep_kernel,
        out_shape=sums_shape(lam, blocks, dofs),
        in_specs=[SMEM, SMEM] + [VMEM] * 9,
        out_specs=[VMEM] * 2,
        scratch_shapes=[
            pltpu.VMEM((blocks, 2 * dofs), jnp.float32),
            pltpu.VMEM(lam.shape, jnp.float32),
        ],
        compiler_params=pltpu.CompilerParams(vmem_limit_bytes=LIMIT),
        name="sweep_step",
    )(tile_count, tile_block, kept, free, mass, beside, bias, step, friction, lam, total)


def per_device(
    jacobian, tile_block, tile_count, vel_free, inv_mass, bias, step_scale, friction, impulse_start
):
    tiles, sides, dofs, rows = jacobian.shape
    blocks = vel_free.shape[0]
    flat = jacobian.reshape(tiles, sides * dofs, rows)
    tile_block = tile_block.T
    beside = shifted(jnp.concatenate([vel_free, inv_mass]), "body", -1)
    beside, flat = lax.optimization_barrier((beside, flat))
    kept, lam, sums = first_push(flat, tile_block, tile_count, impulse_start, blocks)
    for sweep in range(ITERS):
        both = to_speaker(sums)
        own, later = both[:blocks], both[blocks:]
        from_last, from_next = traded(rounded(later), rounded(own))
        total = over_speakers(jnp.concatenate([own + from_last, later + from_next]))
        lam, sums = sweep_step(
            kept, tile_block, tile_count, vel_free, inv_mass, beside,
            bias, step_scale, friction, lam, from_speaker(total),
        )
    both = to_speaker(sums)
    from_last = sent(rounded(both[blocks:]), ahead_of)
    total = from_speaker(over_speakers(both[:blocks] + from_last))
    velocity = vel_free + inv_mass * total
    return (lam, velocity)


def solution(mesh):
    placed = (
        P(("contact", "body"), None, None, None),
        P(("contact", "body"), None),
        P(("contact", "body")),
        P("body", None),
        P("body", None),
        P(("contact", "body"), None),
        P(("contact", "body"), None),
        P(("contact", "body"), None),
        P(("contact", "body"), None),
    )
    return jax.shard_map(
        per_device,
        mesh=mesh,
        in_specs=placed,
        out_specs=(P(("contact", "body"), None), P("body", None)),
        check_vma=False,
    )
```

```python
import jax
import jax.numpy as jnp
from jax import lax
from jax.experimental import pallas as pl
from jax.experimental.pallas import tpu as pltpu
from jax.sharding import PartitionSpec as P

ITERS = 2


def shifted(value, axis, steps):
    count = lax.axis_size(axis)
    pairs = [(source, (source + steps) % count) for source in range(count)]
    return lax.ppermute(value, axis, pairs)


def crossed(value, target):
    count, groups = lax.axis_size("body"), lax.axis_size("contact")
    cross = 1 if groups % 2 == 0 else 0
    pairs = [
        (group * count + place, (group ^ cross) * count + target(place) % count)
        for group in range(groups)
        for place in range(count)
    ]
    return lax.ppermute(value, ("contact", "body"), pairs)


def ahead_of(place):
    return place + 1


def traded(ahead, back):
    if lax.axis_size("body") % 2:
        return crossed(ahead, ahead_of), crossed(back, lambda place: place - 1)
    even = (lax.axis_index("body") & 1) == 0
    wide = crossed(jnp.where(even, back, ahead), lambda place: place + 2 * (place % 2) - 1)
    near = crossed(jnp.where(even, ahead, back), lambda place: place ^ 1)
    return jnp.where(even, wide, near), jnp.where(even, near, wide)


def rounded(value):
    return value.astype(jnp.bfloat16)


def tree(values):
    while len(values) > 1:
        values = [left + right for left, right in zip(values[::2], values[1::2])]
    return values[0]


def pair_sum(value):
    count = lax.axis_size("contact")
    if count % 2:
        return value
    return value + lax.ppermute(value, "contact", [(place, place ^ 1) for place in range(count)])


def over_pairs(value):
    count = lax.axis_size("contact")
    if count & (count - 1):
        mine = (lax.axis_index("contact") & 1) == 0
        return lax.psum(value if count % 2 else jnp.where(mine, value, 0.0), "contact")
    stride = 2
    while stride < count:
        radix = min(count // stride, 4)
        parts = [rounded(value)]
        for digit in range(1, radix):
            pairs = [(place, place ^ (digit * stride) ^ 1) for place in range(count)]
            parts.append(lax.ppermute(rounded(value), "contact", pairs))
        value = tree([part.astype(jnp.float32) for part in parts])
        stride *= radix
    return value


def project(trial, friction, contacts):
    normal = trial[:, :contacts]
    first = trial[:, contacts : 2 * contacts]
    second = trial[:, 2 * contacts :]
    tangent = jnp.sqrt(first * first + second * second)
    inside = tangent <= friction * normal
    below = friction * tangent <= -normal
    moved = (normal + friction * tangent) / (1.0 + friction * friction)
    safe = jnp.where(inside | below, 1.0, tangent)
    factor = jnp.where(inside, 1.0, jnp.where(below, 0.0, friction * moved / safe))
    new_normal = jnp.where(inside, normal, jnp.where(below, 0.0, moved))
    return jnp.concatenate([new_normal, first * factor, second * factor], axis=1)


def push_tile(tile, lam_ref, rows_of, block_ref, sums_ref):
    blocks, dofs = sums_ref.shape[0] // 2, sums_ref.shape[1]
    row = jnp.broadcast_to(lam_ref[pl.ds(tile, 1), :], (16, lam_ref.shape[1]))
    push = lax.dot_general(
        row.astype(jnp.bfloat16),
        rows_of(tile),
        (((1,), (1,)), ((), ())),
        preferred_element_type=jnp.float32,
    )
    sums_ref[pl.ds(block_ref[0, tile], 1), :] += push[:1, :dofs]
    sums_ref[pl.ds(blocks + block_ref[1, tile], 1), :] += push[:1, dofs:]


def first_kernel(
    count_ref, block_ref, jac_ref, start_ref, kept_ref, live_ref, lam_ref, sums_ref,
    block, sems, small_sems,
):
    tiles = start_ref.shape[0]
    small = [
        pltpu.make_async_copy(source, target, small_sems.at[place])
        for place, (source, target) in enumerate(
            [(block_ref, block), (start_ref, lam_ref)]
        )
    ]
    copies = [
        pltpu.make_async_copy(jac_ref.at[tile], kept_ref.at[tile], sems.at[tile])
        for tile in range(tiles)
    ]
    for copy in small + copies[:DEEP]:
        copy.start()
    sums_ref[...] = jnp.zeros_like(sums_ref)
    for copy in small:
        copy.wait()
    order = lax.broadcasted_iota(jnp.int32, lam_ref.shape, 0)
    live_ref[...] = jnp.where(order < count_ref[0], 1.0, 0.0)
    lam_ref[...] = lam_ref[...] * live_ref[...]
    for tile in range(tiles):
        copies[tile].wait()
        if tile + DEEP < tiles:
            copies[tile + DEEP].start()
        push_tile(tile, lam_ref, lambda t: kept_ref[t], block, sums_ref)


def sweep_kernel(
    block_ref, live_ref, jac_ref, free_ref, mass_ref, beside_ref,
    bias_ref, step_ref, friction_ref, old_ref, total_ref,
    lam_ref, sums_ref, vel_ref, rel_ref,
):
    tiles = old_ref.shape[0]
    blocks, dofs = free_ref.shape
    total = total_ref[...]
    own_vel = free_ref[...] + mass_ref[...] * total[:blocks]
    next_vel = beside_ref[:blocks] + beside_ref[blocks:] * total[blocks:]
    vel_ref[:, :dofs] = own_vel
    vel_ref[:, dofs:] = next_vel
    sums_ref[...] = jnp.zeros_like(sums_ref)
    for tile in range(tiles):
        own_row = vel_ref[pl.ds(block_ref[0, tile], 1), :dofs]
        next_row = vel_ref[pl.ds(block_ref[1, tile], 1), dofs:]
        row = jnp.broadcast_to(jnp.concatenate([own_row, next_row], axis=1), (16, 2 * dofs))
        rel = jnp.dot(row.astype(jnp.bfloat16), jac_ref[tile], preferred_element_type=jnp.float32)
        rel_ref[pl.ds(tile, 1), :] = rel[:1]
    trial = old_ref[...] - step_ref[...] * (rel_ref[...] + bias_ref[...])
    lam = project(trial, friction_ref[...], friction_ref.shape[1])
    lam_ref[...] = lam * live_ref[...]
    for tile in range(tiles):
        push_tile(tile, lam_ref, lambda t: jac_ref[t], block_ref, sums_ref)


DEEP = 6
LIMIT = 24 * 1024 * 1024
SMEM = pl.BlockSpec(memory_space=pltpu.SMEM)
VMEM = pl.BlockSpec(memory_space=pltpu.VMEM)


def result_shapes(lam, blocks, dofs):
    return [
        jax.ShapeDtypeStruct(lam.shape, jnp.float32),
        jax.ShapeDtypeStruct((2 * blocks, dofs), jnp.float32),
    ]


def first_push(jacobian, tile_block, tile_count, start, blocks):
    tiles, rows, cols = jacobian.shape
    lam_shape, sums_shape = result_shapes(start, blocks, rows // 2)
    held = [
        pltpu.with_memory_space_constraint(array, pltpu.HBM)
        for array in (tile_block, jacobian, start)
    ]
    return pl.pallas_call(
        first_kernel,
        out_shape=[pltpu.VMEM(jacobian.shape, jacobian.dtype), lam_shape, lam_shape, sums_shape],
        in_specs=[SMEM] + [pl.BlockSpec(memory_space=pltpu.HBM)] * 3,
        out_specs=[VMEM] * 4,
        scratch_shapes=[
            pltpu.SMEM(tile_block.shape, jnp.int32),
            pltpu.SemaphoreType.DMA((tiles,)),
            pltpu.SemaphoreType.DMA((2,)),
        ],
        compiler_params=pltpu.CompilerParams(vmem_limit_bytes=LIMIT),
        cost_estimate=pl.CostEstimate(
            flops=2 * jacobian.size, bytes_accessed=2 * jacobian.size, transcendentals=0
        ),
        name="first_push",
    )(tile_count, *held)


def sweep_step(kept, tile_block, live, free, mass, beside, bias, step, friction, lam, total):
    blocks, dofs = free.shape
    kept = pltpu.with_memory_space_constraint(kept, pltpu.VMEM)
    return pl.pallas_call(
        sweep_kernel,
        out_shape=result_shapes(lam, blocks, dofs),
        in_specs=[SMEM] + [VMEM] * 10,
        out_specs=[VMEM] * 2,
        scratch_shapes=[
            pltpu.VMEM((blocks, 2 * dofs), jnp.float32),
            pltpu.VMEM(lam.shape, jnp.float32),
        ],
        compiler_params=pltpu.CompilerParams(vmem_limit_bytes=LIMIT),
        cost_estimate=pl.CostEstimate(
            flops=4 * kept.size, bytes_accessed=4 * kept.size, transcendentals=0
        ),
        name="sweep_step",
    )(tile_block, live, kept, free, mass, beside, bias, step, friction, lam, total)


def per_device(
    jacobian, tile_block, tile_count, vel_free, inv_mass, bias, step_scale, friction, impulse_start
):
    tiles, sides, dofs, rows = jacobian.shape
    blocks = vel_free.shape[0]
    flat = jacobian.reshape(tiles, sides * dofs, rows)
    tile_block = tile_block.T
    beside = shifted(jnp.concatenate([vel_free, inv_mass]), "body", -1)
    kept, live, lam, sums = first_push(flat, tile_block, tile_count, impulse_start, blocks)
    beside, sums = lax.optimization_barrier((beside, sums))
    for sweep in range(ITERS):
        both = pair_sum(sums)
        own, later = both[:blocks], both[blocks:]
        from_last, from_next = traded(rounded(later), rounded(own))
        total = over_pairs(jnp.concatenate([own + from_last, later + from_next]))
        lam, sums = sweep_step(
            kept, tile_block, live, vel_free, inv_mass, beside,
            bias, step_scale, friction, lam, total,
        )
    both = pair_sum(sums)
    from_last = crossed(rounded(both[blocks:]), ahead_of)
    total = over_pairs(both[:blocks] + from_last)
    velocity = vel_free + inv_mass * total
    return (lam, velocity)


def solution(mesh):
    placed = (
        P(("contact", "body"), None, None, None),
        P(("contact", "body"), None),
        P(("contact", "body")),
        P("body", None),
        P("body", None),
        P(("contact", "body"), None),
        P(("contact", "body"), None),
        P(("contact", "body"), None),
        P(("contact", "body"), None),
    )
    return jax.shard_map(
        per_device,
        mesh=mesh,
        in_specs=placed,
        out_specs=(P(("contact", "body"), None), P("body", None)),
        check_vma=False,
    )
```

```python
import jax
import jax.numpy as jnp
from jax import lax
from jax.experimental import pallas as pl
from jax.experimental.pallas import tpu as pltpu
from jax.sharding import PartitionSpec as P

ITERS = 2


def shifted(value, axis, steps):
    count = lax.axis_size(axis)
    pairs = [(source, (source + steps) % count) for source in range(count)]
    return lax.ppermute(value, axis, pairs)


def crossed(value, target):
    count, groups = lax.axis_size("body"), lax.axis_size("contact")
    cross = 1 if groups % 2 == 0 else 0
    pairs = [
        (group * count + place, (group ^ cross) * count + target(place) % count)
        for group in range(groups)
        for place in range(count)
    ]
    return lax.ppermute(value, ("contact", "body"), pairs)


def ahead_of(place):
    return place + 1


def traded(ahead, back, even):
    if lax.axis_size("body") % 2:
        return crossed(ahead, ahead_of), crossed(back, lambda place: place - 1)
    wide = crossed(jnp.where(even, back, ahead), lambda place: place + 2 * (place % 2) - 1)
    near = crossed(jnp.where(even, ahead, back), lambda place: place ^ 1)
    return jnp.where(even, wide, near), jnp.where(even, near, wide)


def rounded(value):
    return value.astype(jnp.bfloat16)


def tree(values):
    while len(values) > 1:
        values = [left + right for left, right in zip(values[::2], values[1::2])]
    return values[0]


def pair_sum(value):
    count = lax.axis_size("contact")
    if count % 2:
        return value
    return value + lax.ppermute(value, "contact", [(place, place ^ 1) for place in range(count)])


def over_pairs(value):
    count = lax.axis_size("contact")
    if count & (count - 1):
        mine = (lax.axis_index("contact") & 1) == 0
        return lax.psum(value if count % 2 else jnp.where(mine, value, 0.0), "contact")
    stride = 2
    while stride < count:
        radix = min(count // stride, 4)
        parts = [rounded(value)]
        for digit in range(1, radix):
            pairs = [(place, place ^ (digit * stride) ^ 1) for place in range(count)]
            parts.append(lax.ppermute(rounded(value), "contact", pairs))
        value = tree([part.astype(jnp.float32) for part in parts])
        stride *= radix
    return value


def project(trial, friction, contacts):
    normal = trial[:, :contacts]
    first = trial[:, contacts : 2 * contacts]
    second = trial[:, 2 * contacts :]
    tangent = jnp.sqrt(first * first + second * second)
    inside = tangent <= friction * normal
    below = friction * tangent <= -normal
    moved = (normal + friction * tangent) / (1.0 + friction * friction)
    safe = jnp.where(inside | below, 1.0, tangent)
    factor = jnp.where(inside, 1.0, jnp.where(below, 0.0, friction * moved / safe))
    new_normal = jnp.where(inside, normal, jnp.where(below, 0.0, moved))
    return jnp.concatenate([new_normal, first * factor, second * factor], axis=1)


def push_tile(tile, lam_ref, rows_of, block_ref, sums_ref):
    blocks, dofs = sums_ref.shape[0] // 2, sums_ref.shape[1]
    row = jnp.broadcast_to(lam_ref[pl.ds(tile, 1), :], (16, lam_ref.shape[1]))
    push = lax.dot_general(
        row.astype(jnp.bfloat16),
        rows_of(tile),
        (((1,), (1,)), ((), ())),
        preferred_element_type=jnp.float32,
    )
    sums_ref[pl.ds(block_ref[0, tile], 1), :] += push[:1, :dofs]
    sums_ref[pl.ds(blocks + block_ref[1, tile], 1), :] += push[:1, dofs:]


def first_kernel(
    count_ref, block_ref, jac_ref, start_ref, kept_ref, live_ref, lam_ref, sums_ref,
    block, sems, small_sems,
):
    tiles = start_ref.shape[0]
    small = [
        pltpu.make_async_copy(source, target, small_sems.at[place])
        for place, (source, target) in enumerate(
            [(block_ref, block), (start_ref, lam_ref)]
        )
    ]
    copies = [
        pltpu.make_async_copy(jac_ref.at[tile], kept_ref.at[tile], sems.at[tile])
        for tile in range(tiles)
    ]
    for copy in small + copies[:DEEP]:
        copy.start()
    sums_ref[...] = jnp.zeros_like(sums_ref)
    for copy in small:
        copy.wait()
    order = lax.broadcasted_iota(jnp.int32, lam_ref.shape, 0)
    live_ref[...] = jnp.where(order < count_ref[0], 1.0, 0.0)
    lam_ref[...] = lam_ref[...] * live_ref[...]
    for tile in range(tiles):
        copies[tile].wait()
        if tile + DEEP < tiles:
            copies[tile + DEEP].start()
        push_tile(tile, lam_ref, lambda t: kept_ref[t], block, sums_ref)


def sweep_kernel(
    block_ref, live_ref, jac_ref, free_ref, mass_ref, beside_ref,
    bias_ref, step_ref, friction_ref, old_ref, total_ref,
    lam_ref, sums_ref, vel_ref, rel_ref,
):
    tiles = old_ref.shape[0]
    blocks, dofs = free_ref.shape
    total = total_ref[...]
    own_vel = free_ref[...] + mass_ref[...] * total[:blocks]
    next_vel = beside_ref[:blocks] + beside_ref[blocks:] * total[blocks:]
    vel_ref[:, :dofs] = own_vel
    vel_ref[:, dofs:] = next_vel
    sums_ref[...] = jnp.zeros_like(sums_ref)
    for tile in range(tiles):
        own_row = vel_ref[pl.ds(block_ref[0, tile], 1), :dofs]
        next_row = vel_ref[pl.ds(block_ref[1, tile], 1), dofs:]
        row = jnp.broadcast_to(jnp.concatenate([own_row, next_row], axis=1), (16, 2 * dofs))
        rel = jnp.dot(row.astype(jnp.bfloat16), jac_ref[tile], preferred_element_type=jnp.float32)
        rel_ref[pl.ds(tile, 1), :] = rel[:1]
    trial = old_ref[...] - step_ref[...] * (rel_ref[...] + bias_ref[...])
    lam = project(trial, friction_ref[...], friction_ref.shape[1])
    lam_ref[...] = lam * live_ref[...]
    for tile in range(tiles):
        push_tile(tile, lam_ref, lambda t: jac_ref[t], block_ref, sums_ref)


DEEP = 6
LIMIT = 24 * 1024 * 1024
SMEM = pl.BlockSpec(memory_space=pltpu.SMEM)
VMEM = pl.BlockSpec(memory_space=pltpu.VMEM)


def result_shapes(lam, blocks, dofs):
    return [
        jax.ShapeDtypeStruct(lam.shape, jnp.float32),
        jax.ShapeDtypeStruct((2 * blocks, dofs), jnp.float32),
    ]


def first_push(jacobian, tile_block, tile_count, start, blocks):
    tiles, rows, cols = jacobian.shape
    lam_shape, sums_shape = result_shapes(start, blocks, rows // 2)
    held = [
        pltpu.with_memory_space_constraint(array, pltpu.HBM)
        for array in (tile_block, jacobian, start)
    ]
    return pl.pallas_call(
        first_kernel,
        out_shape=[pltpu.VMEM(jacobian.shape, jacobian.dtype), lam_shape, lam_shape, sums_shape],
        in_specs=[SMEM] + [pl.BlockSpec(memory_space=pltpu.HBM)] * 3,
        out_specs=[VMEM] * 4,
        scratch_shapes=[
            pltpu.SMEM(tile_block.shape, jnp.int32),
            pltpu.SemaphoreType.DMA((tiles,)),
            pltpu.SemaphoreType.DMA((2,)),
        ],
        compiler_params=pltpu.CompilerParams(vmem_limit_bytes=LIMIT),
        cost_estimate=pl.CostEstimate(
            flops=2 * jacobian.size, bytes_accessed=2 * jacobian.size, transcendentals=0
        ),
        name="first_push",
    )(tile_count, *held)


def sweep_step(kept, tile_block, live, free, mass, beside, bias, step, friction, lam, total):
    blocks, dofs = free.shape
    kept = pltpu.with_memory_space_constraint(kept, pltpu.VMEM)
    return pl.pallas_call(
        sweep_kernel,
        out_shape=result_shapes(lam, blocks, dofs),
        in_specs=[SMEM] + [VMEM] * 10,
        out_specs=[VMEM] * 2,
        scratch_shapes=[
            pltpu.VMEM((blocks, 2 * dofs), jnp.float32),
            pltpu.VMEM(lam.shape, jnp.float32),
        ],
        compiler_params=pltpu.CompilerParams(vmem_limit_bytes=LIMIT),
        cost_estimate=pl.CostEstimate(
            flops=4 * kept.size, bytes_accessed=4 * kept.size, transcendentals=0
        ),
        name="sweep_step",
    )(tile_block, live, kept, free, mass, beside, bias, step, friction, lam, total)


def per_device(
    jacobian, tile_block, tile_count, vel_free, inv_mass, bias, step_scale, friction, impulse_start
):
    tiles, sides, dofs, rows = jacobian.shape
    blocks = vel_free.shape[0]
    flat = jacobian.reshape(tiles, sides * dofs, rows)
    even = (lax.axis_index("body") & 1) == 0
    even, tile_block = lax.optimization_barrier((even, tile_block.T))
    beside = shifted(jnp.concatenate([vel_free, inv_mass]), "body", -1)
    kept, live, lam, sums = first_push(flat, tile_block, tile_count, impulse_start, blocks)
    beside, sums = lax.optimization_barrier((beside, sums))
    for sweep in range(ITERS):
        both = pair_sum(sums)
        own, later = both[:blocks], both[blocks:]
        from_last, from_next = traded(rounded(later), rounded(own), even)
        total = over_pairs(jnp.concatenate([own + from_last, later + from_next]))
        lam, sums = sweep_step(
            kept, tile_block, live, vel_free, inv_mass, beside,
            bias, step_scale, friction, lam, total,
        )
    both = pair_sum(sums)
    from_last = crossed(rounded(both[blocks:]), ahead_of)
    total = over_pairs(both[:blocks] + from_last)
    velocity = vel_free + inv_mass * total
    return (lam, velocity)


def solution(mesh):
    placed = (
        P(("contact", "body"), None, None, None),
        P(("contact", "body"), None),
        P(("contact", "body")),
        P("body", None),
        P("body", None),
        P(("contact", "body"), None),
        P(("contact", "body"), None),
        P(("contact", "body"), None),
        P(("contact", "body"), None),
    )
    return jax.shard_map(
        per_device,
        mesh=mesh,
        in_specs=placed,
        out_specs=(P(("contact", "body"), None), P("body", None)),
        check_vma=False,
    )
```

```python
import jax
import jax.numpy as jnp
from jax import lax
from jax.experimental import pallas as pl
from jax.experimental.pallas import tpu as pltpu
from jax.sharding import PartitionSpec as P

ITERS = 2


def shifted(value, axis, steps):
    count = lax.axis_size(axis)
    pairs = [(source, (source + steps) % count) for source in range(count)]
    return lax.ppermute(value, axis, pairs)


def crossed(value, target):
    count, groups = lax.axis_size("body"), lax.axis_size("contact")
    cross = 1 if groups % 2 == 0 else 0
    pairs = [
        (group * count + place, (group ^ cross) * count + target(place) % count)
        for group in range(groups)
        for place in range(count)
    ]
    return lax.ppermute(value, ("contact", "body"), pairs)


def ahead_of(place):
    return place + 1


def traded(ahead, back, even):
    if lax.axis_size("body") % 2:
        return crossed(ahead, ahead_of), crossed(back, lambda place: place - 1)
    wide = crossed(jnp.where(even, back, ahead), lambda place: place + 2 * (place % 2) - 1)
    near = crossed(jnp.where(even, ahead, back), lambda place: place ^ 1)
    return jnp.where(even, wide, near), jnp.where(even, near, wide)


def rounded(value):
    return value.astype(jnp.bfloat16)


def tree(values):
    while len(values) > 1:
        values = [left + right for left, right in zip(values[::2], values[1::2])]
    return values[0]


def pair_sum(value):
    count = lax.axis_size("contact")
    if count % 2:
        return value
    return value + lax.ppermute(value, "contact", [(place, place ^ 1) for place in range(count)])


def over_pairs(value):
    count = lax.axis_size("contact")
    if count & (count - 1):
        mine = (lax.axis_index("contact") & 1) == 0
        return lax.psum(value if count % 2 else jnp.where(mine, value, 0.0), "contact")
    stride = 2
    while stride < count:
        radix = min(count // stride, 4)
        parts = []
        for digit in range(1, radix):
            pairs = [(place, place ^ (digit * stride) ^ 1) for place in range(count)]
            parts.append(lax.ppermute(rounded(value), "contact", pairs))
        parts.append(rounded(value))
        value = tree([part.astype(jnp.float32) for part in parts])
        stride *= radix
    return value


def project(trial, friction, contacts):
    normal = trial[:, :contacts]
    first = trial[:, contacts : 2 * contacts]
    second = trial[:, 2 * contacts :]
    tangent = jnp.sqrt(first * first + second * second)
    inside = tangent <= friction * normal
    below = friction * tangent <= -normal
    moved = (normal + friction * tangent) / (1.0 + friction * friction)
    safe = jnp.where(inside | below, 1.0, tangent)
    factor = jnp.where(inside, 1.0, jnp.where(below, 0.0, friction * moved / safe))
    new_normal = jnp.where(inside, normal, jnp.where(below, 0.0, moved))
    return jnp.concatenate([new_normal, first * factor, second * factor], axis=1)


def push_tile(tile, lam_ref, turned_ref, block_ref, sums_ref):
    blocks, dofs = sums_ref.shape[0] // 2, sums_ref.shape[1]
    row = jnp.broadcast_to(lam_ref[pl.ds(tile, 1), :], (16, lam_ref.shape[1]))
    push = jnp.dot(
        row.astype(jnp.bfloat16), turned_ref[tile], preferred_element_type=jnp.float32
    )
    sums_ref[pl.ds(block_ref[0, tile], 1), :] += push[:1, :dofs]
    sums_ref[pl.ds(blocks + block_ref[1, tile], 1), :] += push[:1, dofs:]


def first_kernel(
    count_ref, block_ref, jac_ref, start_ref, kept_ref, turned_ref, live_ref, lam_ref, sums_ref,
    block, sems, small_sems,
):
    tiles = start_ref.shape[0]
    small = [
        pltpu.make_async_copy(source, target, small_sems.at[place])
        for place, (source, target) in enumerate(
            [(block_ref, block), (start_ref, lam_ref)]
        )
    ]
    copies = [
        pltpu.make_async_copy(jac_ref.at[tile], kept_ref.at[tile], sems.at[tile])
        for tile in range(tiles)
    ]
    groups = [range(first, min(first + GROUP, tiles)) for first in range(0, tiles, GROUP)]
    for copy in small + copies[: 2 * GROUP]:
        copy.start()
    sums_ref[...] = jnp.zeros_like(sums_ref)
    for copy in small:
        copy.wait()
    order = lax.broadcasted_iota(jnp.int32, lam_ref.shape, 0)
    live_ref[...] = jnp.where(order < count_ref[0], 1.0, 0.0)
    lam_ref[...] = lam_ref[...] * live_ref[...]
    for group in groups:
        for tile in group:
            copies[tile].wait()
        for copy in copies[group[0] + 2 * GROUP : group[0] + 3 * GROUP]:
            copy.start()
        for tile in group:
            turned_ref[tile] = kept_ref[tile].T
        for tile in group:
            push_tile(tile, lam_ref, turned_ref, block, sums_ref)


def sweep_kernel(
    block_ref, live_ref, jac_ref, turned_ref, free_ref, mass_ref, beside_ref,
    bias_ref, step_ref, friction_ref, old_ref, total_ref,
    lam_ref, sums_ref, vel_ref, rel_ref,
):
    tiles = old_ref.shape[0]
    blocks, dofs = free_ref.shape
    total = total_ref[...]
    own_vel = free_ref[...] + mass_ref[...] * total[:blocks]
    next_vel = beside_ref[:blocks] + beside_ref[blocks:] * total[blocks:]
    vel_ref[:, :dofs] = own_vel
    vel_ref[:, dofs:] = next_vel
    sums_ref[...] = jnp.zeros_like(sums_ref)
    for tile in range(tiles):
        own_row = vel_ref[pl.ds(block_ref[0, tile], 1), :dofs]
        next_row = vel_ref[pl.ds(block_ref[1, tile], 1), dofs:]
        row = jnp.broadcast_to(jnp.concatenate([own_row, next_row], axis=1), (16, 2 * dofs))
        rel = jnp.dot(row.astype(jnp.bfloat16), jac_ref[tile], preferred_element_type=jnp.float32)
        rel_ref[pl.ds(tile, 1), :] = rel[:1]
    trial = old_ref[...] - step_ref[...] * (rel_ref[...] + bias_ref[...])
    lam = project(trial, friction_ref[...], friction_ref.shape[1])
    lam_ref[...] = lam * live_ref[...]
    for tile in range(tiles):
        push_tile(tile, lam_ref, turned_ref, block_ref, sums_ref)


GROUP = 4
LIMIT = 24 * 1024 * 1024
SMEM = pl.BlockSpec(memory_space=pltpu.SMEM)
VMEM = pl.BlockSpec(memory_space=pltpu.VMEM)


def result_shapes(lam, blocks, dofs):
    return [
        jax.ShapeDtypeStruct(lam.shape, jnp.float32),
        jax.ShapeDtypeStruct((2 * blocks, dofs), jnp.float32),
    ]


def first_push(jacobian, tile_block, tile_count, start, blocks):
    tiles, rows, cols = jacobian.shape
    lam_shape, sums_shape = result_shapes(start, blocks, rows // 2)
    held = [
        pltpu.with_memory_space_constraint(array, pltpu.HBM)
        for array in (tile_block, jacobian, start)
    ]
    return pl.pallas_call(
        first_kernel,
        out_shape=[
            pltpu.VMEM((tiles, rows, cols), jacobian.dtype),
            pltpu.VMEM((tiles, cols, rows), jacobian.dtype),
            lam_shape, lam_shape, sums_shape,
        ],
        in_specs=[SMEM] + [pl.BlockSpec(memory_space=pltpu.HBM)] * 3,
        out_specs=[VMEM] * 5,
        scratch_shapes=[
            pltpu.SMEM(tile_block.shape, jnp.int32),
            pltpu.SemaphoreType.DMA((tiles,)),
            pltpu.SemaphoreType.DMA((2,)),
        ],
        compiler_params=pltpu.CompilerParams(vmem_limit_bytes=LIMIT),
        cost_estimate=pl.CostEstimate(
            flops=2 * jacobian.size, bytes_accessed=2 * jacobian.size, transcendentals=0
        ),
        name="first_push",
    )(tile_count, *held)


def sweep_step(kept, turned, tile_block, live, free, mass, beside, bias, step, friction, lam, total):
    blocks, dofs = free.shape
    kept = pltpu.with_memory_space_constraint(kept, pltpu.VMEM)
    turned = pltpu.with_memory_space_constraint(turned, pltpu.VMEM)
    return pl.pallas_call(
        sweep_kernel,
        out_shape=result_shapes(lam, blocks, dofs),
        in_specs=[SMEM] + [VMEM] * 11,
        out_specs=[VMEM] * 2,
        scratch_shapes=[
            pltpu.VMEM((blocks, 2 * dofs), jnp.float32),
            pltpu.VMEM(lam.shape, jnp.float32),
        ],
        compiler_params=pltpu.CompilerParams(vmem_limit_bytes=LIMIT),
        cost_estimate=pl.CostEstimate(
            flops=4 * kept.size, bytes_accessed=4 * kept.size, transcendentals=0
        ),
        name="sweep_step",
    )(tile_block, live, kept, turned, free, mass, beside, bias, step, friction, lam, total)


def per_device(
    jacobian, tile_block, tile_count, vel_free, inv_mass, bias, step_scale, friction, impulse_start
):
    tiles, sides, dofs, rows = jacobian.shape
    blocks = vel_free.shape[0]
    flat = jacobian.reshape(tiles, sides * dofs, rows)
    even = (lax.axis_index("body") & 1) == 0
    even, tile_block = lax.optimization_barrier((even, tile_block.T))
    beside = shifted(jnp.concatenate([vel_free, inv_mass]), "body", -1)
    kept, turned, live, lam, sums = first_push(flat, tile_block, tile_count, impulse_start, blocks)
    beside, sums = lax.optimization_barrier((beside, sums))
    for sweep in range(ITERS):
        both = pair_sum(sums)
        own, later = both[:blocks], both[blocks:]
        from_last, from_next = traded(rounded(later), rounded(own), even)
        total = over_pairs(jnp.concatenate([own + from_last, later + from_next]))
        lam, sums = sweep_step(
            kept, turned, tile_block, live, vel_free, inv_mass, beside,
            bias, step_scale, friction, lam, total,
        )
    both = pair_sum(sums)
    from_last = crossed(rounded(both[blocks:]), ahead_of)
    total = over_pairs(both[:blocks] + from_last)
    velocity = vel_free + inv_mass * total
    return (lam, velocity)


def solution(mesh):
    placed = (
        P(("contact", "body"), None, None, None),
        P(("contact", "body"), None),
        P(("contact", "body")),
        P("body", None),
        P("body", None),
        P(("contact", "body"), None),
        P(("contact", "body"), None),
        P(("contact", "body"), None),
        P(("contact", "body"), None),
    )
    return jax.shard_map(
        per_device,
        mesh=mesh,
        in_specs=placed,
        out_specs=(P(("contact", "body"), None), P("body", None)),
        check_vma=False,
    )
```

```python
import jax
import jax.numpy as jnp
from jax import lax
from jax.experimental import pallas as pl
from jax.experimental.pallas import tpu as pltpu
from jax.sharding import PartitionSpec as P

ITERS = 2


def shifted(value, axis, steps):
    count = lax.axis_size(axis)
    pairs = [(source, (source + steps) % count) for source in range(count)]
    return lax.ppermute(value, axis, pairs)


def crossed(value, target):
    count, groups = lax.axis_size("body"), lax.axis_size("contact")
    cross = 1 if groups % 2 == 0 else 0
    pairs = [
        (group * count + place, (group ^ cross) * count + target(place) % count)
        for group in range(groups)
        for place in range(count)
    ]
    return lax.ppermute(value, ("contact", "body"), pairs)


def ahead_of(place):
    return place + 1


def traded(ahead, back, even):
    if lax.axis_size("body") % 2:
        return crossed(ahead, ahead_of), crossed(back, lambda place: place - 1)
    wide = crossed(jnp.where(even, back, ahead), lambda place: place + 2 * (place % 2) - 1)
    near = crossed(jnp.where(even, ahead, back), lambda place: place ^ 1)
    return jnp.where(even, wide, near), jnp.where(even, near, wide)


def rounded(value):
    return value.astype(jnp.bfloat16)


def tree(values):
    while len(values) > 1:
        values = [left + right for left, right in zip(values[::2], values[1::2])]
    return values[0]


def pair_sum(value):
    count = lax.axis_size("contact")
    if count % 2:
        return value
    return value + lax.ppermute(value, "contact", [(place, place ^ 1) for place in range(count)])


def over_pairs(value):
    count = lax.axis_size("contact")
    if count & (count - 1):
        mine = (lax.axis_index("contact") & 1) == 0
        return lax.psum(value if count % 2 else jnp.where(mine, value, 0.0), "contact")
    stride = 2
    while stride < count:
        radix = min(count // stride, 4)
        groups = [
            [base + digit * stride ^ (digit.bit_count() & 1) for digit in range(radix)]
            for base in range(count)
            if base // stride % radix == 0
        ]
        copies = jnp.broadcast_to(rounded(value), (radix,) + value.shape)
        parts = lax.all_to_all(copies, "contact", 0, 0, axis_index_groups=groups)
        value = tree([parts[digit].astype(jnp.float32) for digit in range(radix)])
        stride *= radix
    return value


def project(trial, friction, contacts):
    normal = trial[:, :contacts]
    first = trial[:, contacts : 2 * contacts]
    second = trial[:, 2 * contacts :]
    tangent = jnp.sqrt(first * first + second * second)
    inside = tangent <= friction * normal
    below = friction * tangent <= -normal
    moved = (normal + friction * tangent) / (1.0 + friction * friction)
    safe = jnp.where(inside | below, 1.0, tangent)
    factor = jnp.where(inside, 1.0, jnp.where(below, 0.0, friction * moved / safe))
    new_normal = jnp.where(inside, normal, jnp.where(below, 0.0, moved))
    return jnp.concatenate([new_normal, first * factor, second * factor], axis=1)


def push_tile(tile, lam_ref, turned_ref, block_ref, sums_ref):
    blocks, dofs = sums_ref.shape[0] // 2, sums_ref.shape[1]
    row = jnp.broadcast_to(lam_ref[pl.ds(tile, 1), :], (16, lam_ref.shape[1]))
    push = jnp.dot(
        row.astype(jnp.bfloat16), turned_ref[tile], preferred_element_type=jnp.float32
    )
    sums_ref[pl.ds(block_ref[0, tile], 1), :] += push[:1, :dofs]
    sums_ref[pl.ds(blocks + block_ref[1, tile], 1), :] += push[:1, dofs:]


def first_kernel(
    count_ref, block_ref, jac_ref, start_ref, kept_ref, turned_ref, live_ref, lam_ref, sums_ref,
    block, sems, small_sems,
):
    tiles = start_ref.shape[0]
    small = [
        pltpu.make_async_copy(source, target, small_sems.at[place])
        for place, (source, target) in enumerate(
            [(block_ref, block), (start_ref, lam_ref)]
        )
    ]
    copies = [
        pltpu.make_async_copy(jac_ref.at[tile], kept_ref.at[tile], sems.at[tile])
        for tile in range(tiles)
    ]
    groups = [range(first, min(first + GROUP, tiles)) for first in range(0, tiles, GROUP)]
    for copy in small + copies[: 2 * GROUP]:
        copy.start()
    sums_ref[...] = jnp.zeros_like(sums_ref)
    for copy in small:
        copy.wait()
    order = lax.broadcasted_iota(jnp.int32, lam_ref.shape, 0)
    live_ref[...] = jnp.where(order < count_ref[0], 1.0, 0.0)
    lam_ref[...] = lam_ref[...] * live_ref[...]
    for group in groups:
        for tile in group:
            copies[tile].wait()
        for copy in copies[group[0] + 2 * GROUP : group[0] + 3 * GROUP]:
            copy.start()
        for tile in group:
            turned_ref[tile] = kept_ref[tile].T
        for tile in group:
            push_tile(tile, lam_ref, turned_ref, block, sums_ref)


def sweep_kernel(
    block_ref, live_ref, jac_ref, turned_ref, free_ref, mass_ref, beside_ref,
    bias_ref, step_ref, friction_ref, old_ref, total_ref,
    lam_ref, sums_ref, vel_ref, rel_ref,
):
    tiles = old_ref.shape[0]
    blocks, dofs = free_ref.shape
    total = total_ref[...]
    own_vel = free_ref[...] + mass_ref[...] * total[:blocks]
    next_vel = beside_ref[:blocks] + beside_ref[blocks:] * total[blocks:]
    vel_ref[:, :dofs] = own_vel
    vel_ref[:, dofs:] = next_vel
    sums_ref[...] = jnp.zeros_like(sums_ref)
    for tile in range(tiles):
        own_row = vel_ref[pl.ds(block_ref[0, tile], 1), :dofs]
        next_row = vel_ref[pl.ds(block_ref[1, tile], 1), dofs:]
        row = jnp.broadcast_to(jnp.concatenate([own_row, next_row], axis=1), (16, 2 * dofs))
        rel = jnp.dot(row.astype(jnp.bfloat16), jac_ref[tile], preferred_element_type=jnp.float32)
        rel_ref[pl.ds(tile, 1), :] = rel[:1]
    trial = old_ref[...] - step_ref[...] * (rel_ref[...] + bias_ref[...])
    lam = project(trial, friction_ref[...], friction_ref.shape[1])
    lam_ref[...] = lam * live_ref[...]
    for tile in range(tiles):
        push_tile(tile, lam_ref, turned_ref, block_ref, sums_ref)


GROUP = 4
LIMIT = 24 * 1024 * 1024
SMEM = pl.BlockSpec(memory_space=pltpu.SMEM)
VMEM = pl.BlockSpec(memory_space=pltpu.VMEM)


def result_shapes(lam, blocks, dofs):
    return [
        jax.ShapeDtypeStruct(lam.shape, jnp.float32),
        jax.ShapeDtypeStruct((2 * blocks, dofs), jnp.float32),
    ]


def first_push(jacobian, tile_block, tile_count, start, blocks):
    tiles, rows, cols = jacobian.shape
    lam_shape, sums_shape = result_shapes(start, blocks, rows // 2)
    held = [
        pltpu.with_memory_space_constraint(array, pltpu.HBM)
        for array in (tile_block, jacobian, start)
    ]
    return pl.pallas_call(
        first_kernel,
        out_shape=[
            pltpu.VMEM((tiles, rows, cols), jacobian.dtype),
            pltpu.VMEM((tiles, cols, rows), jacobian.dtype),
            lam_shape, lam_shape, sums_shape,
        ],
        in_specs=[SMEM] + [pl.BlockSpec(memory_space=pltpu.HBM)] * 3,
        out_specs=[VMEM] * 5,
        scratch_shapes=[
            pltpu.SMEM(tile_block.shape, jnp.int32),
            pltpu.SemaphoreType.DMA((tiles,)),
            pltpu.SemaphoreType.DMA((2,)),
        ],
        compiler_params=pltpu.CompilerParams(vmem_limit_bytes=LIMIT),
        cost_estimate=pl.CostEstimate(
            flops=2 * jacobian.size, bytes_accessed=2 * jacobian.size, transcendentals=0
        ),
        name="first_push",
    )(tile_count, *held)


def sweep_step(kept, turned, tile_block, live, free, mass, beside, bias, step, friction, lam, total):
    blocks, dofs = free.shape
    kept = pltpu.with_memory_space_constraint(kept, pltpu.VMEM)
    turned = pltpu.with_memory_space_constraint(turned, pltpu.VMEM)
    return pl.pallas_call(
        sweep_kernel,
        out_shape=result_shapes(lam, blocks, dofs),
        in_specs=[SMEM] + [VMEM] * 11,
        out_specs=[VMEM] * 2,
        scratch_shapes=[
            pltpu.VMEM((blocks, 2 * dofs), jnp.float32),
            pltpu.VMEM(lam.shape, jnp.float32),
        ],
        compiler_params=pltpu.CompilerParams(vmem_limit_bytes=LIMIT),
        cost_estimate=pl.CostEstimate(
            flops=4 * kept.size, bytes_accessed=4 * kept.size, transcendentals=0
        ),
        name="sweep_step",
    )(tile_block, live, kept, turned, free, mass, beside, bias, step, friction, lam, total)


def per_device(
    jacobian, tile_block, tile_count, vel_free, inv_mass, bias, step_scale, friction, impulse_start
):
    tiles, sides, dofs, rows = jacobian.shape
    blocks = vel_free.shape[0]
    flat = jacobian.reshape(tiles, sides * dofs, rows)
    even = (lax.axis_index("body") & 1) == 0
    even, tile_block = lax.optimization_barrier((even, tile_block.T))
    beside = shifted(jnp.concatenate([vel_free, inv_mass]), "body", -1)
    kept, turned, live, lam, sums = first_push(flat, tile_block, tile_count, impulse_start, blocks)
    beside, sums = lax.optimization_barrier((beside, sums))
    for sweep in range(ITERS):
        both = pair_sum(sums)
        own, later = both[:blocks], both[blocks:]
        from_last, from_next = traded(rounded(later), rounded(own), even)
        total = over_pairs(jnp.concatenate([own + from_last, later + from_next]))
        lam, sums = sweep_step(
            kept, turned, tile_block, live, vel_free, inv_mass, beside,
            bias, step_scale, friction, lam, total,
        )
    both = pair_sum(sums)
    from_last = crossed(rounded(both[blocks:]), ahead_of)
    total = over_pairs(both[:blocks] + from_last)
    velocity = vel_free + inv_mass * total
    return (lam, velocity)


def solution(mesh):
    placed = (
        P(("contact", "body"), None, None, None),
        P(("contact", "body"), None),
        P(("contact", "body")),
        P("body", None),
        P("body", None),
        P(("contact", "body"), None),
        P(("contact", "body"), None),
        P(("contact", "body"), None),
        P(("contact", "body"), None),
    )
    return jax.shard_map(
        per_device,
        mesh=mesh,
        in_specs=placed,
        out_specs=(P(("contact", "body"), None), P("body", None)),
        check_vma=False,
    )
```

```python
import functools

import jax
import jax.numpy as jnp
from jax import lax
from jax.experimental import pallas as pl
from jax.experimental.pallas import tpu as pltpu
from jax.sharding import PartitionSpec as P

ITERS = 2


def shifted(value, axis, steps):
    count = lax.axis_size(axis)
    pairs = [(source, (source + steps) % count) for source in range(count)]
    return lax.ppermute(value, axis, pairs)


def crossed(value, target):
    count, groups = lax.axis_size("body"), lax.axis_size("contact")
    cross = 1 if groups % 2 == 0 else 0
    pairs = [
        (group * count + place, (group ^ cross) * count + target(place) % count)
        for group in range(groups)
        for place in range(count)
    ]
    return lax.ppermute(value, ("contact", "body"), pairs)


def ahead_of(place):
    return place + 1


def traded(ahead, back, even):
    if lax.axis_size("body") % 2:
        return crossed(ahead, ahead_of), crossed(back, lambda place: place - 1)
    far, close = lax.optimization_barrier(
        (jnp.where(even, back, ahead), jnp.where(even, ahead, back))
    )
    wide = crossed(far, lambda place: place + 2 * (place % 2) - 1)
    near = crossed(close, lambda place: place ^ 1)
    return jnp.where(even, wide, near), jnp.where(even, near, wide)


def rounded(value):
    return value.astype(jnp.bfloat16)


def tree(values):
    while len(values) > 1:
        values = [left + right for left, right in zip(values[::2], values[1::2])]
    return values[0]


def pair_sum(value):
    count = lax.axis_size("contact")
    if count % 2:
        return value
    return value + lax.ppermute(value, "contact", [(place, place ^ 1) for place in range(count)])


def pair_count():
    count = lax.axis_size("contact")
    return count if count % 2 else count // 2


def over_pairs(value):
    count = lax.axis_size("contact")
    if count & (count - 1):
        mine = (lax.axis_index("contact") & 1) == 0
        return [lax.psum(value if count % 2 else jnp.where(mine, value, 0.0), "contact")]
    stride, parts = 2, [value]
    while stride < count:
        radix = min(count // stride, 4)
        value = rounded(tree([part.astype(jnp.float32) for part in parts]))
        parts = []
        for digit in range(1, radix):
            pairs = [(place, place ^ (digit * stride) ^ 1) for place in range(count)]
            parts.append(lax.ppermute(value, "contact", pairs))
        parts.append(value)
        stride *= radix
    return parts


def project(trial, friction, contacts):
    normal = trial[:, :contacts]
    first = trial[:, contacts : 2 * contacts]
    second = trial[:, 2 * contacts :]
    tangent = jnp.sqrt(first * first + second * second)
    inside = tangent <= friction * normal
    below = friction * tangent <= -normal
    moved = (normal + friction * tangent) / (1.0 + friction * friction)
    safe = jnp.where(inside | below, 1.0, tangent)
    factor = jnp.where(inside, 1.0, jnp.where(below, 0.0, friction * moved / safe))
    new_normal = jnp.where(inside, normal, jnp.where(below, 0.0, moved))
    return jnp.concatenate([new_normal, first * factor, second * factor], axis=1)


def push_tile(tile, lam_ref, turned_ref, block_ref, sums_ref):
    blocks, dofs = sums_ref.shape[0] // 2, sums_ref.shape[1]
    row = jnp.broadcast_to(lam_ref[pl.ds(tile, 1), :], (16, lam_ref.shape[1]))
    push = jnp.dot(
        row.astype(jnp.bfloat16), turned_ref[tile], preferred_element_type=jnp.float32
    )
    sums_ref[pl.ds(block_ref[0, tile], 1), :] += push[:1, :dofs]
    sums_ref[pl.ds(blocks + block_ref[1, tile], 1), :] += push[:1, dofs:]


def first_kernel(
    count_ref, block_ref, jac_ref, start_ref, kept_ref, turned_ref, live_ref, lam_ref, sums_ref,
    block, sems, small_sems,
):
    tiles = start_ref.shape[0]
    small = [
        pltpu.make_async_copy(source, target, small_sems.at[place])
        for place, (source, target) in enumerate(
            [(block_ref, block), (start_ref, lam_ref)]
        )
    ]
    copies = [
        pltpu.make_async_copy(jac_ref.at[tile], kept_ref.at[tile], sems.at[tile])
        for tile in range(tiles)
    ]
    cuts = sorted({*range(0, tiles, GROUP), max(tiles - GROUP // 2, 0), tiles})
    started = 2 * GROUP
    for copy in small + copies[:started]:
        copy.start()
    sums_ref[...] = jnp.zeros_like(sums_ref)
    for copy in small:
        copy.wait()
    order = lax.broadcasted_iota(jnp.int32, lam_ref.shape, 0)
    live_ref[...] = jnp.where(order < count_ref[0], 1.0, 0.0)
    lam_ref[...] = lam_ref[...] * live_ref[...]
    for group in [range(first, after) for first, after in zip(cuts, cuts[1:])]:
        for tile in group:
            copies[tile].wait()
        for copy in copies[started : group[-1] + 1 + 2 * GROUP]:
            copy.start()
        started = max(started, group[-1] + 1 + 2 * GROUP)
        for tile in group:
            turned_ref[tile] = kept_ref[tile].T
        for tile in group:
            push_tile(tile, lam_ref, turned_ref, block, sums_ref)


def sweep_kernel(
    parts, block_ref, live_ref, jac_ref, turned_ref, bias_ref, step_ref, friction_ref, old_ref, *refs
):
    part_refs, (lam_ref, sums_ref, vel_ref, rel_ref) = refs[:parts], refs[parts:]
    tiles = old_ref.shape[0]
    blocks, dofs = vel_ref.shape[0] // 2, vel_ref.shape[1]
    vel_ref[...] = tree([ref[...].astype(jnp.float32) for ref in part_refs])
    sums_ref[...] = jnp.zeros_like(sums_ref)
    for tile in range(tiles):
        own_row = vel_ref[pl.ds(block_ref[0, tile], 1), :]
        next_row = vel_ref[pl.ds(blocks + block_ref[1, tile], 1), :]
        row = jnp.broadcast_to(jnp.concatenate([own_row, next_row], axis=1), (16, 2 * dofs))
        rel = jnp.dot(row.astype(jnp.bfloat16), jac_ref[tile], preferred_element_type=jnp.float32)
        rel_ref[pl.ds(tile, 1), :] = rel[:1]
    trial = old_ref[...] - step_ref[...] * (rel_ref[...] + bias_ref[...])
    lam = project(trial, friction_ref[...], friction_ref.shape[1])
    lam_ref[...] = lam * live_ref[...]
    for tile in range(tiles):
        push_tile(tile, lam_ref, turned_ref, block_ref, sums_ref)


GROUP = 4
LIMIT = 24 * 1024 * 1024
SMEM = pl.BlockSpec(memory_space=pltpu.SMEM)
VMEM = pl.BlockSpec(memory_space=pltpu.VMEM)


def result_shapes(lam, blocks, dofs):
    return [
        jax.ShapeDtypeStruct(lam.shape, jnp.float32),
        jax.ShapeDtypeStruct((2 * blocks, dofs), jnp.float32),
    ]


def first_push(jacobian, tile_block, tile_count, start, blocks):
    tiles, rows, cols = jacobian.shape
    lam_shape, sums_shape = result_shapes(start, blocks, rows // 2)
    held = [
        pltpu.with_memory_space_constraint(array, pltpu.HBM)
        for array in (tile_block, jacobian, start)
    ]
    return pl.pallas_call(
        first_kernel,
        out_shape=[
            pltpu.VMEM((tiles, rows, cols), jacobian.dtype),
            pltpu.VMEM((tiles, cols, rows), jacobian.dtype),
            lam_shape, lam_shape, sums_shape,
        ],
        in_specs=[SMEM] + [pl.BlockSpec(memory_space=pltpu.HBM)] * 3,
        out_specs=[VMEM] * 5,
        scratch_shapes=[
            pltpu.SMEM(tile_block.shape, jnp.int32),
            pltpu.SemaphoreType.DMA((tiles,)),
            pltpu.SemaphoreType.DMA((2,)),
        ],
        compiler_params=pltpu.CompilerParams(vmem_limit_bytes=LIMIT),
        cost_estimate=pl.CostEstimate(
            flops=2 * jacobian.size, bytes_accessed=2 * jacobian.size, transcendentals=0
        ),
        name="first_push",
    )(tile_count, *held)


def sweep_step(kept, turned, tile_block, live, bias, step, friction, lam, parts):
    rows, dofs = parts[0].shape
    kept = pltpu.with_memory_space_constraint(kept, pltpu.VMEM)
    turned = pltpu.with_memory_space_constraint(turned, pltpu.VMEM)
    return pl.pallas_call(
        functools.partial(sweep_kernel, len(parts)),
        out_shape=result_shapes(lam, rows // 2, dofs),
        in_specs=[SMEM] + [VMEM] * (7 + len(parts)),
        out_specs=[VMEM] * 2,
        scratch_shapes=[
            pltpu.VMEM((rows, dofs), jnp.float32),
            pltpu.VMEM(lam.shape, jnp.float32),
        ],
        compiler_params=pltpu.CompilerParams(vmem_limit_bytes=LIMIT),
        cost_estimate=pl.CostEstimate(
            flops=4 * kept.size, bytes_accessed=4 * kept.size, transcendentals=0
        ),
        name="sweep_step",
    )(tile_block, live, kept, turned, bias, step, friction, lam, *parts)


def per_device(
    jacobian, tile_block, tile_count, vel_free, inv_mass, bias, step_scale, friction, impulse_start
):
    tiles, sides, dofs, rows = jacobian.shape
    blocks = vel_free.shape[0]
    flat = jacobian.reshape(tiles, sides * dofs, rows)
    even = (lax.axis_index("body") & 1) == 0
    even, tile_block = lax.optimization_barrier((even, tile_block.T))
    mass_next = shifted(inv_mass, "body", -1)
    kept, turned, live, lam, sums = first_push(
        flat, tile_block, tile_count, impulse_start, blocks
    )
    mass_next, sums = lax.optimization_barrier((mass_next, sums))
    share = vel_free * (1.0 / pair_count())
    for sweep in range(ITERS):
        both = pair_sum(sums)
        own, later = both[:blocks], both[blocks:]
        from_last, from_next = traded(rounded(later), rounded(share + inv_mass * own), even)
        parts = over_pairs(
            jnp.concatenate(
                [share + inv_mass * (own + from_last), from_next + mass_next * later]
            )
        )
        lam, sums = sweep_step(
            kept, turned, tile_block, live, bias, step_scale, friction, lam, parts
        )
    both = pair_sum(sums)
    from_last = crossed(rounded(both[blocks:]), ahead_of)
    total = tree([part.astype(jnp.float32) for part in over_pairs(both[:blocks] + from_last)])
    velocity = vel_free + inv_mass * total
    return (lam, velocity)


def solution(mesh):
    placed = (
        P(("contact", "body"), None, None, None),
        P(("contact", "body"), None),
        P(("contact", "body")),
        P("body", None),
        P("body", None),
        P(("contact", "body"), None),
        P(("contact", "body"), None),
        P(("contact", "body"), None),
        P(("contact", "body"), None),
    )
    return jax.shard_map(
        per_device,
        mesh=mesh,
        in_specs=placed,
        out_specs=(P(("contact", "body"), None), P("body", None)),
        check_vma=False,
    )
```

```python
import functools

import jax
import jax.numpy as jnp
from jax import lax
from jax.experimental import pallas as pl
from jax.experimental.pallas import tpu as pltpu
from jax.sharding import PartitionSpec as P

ITERS = 2


def shifted(value, axis, steps):
    count = lax.axis_size(axis)
    pairs = [(source, (source + steps) % count) for source in range(count)]
    return lax.ppermute(value, axis, pairs)


def crossed(value, target):
    count, groups = lax.axis_size("body"), lax.axis_size("contact")
    cross = 1 if groups % 2 == 0 else 0
    pairs = [
        (group * count + place, (group ^ cross) * count + target(place) % count)
        for group in range(groups)
        for place in range(count)
    ]
    return lax.ppermute(value, ("contact", "body"), pairs)


def ahead_of(place):
    return place + 1


def traded(ahead, back, even):
    if lax.axis_size("body") % 2:
        return crossed(ahead, ahead_of), crossed(back, lambda place: place - 1)
    far, close = lax.optimization_barrier(
        (jnp.where(even, back, ahead), jnp.where(even, ahead, back))
    )
    wide = crossed(far, lambda place: place + 2 * (place % 2) - 1)
    near = crossed(close, lambda place: place ^ 1)
    return jnp.where(even, wide, near), jnp.where(even, near, wide)


def rounded(value):
    return value.astype(jnp.bfloat16)


def tree(values):
    while len(values) > 1:
        values = [left + right for left, right in zip(values[::2], values[1::2])]
    return values[0]


def pair_sum(value):
    count = lax.axis_size("contact")
    if count % 2:
        return value
    return value + lax.ppermute(value, "contact", [(place, place ^ 1) for place in range(count)])


def pair_count():
    count = lax.axis_size("contact")
    return count if count % 2 else count // 2


def over_pairs(value):
    count = lax.axis_size("contact")
    if count & (count - 1):
        mine = (lax.axis_index("contact") & 1) == 0
        return [lax.psum(value if count % 2 else jnp.where(mine, value, 0.0), "contact")]
    stride, parts = 2, [value]
    while stride < count:
        radix = min(count // stride, 4)
        value = rounded(tree([part.astype(jnp.float32) for part in parts]))
        parts = []
        for digit in range(1, radix):
            pairs = [(place, place ^ (digit * stride) ^ 1) for place in range(count)]
            parts.append(lax.ppermute(value, "contact", pairs))
        parts.append(value)
        stride *= radix
    return parts


def project(trial, friction, contacts):
    normal = trial[:, :contacts]
    first = trial[:, contacts : 2 * contacts]
    second = trial[:, 2 * contacts :]
    tangent = jnp.sqrt(first * first + second * second)
    inside = tangent <= friction * normal
    below = friction * tangent <= -normal
    moved = (normal + friction * tangent) / (1.0 + friction * friction)
    safe = jnp.where(inside | below, 1.0, tangent)
    factor = jnp.where(inside, 1.0, jnp.where(below, 0.0, friction * moved / safe))
    new_normal = jnp.where(inside, normal, jnp.where(below, 0.0, moved))
    return jnp.concatenate([new_normal, first * factor, second * factor], axis=1)


WIDE = 256


def paired(first, second):
    wide = (8, first.shape[1])
    return jnp.concatenate([jnp.broadcast_to(first, wide), jnp.broadcast_to(second, wide)])


def product(left, right):
    return jnp.dot(left, right, preferred_element_type=jnp.float32)


def push_pair(tile, lam_ref, turned_ref, block_ref, sums_ref):
    blocks, dofs = sums_ref.shape[0] // 2, sums_ref.shape[1]
    main = lam_ref.shape[1] // WIDE * WIDE
    row, other = (lam_ref[pl.ds(place, 1), :] for place in (tile, tile + 1))
    whole = paired(row[:, :main], other[:, :main]).astype(jnp.bfloat16)
    nothing = jnp.zeros_like(row[:, main:])
    rest = paired(
        jnp.concatenate([row[:, main:], nothing], axis=1),
        jnp.concatenate([nothing, other[:, main:]], axis=1),
    ).astype(jnp.bfloat16)
    ends = jnp.concatenate([turned_ref[tile, main:], turned_ref[tile + 1, main:]])
    shared = product(rest, ends)
    for place, line in ((tile, 0), (tile + 1, 8)):
        push = product(whole, turned_ref[place, :main]) + shared
        push = push[line : line + 1]
        sums_ref[pl.ds(block_ref[0, place], 1), :] += push[:, :dofs]
        sums_ref[pl.ds(blocks + block_ref[1, place], 1), :] += push[:, dofs:]


def rel_pair(tile, vel_ref, jac_ref, block_ref, rel_ref):
    blocks = vel_ref.shape[0] // 2
    main = jac_ref.shape[2] // WIDE * WIDE
    rows = [
        jnp.concatenate(
            [
                vel_ref[pl.ds(block_ref[0, place], 1), :],
                vel_ref[pl.ds(blocks + block_ref[1, place], 1), :],
            ],
            axis=1,
        )
        for place in (tile, tile + 1)
    ]
    left = paired(*rows).astype(jnp.bfloat16)
    ends = jnp.concatenate([jac_ref[tile, :, main:], jac_ref[tile + 1, :, main:]], axis=1)
    shared = product(left, ends)
    rest = jac_ref.shape[2] - main
    for place, line in ((tile, 0), (tile + 1, 8)):
        whole = product(left, jac_ref[place, :, :main])
        rel_ref[pl.ds(place, 1), :main] = whole[line : line + 1]
        start = rest * (place - tile)
        rel_ref[pl.ds(place, 1), main:] = shared[line : line + 1, start : start + rest]


def first_kernel(
    count_ref, block_ref, jac_ref, start_ref, kept_ref, turned_ref, live_ref, lam_ref, sums_ref,
    block, sems, small_sems,
):
    tiles = start_ref.shape[0]
    small = [
        pltpu.make_async_copy(source, target, small_sems.at[place])
        for place, (source, target) in enumerate(
            [(block_ref, block), (start_ref, lam_ref)]
        )
    ]
    copies = [
        pltpu.make_async_copy(jac_ref.at[tile], kept_ref.at[tile], sems.at[tile])
        for tile in range(tiles)
    ]
    cuts = sorted({*range(0, tiles, GROUP), max(tiles - GROUP // 2, 0), tiles})
    started = 2 * GROUP
    for copy in small + copies[:started]:
        copy.start()
    sums_ref[...] = jnp.zeros_like(sums_ref)
    for copy in small:
        copy.wait()
    order = lax.broadcasted_iota(jnp.int32, lam_ref.shape, 0)
    live_ref[...] = jnp.where(order < count_ref[0], 1.0, 0.0)
    lam_ref[...] = lam_ref[...] * live_ref[...]
    for group in [range(first, after) for first, after in zip(cuts, cuts[1:])]:
        for tile in group:
            copies[tile].wait()
        for copy in copies[started : group[-1] + 1 + 2 * GROUP]:
            copy.start()
        started = max(started, group[-1] + 1 + 2 * GROUP)
        for tile in group:
            turned_ref[tile] = kept_ref[tile].T
        for tile in group[::2]:
            push_pair(tile, lam_ref, turned_ref, block, sums_ref)


def sweep_kernel(
    parts, block_ref, live_ref, jac_ref, turned_ref, bias_ref, step_ref, friction_ref, old_ref, *refs
):
    part_refs, (out_ref, sums_ref, vel_ref, rel_ref, lam_ref, sem) = refs[:parts], refs[parts:]
    tiles = old_ref.shape[0]
    vel_ref[...] = tree([ref[...].astype(jnp.float32) for ref in part_refs])
    sums_ref[...] = jnp.zeros_like(sums_ref)
    for tile in range(0, tiles, 2):
        rel_pair(tile, vel_ref, jac_ref, block_ref, rel_ref)
    trial = old_ref[...] - step_ref[...] * (rel_ref[...] + bias_ref[...])
    lam = project(trial, friction_ref[...], friction_ref.shape[1])
    lam_ref[...] = lam * live_ref[...]
    copy = pltpu.make_async_copy(lam_ref, out_ref, sem)
    copy.start()
    for tile in range(0, tiles, 2):
        push_pair(tile, lam_ref, turned_ref, block_ref, sums_ref)
    copy.wait()


GROUP = 4
LIMIT = 24 * 1024 * 1024
SMEM = pl.BlockSpec(memory_space=pltpu.SMEM)
VMEM = pl.BlockSpec(memory_space=pltpu.VMEM)


def result_shapes(lam, blocks, dofs):
    return [
        jax.ShapeDtypeStruct(lam.shape, jnp.float32),
        jax.ShapeDtypeStruct((2 * blocks, dofs), jnp.float32),
    ]


def first_push(jacobian, tile_block, tile_count, start, blocks):
    tiles, rows, cols = jacobian.shape
    lam_shape, sums_shape = result_shapes(start, blocks, rows // 2)
    held = [
        pltpu.with_memory_space_constraint(array, pltpu.HBM)
        for array in (tile_block, jacobian, start)
    ]
    return pl.pallas_call(
        first_kernel,
        out_shape=[
            pltpu.VMEM((tiles, rows, cols), jacobian.dtype),
            pltpu.VMEM((tiles, cols, rows), jacobian.dtype),
            lam_shape, lam_shape, sums_shape,
        ],
        in_specs=[SMEM] + [pl.BlockSpec(memory_space=pltpu.HBM)] * 3,
        out_specs=[VMEM] * 5,
        scratch_shapes=[
            pltpu.SMEM(tile_block.shape, jnp.int32),
            pltpu.SemaphoreType.DMA((tiles,)),
            pltpu.SemaphoreType.DMA((2,)),
        ],
        compiler_params=pltpu.CompilerParams(vmem_limit_bytes=LIMIT),
        cost_estimate=pl.CostEstimate(
            flops=2 * jacobian.size, bytes_accessed=2 * jacobian.size, transcendentals=0
        ),
        name="first_push",
    )(tile_count, *held)


def sweep_step(kept, turned, tile_block, live, bias, step, friction, lam, parts):
    rows, dofs = parts[0].shape
    kept = pltpu.with_memory_space_constraint(kept, pltpu.VMEM)
    turned = pltpu.with_memory_space_constraint(turned, pltpu.VMEM)
    return pl.pallas_call(
        functools.partial(sweep_kernel, len(parts)),
        out_shape=result_shapes(lam, rows // 2, dofs),
        in_specs=[SMEM] + [VMEM] * (7 + len(parts)),
        out_specs=[pl.BlockSpec(memory_space=pl.ANY), VMEM],
        scratch_shapes=[
            pltpu.VMEM((rows, dofs), jnp.float32),
            pltpu.VMEM(lam.shape, jnp.float32),
            pltpu.VMEM(lam.shape, jnp.float32),
            pltpu.SemaphoreType.DMA,
        ],
        compiler_params=pltpu.CompilerParams(vmem_limit_bytes=LIMIT),
        cost_estimate=pl.CostEstimate(
            flops=4 * kept.size, bytes_accessed=4 * kept.size, transcendentals=0
        ),
        name="sweep_step",
    )(tile_block, live, kept, turned, bias, step, friction, lam, *parts)


def per_device(
    jacobian, tile_block, tile_count, vel_free, inv_mass, bias, step_scale, friction, impulse_start
):
    tiles, sides, dofs, rows = jacobian.shape
    blocks = vel_free.shape[0]
    flat = jacobian.reshape(tiles, sides * dofs, rows)
    even = (lax.axis_index("body") & 1) == 0
    even, tile_block = lax.optimization_barrier((even, tile_block.T))
    mass_next = shifted(inv_mass, "body", -1)
    kept, turned, live, lam, sums = first_push(
        flat, tile_block, tile_count, impulse_start, blocks
    )
    mass_next, sums = lax.optimization_barrier((mass_next, sums))
    share = vel_free * (1.0 / pair_count())
    for sweep in range(ITERS):
        both = pair_sum(sums)
        own, later = both[:blocks], both[blocks:]
        from_last, from_next = traded(rounded(later), rounded(share + inv_mass * own), even)
        parts = over_pairs(
            jnp.concatenate(
                [share + inv_mass * (own + from_last), from_next + mass_next * later]
            )
        )
        lam, sums = sweep_step(
            kept, turned, tile_block, live, bias, step_scale, friction, lam, parts
        )
    both = pair_sum(sums)
    from_last = crossed(rounded(both[blocks:]), ahead_of)
    total = tree([part.astype(jnp.float32) for part in over_pairs(both[:blocks] + from_last)])
    velocity = vel_free + inv_mass * total
    return (lam, velocity)


def solution(mesh):
    placed = (
        P(("contact", "body"), None, None, None),
        P(("contact", "body"), None),
        P(("contact", "body")),
        P("body", None),
        P("body", None),
        P(("contact", "body"), None),
        P(("contact", "body"), None),
        P(("contact", "body"), None),
        P(("contact", "body"), None),
    )
    return jax.shard_map(
        per_device,
        mesh=mesh,
        in_specs=placed,
        out_specs=(P(("contact", "body"), None), P("body", None)),
        check_vma=False,
    )
```

```python
import functools

import jax
import jax.numpy as jnp
from jax import lax
from jax.experimental import pallas as pl
from jax.experimental.pallas import tpu as pltpu
from jax.sharding import PartitionSpec as P

ITERS = 2


def shifted(value, axis, steps):
    count = lax.axis_size(axis)
    pairs = [(source, (source + steps) % count) for source in range(count)]
    return lax.ppermute(value, axis, pairs)


def crossed(value, target):
    count, groups = lax.axis_size("body"), lax.axis_size("contact")
    cross = 1 if groups % 2 == 0 else 0
    pairs = [
        (group * count + place, (group ^ cross) * count + target(place) % count)
        for group in range(groups)
        for place in range(count)
    ]
    return lax.ppermute(value, ("contact", "body"), pairs)


def ahead_of(place):
    return place + 1


def traded(ahead, back, even):
    if lax.axis_size("body") % 2:
        return crossed(ahead, ahead_of), crossed(back, lambda place: place - 1)
    far, close = lax.optimization_barrier(
        (jnp.where(even, back, ahead), jnp.where(even, ahead, back))
    )
    wide = crossed(far, lambda place: place + 2 * (place % 2) - 1)
    near = crossed(close, lambda place: place ^ 1)
    return jnp.where(even, wide, near), jnp.where(even, near, wide)


def rounded(value):
    return value.astype(jnp.bfloat16)


def tree(values):
    while len(values) > 1:
        values = [left + right for left, right in zip(values[::2], values[1::2])]
    return values[0]


def pair_sum(value):
    count = lax.axis_size("contact")
    if count % 2:
        return value
    return value + lax.ppermute(value, "contact", [(place, place ^ 1) for place in range(count)])


def pair_count():
    count = lax.axis_size("contact")
    return count if count % 2 else count // 2


def over_pairs(value):
    count = lax.axis_size("contact")
    if count & (count - 1):
        mine = (lax.axis_index("contact") & 1) == 0
        return [lax.psum(value if count % 2 else jnp.where(mine, value, 0.0), "contact")]
    stride, parts = 2, [value]
    while stride < count:
        radix = min(count // stride, 4)
        value = rounded(tree([part.astype(jnp.float32) for part in parts]))
        parts = []
        for digit in range(1, radix):
            pairs = [(place, place ^ (digit * stride) ^ 1) for place in range(count)]
            parts.append(lax.ppermute(value, "contact", pairs))
        parts.append(value)
        stride *= radix
    return parts


def project(trial, friction, contacts):
    normal = trial[:, :contacts]
    first = trial[:, contacts : 2 * contacts]
    second = trial[:, 2 * contacts :]
    tangent = jnp.sqrt(first * first + second * second)
    inside = tangent <= friction * normal
    below = friction * tangent <= -normal
    moved = (normal + friction * tangent) / (1.0 + friction * friction)
    safe = jnp.where(inside | below, 1.0, tangent)
    factor = jnp.where(inside, 1.0, jnp.where(below, 0.0, friction * moved / safe))
    new_normal = jnp.where(inside, normal, jnp.where(below, 0.0, moved))
    return jnp.concatenate([new_normal, first * factor, second * factor], axis=1)


def beside(rows, blocks):
    each = 16 // len(rows)
    left = jnp.concatenate([jnp.broadcast_to(row, (each, row.shape[1])) for row in rows])
    out = jnp.dot(
        left.astype(jnp.bfloat16),
        jnp.concatenate(blocks, axis=1),
        preferred_element_type=jnp.float32,
    )
    width = blocks[0].shape[1]
    return [
        out[place * each : place * each + 1, place * width : (place + 1) * width]
        for place in range(len(rows))
    ]


def push_tiles(group, lam_ref, turned_ref, block_ref, sums_ref):
    blocks, dofs = sums_ref.shape[0] // 2, sums_ref.shape[1]
    pushes = beside(
        [lam_ref[pl.ds(tile, 1), :] for tile in group], [turned_ref[tile] for tile in group]
    )
    for tile, push in zip(group, pushes):
        sums_ref[pl.ds(block_ref[0, tile], 1), :] += push[:, :dofs]
        sums_ref[pl.ds(blocks + block_ref[1, tile], 1), :] += push[:, dofs:]


def rel_tiles(group, vel_ref, jac_ref, block_ref, rel_ref):
    blocks = vel_ref.shape[0] // 2
    rows = [
        jnp.concatenate(
            [
                vel_ref[pl.ds(block_ref[0, tile], 1), :],
                vel_ref[pl.ds(blocks + block_ref[1, tile], 1), :],
            ],
            axis=1,
        )
        for tile in group
    ]
    for tile, rel in zip(group, beside(rows, [jac_ref[tile] for tile in group])):
        rel_ref[pl.ds(tile, 1), :] = rel


def grouped(tiles, size):
    return [tiles[first : first + size] for first in range(0, len(tiles), size)]


def first_kernel(
    count_ref, block_ref, jac_ref, start_ref, kept_ref, turned_ref, live_ref, lam_ref, sums_ref,
    block, sems, small_sems,
):
    tiles = start_ref.shape[0]
    small = [
        pltpu.make_async_copy(source, target, small_sems.at[place])
        for place, (source, target) in enumerate(
            [(block_ref, block), (start_ref, lam_ref)]
        )
    ]
    copies = [
        pltpu.make_async_copy(jac_ref.at[tile], kept_ref.at[tile], sems.at[tile])
        for tile in range(tiles)
    ]
    cuts = sorted({*range(0, tiles, GROUP), max(tiles - GROUP // 2, 0), tiles})
    started = 2 * GROUP
    for copy in small + copies[:started]:
        copy.start()
    sums_ref[...] = jnp.zeros_like(sums_ref)
    for copy in small:
        copy.wait()
    order = lax.broadcasted_iota(jnp.int32, lam_ref.shape, 0)
    live_ref[...] = jnp.where(order < count_ref[0], 1.0, 0.0)
    lam_ref[...] = lam_ref[...] * live_ref[...]
    for group in [range(first, after) for first, after in zip(cuts, cuts[1:])]:
        for tile in group:
            copies[tile].wait()
        for copy in copies[started : group[-1] + 1 + 2 * GROUP]:
            copy.start()
        started = max(started, group[-1] + 1 + 2 * GROUP)
        for tile in group:
            turned_ref[tile] = kept_ref[tile].T
        for few in grouped(group, 2):
            push_tiles(few, lam_ref, turned_ref, block, sums_ref)


def sweep_kernel(
    parts, block_ref, live_ref, jac_ref, turned_ref, bias_ref, step_ref, friction_ref, old_ref, *refs
):
    part_refs, (out_ref, sums_ref, vel_ref, rel_ref, lam_ref, sem) = refs[:parts], refs[parts:]
    tiles = old_ref.shape[0]
    vel_ref[...] = tree([ref[...].astype(jnp.float32) for ref in part_refs])
    sums_ref[...] = jnp.zeros_like(sums_ref)
    for few in grouped(range(tiles), 4):
        rel_tiles(few, vel_ref, jac_ref, block_ref, rel_ref)
    trial = old_ref[...] - step_ref[...] * (rel_ref[...] + bias_ref[...])
    lam = project(trial, friction_ref[...], friction_ref.shape[1])
    lam_ref[...] = lam * live_ref[...]
    copy = pltpu.make_async_copy(lam_ref, out_ref, sem)
    copy.start()
    for few in grouped(range(tiles), 2):
        push_tiles(few, lam_ref, turned_ref, block_ref, sums_ref)
    copy.wait()


GROUP = 4
LIMIT = 24 * 1024 * 1024
SMEM = pl.BlockSpec(memory_space=pltpu.SMEM)
VMEM = pl.BlockSpec(memory_space=pltpu.VMEM)


def result_shapes(lam, blocks, dofs):
    return [
        jax.ShapeDtypeStruct(lam.shape, jnp.float32),
        jax.ShapeDtypeStruct((2 * blocks, dofs), jnp.float32),
    ]


def first_push(jacobian, tile_block, tile_count, start, blocks):
    tiles, rows, cols = jacobian.shape
    lam_shape, sums_shape = result_shapes(start, blocks, rows // 2)
    held = [
        pltpu.with_memory_space_constraint(array, pltpu.HBM)
        for array in (tile_block, jacobian, start)
    ]
    return pl.pallas_call(
        first_kernel,
        out_shape=[
            pltpu.VMEM((tiles, rows, cols), jacobian.dtype),
            pltpu.VMEM((tiles, cols, rows), jacobian.dtype),
            lam_shape, lam_shape, sums_shape,
        ],
        in_specs=[SMEM] + [pl.BlockSpec(memory_space=pltpu.HBM)] * 3,
        out_specs=[VMEM] * 5,
        scratch_shapes=[
            pltpu.SMEM(tile_block.shape, jnp.int32),
            pltpu.SemaphoreType.DMA((tiles,)),
            pltpu.SemaphoreType.DMA((2,)),
        ],
        compiler_params=pltpu.CompilerParams(vmem_limit_bytes=LIMIT),
        cost_estimate=pl.CostEstimate(
            flops=2 * jacobian.size, bytes_accessed=2 * jacobian.size, transcendentals=0
        ),
        name="first_push",
    )(tile_count, *held)


def sweep_step(kept, turned, tile_block, live, bias, step, friction, lam, parts):
    rows, dofs = parts[0].shape
    kept = pltpu.with_memory_space_constraint(kept, pltpu.VMEM)
    turned = pltpu.with_memory_space_constraint(turned, pltpu.VMEM)
    return pl.pallas_call(
        functools.partial(sweep_kernel, len(parts)),
        out_shape=result_shapes(lam, rows // 2, dofs),
        in_specs=[SMEM] + [VMEM] * (7 + len(parts)),
        out_specs=[pl.BlockSpec(memory_space=pl.ANY), VMEM],
        scratch_shapes=[
            pltpu.VMEM((rows, dofs), jnp.float32),
            pltpu.VMEM(lam.shape, jnp.float32),
            pltpu.VMEM(lam.shape, jnp.float32),
            pltpu.SemaphoreType.DMA,
        ],
        compiler_params=pltpu.CompilerParams(vmem_limit_bytes=LIMIT),
        cost_estimate=pl.CostEstimate(
            flops=4 * kept.size, bytes_accessed=4 * kept.size, transcendentals=0
        ),
        name="sweep_step",
    )(tile_block, live, kept, turned, bias, step, friction, lam, *parts)


def per_device(
    jacobian, tile_block, tile_count, vel_free, inv_mass, bias, step_scale, friction, impulse_start
):
    tiles, sides, dofs, rows = jacobian.shape
    blocks = vel_free.shape[0]
    flat = jacobian.reshape(tiles, sides * dofs, rows)
    even = (lax.axis_index("body") & 1) == 0
    even, tile_block = lax.optimization_barrier((even, tile_block.T))
    mass_next = shifted(inv_mass, "body", -1)
    kept, turned, live, lam, sums = first_push(
        flat, tile_block, tile_count, impulse_start, blocks
    )
    mass_next, sums = lax.optimization_barrier((mass_next, sums))
    share = vel_free * (1.0 / pair_count())
    for sweep in range(ITERS):
        both = pair_sum(sums)
        own, later = both[:blocks], both[blocks:]
        from_last, from_next = traded(rounded(later), rounded(share + inv_mass * own), even)
        parts = over_pairs(
            jnp.concatenate(
                [share + inv_mass * (own + from_last), from_next + mass_next * later]
            )
        )
        lam, sums = sweep_step(
            kept, turned, tile_block, live, bias, step_scale, friction, lam, parts
        )
    both = pair_sum(sums)
    from_last = crossed(rounded(both[blocks:]), ahead_of)
    total = tree([part.astype(jnp.float32) for part in over_pairs(both[:blocks] + from_last)])
    velocity = vel_free + inv_mass * total
    return (lam, velocity)


def solution(mesh):
    placed = (
        P(("contact", "body"), None, None, None),
        P(("contact", "body"), None),
        P(("contact", "body")),
        P("body", None),
        P("body", None),
        P(("contact", "body"), None),
        P(("contact", "body"), None),
        P(("contact", "body"), None),
        P(("contact", "body"), None),
    )
    return jax.shard_map(
        per_device,
        mesh=mesh,
        in_specs=placed,
        out_specs=(P(("contact", "body"), None), P("body", None)),
        check_vma=False,
    )
```

```python
import functools

import jax
import jax.numpy as jnp
from jax import lax
from jax.experimental import pallas as pl
from jax.experimental.pallas import tpu as pltpu
from jax.sharding import PartitionSpec as P

ITERS = 2


def crossed(value, target):
    count, groups = lax.axis_size("body"), lax.axis_size("contact")
    cross = 1 if groups % 2 == 0 else 0
    pairs = [
        (group * count + place, (group ^ cross) * count + target(place) % count)
        for group in range(groups)
        for place in range(count)
    ]
    return lax.ppermute(value, ("contact", "body"), pairs)


def ahead_of(place):
    return place + 1


def traded(ahead, back, even, *extra):
    both = lambda value: jnp.concatenate([value, *extra]) if extra else value
    if lax.axis_size("body") % 2:
        return crossed(ahead, ahead_of), crossed(both(back), lambda place: place - 1)
    far, close = lax.optimization_barrier(
        (both(jnp.where(even, back, ahead)), both(jnp.where(even, ahead, back)))
    )
    wide = crossed(far, lambda place: place + 2 * (place % 2) - 1)
    near = crossed(close, lambda place: place ^ 1)
    rows = ahead.shape[0]
    return jnp.where(even, wide[:rows], near[:rows]), jnp.where(even, near, wide)


def rounded(value):
    return value.astype(jnp.bfloat16)


def tree(values):
    while len(values) > 1:
        values = [left + right for left, right in zip(values[::2], values[1::2])]
    return values[0]


def pair_sum(value):
    count = lax.axis_size("contact")
    if count % 2:
        return value
    return value + lax.ppermute(value, "contact", [(place, place ^ 1) for place in range(count)])


def pair_count():
    count = lax.axis_size("contact")
    return count if count % 2 else count // 2


def over_pairs(value):
    count = lax.axis_size("contact")
    if count & (count - 1):
        mine = (lax.axis_index("contact") & 1) == 0
        return [lax.psum(value if count % 2 else jnp.where(mine, value, 0.0), "contact")]
    stride, parts = 2, [value]
    while stride < count:
        radix = min(count // stride, 4)
        value = rounded(tree([part.astype(jnp.float32) for part in parts]))
        parts = []
        for digit in range(1, radix):
            pairs = [(place, place ^ (digit * stride) ^ 1) for place in range(count)]
            parts.append(lax.ppermute(value, "contact", pairs))
        parts.append(value)
        stride *= radix
    return parts


def project(trial, friction, contacts):
    normal = trial[:, :contacts]
    first = trial[:, contacts : 2 * contacts]
    second = trial[:, 2 * contacts :]
    tangent = jnp.sqrt(first * first + second * second)
    inside = tangent <= friction * normal
    below = friction * tangent <= -normal
    moved = (normal + friction * tangent) / (1.0 + friction * friction)
    safe = jnp.where(inside | below, 1.0, tangent)
    factor = jnp.where(inside, 1.0, jnp.where(below, 0.0, friction * moved / safe))
    new_normal = jnp.where(inside, normal, jnp.where(below, 0.0, moved))
    return jnp.concatenate([new_normal, first * factor, second * factor], axis=1)


def push_tile(tile, lam_ref, turned_ref, block_ref, sums_ref):
    blocks, dofs = sums_ref.shape[0] // 2, sums_ref.shape[1]
    row = jnp.broadcast_to(lam_ref[pl.ds(tile, 1), :], (16, lam_ref.shape[1]))
    push = jnp.dot(
        row.astype(jnp.bfloat16), turned_ref[tile], preferred_element_type=jnp.float32
    )
    sums_ref[pl.ds(block_ref[0, tile], 1), :] += push[:1, :dofs]
    sums_ref[pl.ds(blocks + block_ref[1, tile], 1), :] += push[:1, dofs:]


def first_kernel(
    count_ref, block_ref, jac_ref, start_ref, kept_ref, turned_ref, live_ref, lam_ref, sums_ref,
    block, sems, small_sems,
):
    tiles = start_ref.shape[0]
    small = [
        pltpu.make_async_copy(source, target, small_sems.at[place])
        for place, (source, target) in enumerate(
            [(block_ref, block), (start_ref, lam_ref)]
        )
    ]
    copies = [
        pltpu.make_async_copy(jac_ref.at[tile], kept_ref.at[tile], sems.at[tile])
        for tile in range(tiles)
    ]
    cuts = sorted({*range(0, tiles, GROUP), max(tiles - GROUP // 2, 0), tiles})
    started = 2 * GROUP
    for copy in small + copies[:started]:
        copy.start()
    sums_ref[...] = jnp.zeros_like(sums_ref)
    for copy in small:
        copy.wait()
    order = lax.broadcasted_iota(jnp.int32, lam_ref.shape, 0)
    live_ref[...] = jnp.where(order < count_ref[0], 1.0, 0.0)
    lam_ref[...] = lam_ref[...] * live_ref[...]
    for group in [range(first, after) for first, after in zip(cuts, cuts[1:])]:
        for tile in group:
            copies[tile].wait()
        for copy in copies[started : group[-1] + 1 + 2 * GROUP]:
            copy.start()
        started = max(started, group[-1] + 1 + 2 * GROUP)
        for tile in group:
            turned_ref[tile] = kept_ref[tile].T
        for tile in group:
            push_tile(tile, lam_ref, turned_ref, block, sums_ref)


def sweep_kernel(
    parts, block_ref, live_ref, jac_ref, turned_ref, bias_ref, step_ref, friction_ref, old_ref, *refs
):
    part_refs, (out_ref, sums_ref, vel_ref, rel_ref, lam_ref, sem) = refs[:parts], refs[parts:]
    tiles = old_ref.shape[0]
    blocks, dofs = vel_ref.shape[0] // 2, vel_ref.shape[1]
    vel_ref[...] = tree([ref[...].astype(jnp.float32) for ref in part_refs])
    sums_ref[...] = jnp.zeros_like(sums_ref)
    for tile in range(tiles):
        own_row = vel_ref[pl.ds(block_ref[0, tile], 1), :]
        next_row = vel_ref[pl.ds(blocks + block_ref[1, tile], 1), :]
        row = jnp.broadcast_to(jnp.concatenate([own_row, next_row], axis=1), (16, 2 * dofs))
        rel = jnp.dot(row.astype(jnp.bfloat16), jac_ref[tile], preferred_element_type=jnp.float32)
        rel_ref[pl.ds(tile, 1), :] = rel[:1]
    trial = old_ref[...] - step_ref[...] * (rel_ref[...] + bias_ref[...])
    lam = project(trial, friction_ref[...], friction_ref.shape[1])
    lam_ref[...] = lam * live_ref[...]
    copy = pltpu.make_async_copy(lam_ref, out_ref, sem)
    copy.start()
    for tile in range(tiles):
        push_tile(tile, lam_ref, turned_ref, block_ref, sums_ref)
    copy.wait()


GROUP = 4
LIMIT = 24 * 1024 * 1024
SMEM = pl.BlockSpec(memory_space=pltpu.SMEM)
VMEM = pl.BlockSpec(memory_space=pltpu.VMEM)


def result_shapes(lam, blocks, dofs):
    return [
        jax.ShapeDtypeStruct(lam.shape, jnp.float32),
        jax.ShapeDtypeStruct((2 * blocks, dofs), jnp.float32),
    ]


def first_push(jacobian, tile_block, tile_count, start, blocks):
    tiles, rows, cols = jacobian.shape
    lam_shape, sums_shape = result_shapes(start, blocks, rows // 2)
    held = [
        pltpu.with_memory_space_constraint(array, pltpu.HBM)
        for array in (tile_block, jacobian, start)
    ]
    return pl.pallas_call(
        first_kernel,
        out_shape=[
            pltpu.VMEM((tiles, rows, cols), jacobian.dtype),
            pltpu.VMEM((tiles, cols, rows), jacobian.dtype),
            lam_shape, lam_shape, sums_shape,
        ],
        in_specs=[SMEM] + [pl.BlockSpec(memory_space=pltpu.HBM)] * 3,
        out_specs=[VMEM] * 5,
        scratch_shapes=[
            pltpu.SMEM(tile_block.shape, jnp.int32),
            pltpu.SemaphoreType.DMA((tiles,)),
            pltpu.SemaphoreType.DMA((2,)),
        ],
        compiler_params=pltpu.CompilerParams(vmem_limit_bytes=LIMIT),
        cost_estimate=pl.CostEstimate(
            flops=2 * jacobian.size, bytes_accessed=2 * jacobian.size, transcendentals=0
        ),
        name="first_push",
    )(tile_count, *held)


def sweep_step(kept, turned, tile_block, live, bias, step, friction, lam, parts):
    rows, dofs = parts[0].shape
    kept = pltpu.with_memory_space_constraint(kept, pltpu.VMEM)
    turned = pltpu.with_memory_space_constraint(turned, pltpu.VMEM)
    return pl.pallas_call(
        functools.partial(sweep_kernel, len(parts)),
        out_shape=result_shapes(lam, rows // 2, dofs),
        in_specs=[SMEM] + [VMEM] * (7 + len(parts)),
        out_specs=[pl.BlockSpec(memory_space=pl.ANY), VMEM],
        scratch_shapes=[
            pltpu.VMEM((rows, dofs), jnp.float32),
            pltpu.VMEM(lam.shape, jnp.float32),
            pltpu.VMEM(lam.shape, jnp.float32),
            pltpu.SemaphoreType.DMA,
        ],
        compiler_params=pltpu.CompilerParams(vmem_limit_bytes=LIMIT),
        cost_estimate=pl.CostEstimate(
            flops=4 * kept.size, bytes_accessed=4 * kept.size, transcendentals=0
        ),
        name="sweep_step",
    )(tile_block, live, kept, turned, bias, step, friction, lam, *parts)


def per_device(
    jacobian, tile_block, tile_count, vel_free, inv_mass, bias, step_scale, friction, impulse_start
):
    tiles, sides, dofs, rows = jacobian.shape
    blocks = vel_free.shape[0]
    flat = jacobian.reshape(tiles, sides * dofs, rows)
    even = (lax.axis_index("body") & 1) == 0
    even, tile_block = lax.optimization_barrier((even, tile_block.T))
    kept, turned, live, lam, sums = first_push(
        flat, tile_block, tile_count, impulse_start, blocks
    )
    share, mass_next = vel_free * (1.0 / pair_count()), None
    for sweep in range(ITERS):
        both = pair_sum(sums)
        own, later = both[:blocks], both[blocks:]
        extra = [rounded(inv_mass)] if mass_next is None else []
        from_last, from_next = traded(
            rounded(later), rounded(share + inv_mass * own), even, *extra
        )
        if mass_next is None:
            mass_next = from_next[blocks:].astype(jnp.float32)
        parts = over_pairs(
            jnp.concatenate(
                [share + inv_mass * (own + from_last), from_next[:blocks] + mass_next * later]
            )
        )
        lam, sums = sweep_step(
            kept, turned, tile_block, live, bias, step_scale, friction, lam, parts
        )
    both = pair_sum(sums)
    from_last = crossed(rounded(both[blocks:]), ahead_of)
    total = tree([part.astype(jnp.float32) for part in over_pairs(both[:blocks] + from_last)])
    velocity = vel_free + inv_mass * total
    return (lam, velocity)


def solution(mesh):
    placed = (
        P(("contact", "body"), None, None, None),
        P(("contact", "body"), None),
        P(("contact", "body")),
        P("body", None),
        P("body", None),
        P(("contact", "body"), None),
        P(("contact", "body"), None),
        P(("contact", "body"), None),
        P(("contact", "body"), None),
    )
    return jax.shard_map(
        per_device,
        mesh=mesh,
        in_specs=placed,
        out_specs=(P(("contact", "body"), None), P("body", None)),
        check_vma=False,
    )
```

```python
import functools

import jax
import jax.numpy as jnp
from jax import lax
from jax.experimental import pallas as pl
from jax.experimental.pallas import tpu as pltpu
from jax.sharding import PartitionSpec as P

ITERS = 2


def crossed(value, target):
    count, groups = lax.axis_size("body"), lax.axis_size("contact")
    cross = 1 if groups % 2 == 0 else 0
    pairs = [
        (group * count + place, (group ^ cross) * count + target(place) % count)
        for group in range(groups)
        for place in range(count)
    ]
    return lax.ppermute(value, ("contact", "body"), pairs)


def ahead_of(place):
    return place + 1


def traded(ahead, back, even, *extra):
    both = lambda value: jnp.concatenate([value, *extra]) if extra else value
    if lax.axis_size("body") % 2:
        return crossed(ahead, ahead_of), crossed(both(back), lambda place: place - 1)
    far, close = lax.optimization_barrier(
        (both(jnp.where(even, back, ahead)), both(jnp.where(even, ahead, back)))
    )
    wide = crossed(far, lambda place: place + 2 * (place % 2) - 1)
    near = crossed(close, lambda place: place ^ 1)
    rows = ahead.shape[0]
    return jnp.where(even, wide[:rows], near[:rows]), jnp.where(even, near, wide)


def rounded(value):
    return value.astype(jnp.bfloat16)


def tree(values):
    while len(values) > 1:
        values = [left + right for left, right in zip(values[::2], values[1::2])]
    return values[0]


def pair_sum(value):
    count = lax.axis_size("contact")
    if count % 2:
        return value
    return value + lax.ppermute(value, "contact", [(place, place ^ 1) for place in range(count)])


def pair_count():
    count = lax.axis_size("contact")
    return count if count % 2 else count // 2


def over_pairs(value):
    count = lax.axis_size("contact")
    if count & (count - 1):
        mine = (lax.axis_index("contact") & 1) == 0
        return [lax.psum(value if count % 2 else jnp.where(mine, value, 0.0), "contact")]
    stride, parts = 2, [value]
    while stride < count:
        radix = min(count // stride, 4)
        value = rounded(tree([part.astype(jnp.float32) for part in parts]))
        parts = []
        for digit in range(1, radix):
            pairs = [(place, place ^ (digit * stride) ^ 1) for place in range(count)]
            parts.append(lax.ppermute(value, "contact", pairs))
        parts.append(value)
        stride *= radix
    return parts


def project(trial, friction, contacts):
    normal = trial[:, :contacts]
    first = trial[:, contacts : 2 * contacts]
    second = trial[:, 2 * contacts :]
    tangent = jnp.sqrt(first * first + second * second)
    inside = tangent <= friction * normal
    below = friction * tangent <= -normal
    moved = (normal + friction * tangent) / (1.0 + friction * friction)
    safe = jnp.where(inside | below, 1.0, tangent)
    factor = jnp.where(inside, 1.0, jnp.where(below, 0.0, friction * moved / safe))
    new_normal = jnp.where(inside, normal, jnp.where(below, 0.0, moved))
    return jnp.concatenate([new_normal, first * factor, second * factor], axis=1)


def push_tile(tile, lam_ref, turned_ref, block_ref, sums_ref):
    blocks, dofs = sums_ref.shape[0] // 2, sums_ref.shape[1]
    row = jnp.broadcast_to(lam_ref[pl.ds(tile, 1), :], (16, lam_ref.shape[1]))
    push = jnp.dot(
        row.astype(jnp.bfloat16), turned_ref[tile], preferred_element_type=jnp.float32
    )
    sums_ref[pl.ds(block_ref[0, tile], 1), :] += push[:1, :dofs]
    sums_ref[pl.ds(blocks + block_ref[1, tile], 1), :] += push[:1, dofs:]


def first_kernel(
    count_ref, block_ref, jac_ref, start_ref, kept_ref, turned_ref, live_ref, lam_ref, sums_ref,
    block, sems, small_sems,
):
    tiles = start_ref.shape[0]
    small = [
        pltpu.make_async_copy(source, target, small_sems.at[place])
        for place, (source, target) in enumerate(
            [(block_ref, block), (start_ref, lam_ref)]
        )
    ]
    copies = [
        pltpu.make_async_copy(jac_ref.at[tile], kept_ref.at[tile], sems.at[tile])
        for tile in range(tiles)
    ]
    groups = [range(first, min(first + GROUP, tiles)) for first in range(0, tiles, GROUP)]
    started = 2 * GROUP
    for copy in small + copies[:started]:
        copy.start()
    sums_ref[...] = jnp.zeros_like(sums_ref)
    for copy in small:
        copy.wait()
    order = lax.broadcasted_iota(jnp.int32, lam_ref.shape, 0)
    live_ref[...] = jnp.where(order < count_ref[0], 1.0, 0.0)
    lam_ref[...] = lam_ref[...] * live_ref[...]
    for group, before in zip(groups + [[]], [[]] + groups):
        for tile in group:
            copies[tile].wait()
        for copy in copies[started : started + len(group)]:
            copy.start()
        started += len(group)
        for tile in group:
            turned_ref[tile] = kept_ref[tile].T
        for tile in before:
            push_tile(tile, lam_ref, turned_ref, block, sums_ref)


def sweep_kernel(
    parts, block_ref, live_ref, jac_ref, turned_ref, bias_ref, step_ref, friction_ref, old_ref, *refs
):
    part_refs, (out_ref, sums_ref, vel_ref, rel_ref, lam_ref, sem) = refs[:parts], refs[parts:]
    tiles = old_ref.shape[0]
    blocks, dofs = vel_ref.shape[0] // 2, vel_ref.shape[1]
    vel_ref[...] = tree([ref[...].astype(jnp.float32) for ref in part_refs])
    sums_ref[...] = jnp.zeros_like(sums_ref)
    for tile in range(tiles):
        own_row = vel_ref[pl.ds(block_ref[0, tile], 1), :]
        next_row = vel_ref[pl.ds(blocks + block_ref[1, tile], 1), :]
        row = jnp.broadcast_to(jnp.concatenate([own_row, next_row], axis=1), (16, 2 * dofs))
        rel = jnp.dot(row.astype(jnp.bfloat16), jac_ref[tile], preferred_element_type=jnp.float32)
        rel_ref[pl.ds(tile, 1), :] = rel[:1]
    trial = old_ref[...] - step_ref[...] * (rel_ref[...] + bias_ref[...])
    lam = project(trial, friction_ref[...], friction_ref.shape[1])
    lam_ref[...] = lam * live_ref[...]
    copy = pltpu.make_async_copy(lam_ref, out_ref, sem)
    copy.start()
    for tile in range(tiles):
        push_tile(tile, lam_ref, turned_ref, block_ref, sums_ref)
    copy.wait()


GROUP = 4
LIMIT = 24 * 1024 * 1024
SMEM = pl.BlockSpec(memory_space=pltpu.SMEM)
VMEM = pl.BlockSpec(memory_space=pltpu.VMEM)


def result_shapes(lam, blocks, dofs):
    return [
        jax.ShapeDtypeStruct(lam.shape, jnp.float32),
        jax.ShapeDtypeStruct((2 * blocks, dofs), jnp.float32),
    ]


def first_push(jacobian, tile_block, tile_count, start, blocks):
    tiles, rows, cols = jacobian.shape
    lam_shape, sums_shape = result_shapes(start, blocks, rows // 2)
    held = [
        pltpu.with_memory_space_constraint(array, pltpu.HBM)
        for array in (tile_block, jacobian, start)
    ]
    return pl.pallas_call(
        first_kernel,
        out_shape=[
            pltpu.VMEM((tiles, rows, cols), jacobian.dtype),
            pltpu.VMEM((tiles, cols, rows), jacobian.dtype),
            lam_shape, lam_shape, sums_shape,
        ],
        in_specs=[SMEM] + [pl.BlockSpec(memory_space=pltpu.HBM)] * 3,
        out_specs=[VMEM] * 5,
        scratch_shapes=[
            pltpu.SMEM(tile_block.shape, jnp.int32),
            pltpu.SemaphoreType.DMA((tiles,)),
            pltpu.SemaphoreType.DMA((2,)),
        ],
        compiler_params=pltpu.CompilerParams(vmem_limit_bytes=LIMIT),
        cost_estimate=pl.CostEstimate(
            flops=2 * jacobian.size, bytes_accessed=2 * jacobian.size, transcendentals=0
        ),
        name="first_push",
    )(tile_count, *held)


def sweep_step(kept, turned, tile_block, live, bias, step, friction, lam, parts):
    rows, dofs = parts[0].shape
    kept = pltpu.with_memory_space_constraint(kept, pltpu.VMEM)
    turned = pltpu.with_memory_space_constraint(turned, pltpu.VMEM)
    return pl.pallas_call(
        functools.partial(sweep_kernel, len(parts)),
        out_shape=result_shapes(lam, rows // 2, dofs),
        in_specs=[SMEM] + [VMEM] * (7 + len(parts)),
        out_specs=[pl.BlockSpec(memory_space=pl.ANY), VMEM],
        scratch_shapes=[
            pltpu.VMEM((rows, dofs), jnp.float32),
            pltpu.VMEM(lam.shape, jnp.float32),
            pltpu.VMEM(lam.shape, jnp.float32),
            pltpu.SemaphoreType.DMA,
        ],
        compiler_params=pltpu.CompilerParams(vmem_limit_bytes=LIMIT),
        cost_estimate=pl.CostEstimate(
            flops=4 * kept.size, bytes_accessed=4 * kept.size, transcendentals=0
        ),
        name="sweep_step",
    )(tile_block, live, kept, turned, bias, step, friction, lam, *parts)


def per_device(
    jacobian, tile_block, tile_count, vel_free, inv_mass, bias, step_scale, friction, impulse_start
):
    tiles, sides, dofs, rows = jacobian.shape
    blocks = vel_free.shape[0]
    flat = jacobian.reshape(tiles, sides * dofs, rows)
    even = (lax.axis_index("body") & 1) == 0
    even, tile_block = lax.optimization_barrier((even, tile_block.T))
    kept, turned, live, lam, sums = first_push(
        flat, tile_block, tile_count, impulse_start, blocks
    )
    share, mass_next = vel_free * (1.0 / pair_count()), None
    for sweep in range(ITERS):
        both = pair_sum(sums)
        own, later = both[:blocks], both[blocks:]
        extra = [rounded(inv_mass)] if mass_next is None else []
        from_last, from_next = traded(
            rounded(later), rounded(share + inv_mass * own), even, *extra
        )
        if mass_next is None:
            mass_next = from_next[blocks:].astype(jnp.float32)
        parts = over_pairs(
            jnp.concatenate(
                [share + inv_mass * (own + from_last), from_next[:blocks] + mass_next * later]
            )
        )
        lam, sums = sweep_step(
            kept, turned, tile_block, live, bias, step_scale, friction, lam, parts
        )
    both = pair_sum(sums)
    from_last = crossed(rounded(both[blocks:]), ahead_of)
    total = tree([part.astype(jnp.float32) for part in over_pairs(both[:blocks] + from_last)])
    velocity = vel_free + inv_mass * total
    return (lam, velocity)


def solution(mesh):
    placed = (
        P(("contact", "body"), None, None, None),
        P(("contact", "body"), None),
        P(("contact", "body")),
        P("body", None),
        P("body", None),
        P(("contact", "body"), None),
        P(("contact", "body"), None),
        P(("contact", "body"), None),
        P(("contact", "body"), None),
    )
    return jax.shard_map(
        per_device,
        mesh=mesh,
        in_specs=placed,
        out_specs=(P(("contact", "body"), None), P("body", None)),
        check_vma=False,
    )
```

```python
import functools

import jax
import jax.numpy as jnp
from jax import lax
from jax.experimental import pallas as pl
from jax.experimental.pallas import tpu as pltpu
from jax.sharding import PartitionSpec as P

ITERS = 2


def crossed(value, target):
    count, groups = lax.axis_size("body"), lax.axis_size("contact")
    cross = 1 if groups % 2 == 0 else 0
    pairs = [
        (group * count + place, (group ^ cross) * count + target(place) % count)
        for group in range(groups)
        for place in range(count)
    ]
    return lax.ppermute(value, ("contact", "body"), pairs)


def ahead_of(place):
    return place + 1


def traded(ahead, back, even, *extra):
    both = lambda value: jnp.concatenate([value, *extra]) if extra else value
    if lax.axis_size("body") % 2:
        return crossed(ahead, ahead_of), crossed(both(back), lambda place: place - 1)
    far, close = lax.optimization_barrier(
        (both(jnp.where(even, back, ahead)), both(jnp.where(even, ahead, back)))
    )
    wide = crossed(far, lambda place: place + 2 * (place % 2) - 1)
    near = crossed(close, lambda place: place ^ 1)
    rows = ahead.shape[0]
    return jnp.where(even, wide[:rows], near[:rows]), jnp.where(even, near, wide)


def rounded(value):
    return value.astype(jnp.bfloat16)


def tree(values):
    while len(values) > 1:
        values = [left + right for left, right in zip(values[::2], values[1::2])]
    return values[0]


def pair_sum(value):
    count = lax.axis_size("contact")
    if count % 2:
        return value
    return value + lax.ppermute(value, "contact", [(place, place ^ 1) for place in range(count)])


def pair_count():
    count = lax.axis_size("contact")
    return count if count % 2 else count // 2


def over_pairs(value):
    count = lax.axis_size("contact")
    if count & (count - 1):
        mine = (lax.axis_index("contact") & 1) == 0
        return [lax.psum(value if count % 2 else jnp.where(mine, value, 0.0), "contact")]
    stride, parts = 2, [value]
    while stride < count:
        radix = min(count // stride, 4)
        value = rounded(tree([part.astype(jnp.float32) for part in parts]))
        parts = []
        for digit in range(1, radix):
            pairs = [(place, place ^ (digit * stride) ^ 1) for place in range(count)]
            parts.append(lax.ppermute(value, "contact", pairs))
        parts.append(value)
        stride *= radix
    return parts


def project(trial, friction, contacts):
    normal = trial[:, :contacts]
    first = trial[:, contacts : 2 * contacts]
    second = trial[:, 2 * contacts :]
    tangent = jnp.sqrt(first * first + second * second)
    inside = tangent <= friction * normal
    below = friction * tangent <= -normal
    moved = (normal + friction * tangent) / (1.0 + friction * friction)
    safe = jnp.where(inside | below, 1.0, tangent)
    factor = jnp.where(inside, 1.0, jnp.where(below, 0.0, friction * moved / safe))
    new_normal = jnp.where(inside, normal, jnp.where(below, 0.0, moved))
    return jnp.concatenate([new_normal, first * factor, second * factor], axis=1)


def push_tile(tile, lam_ref, turned_ref, block_ref, sums_ref):
    blocks, dofs = sums_ref.shape[0] // 2, sums_ref.shape[1]
    row = jnp.broadcast_to(lam_ref[pl.ds(tile, 1), :], (16, lam_ref.shape[1]))
    push = jnp.dot(
        row.astype(jnp.bfloat16), turned_ref[tile], preferred_element_type=jnp.float32
    )
    sums_ref[pl.ds(block_ref[0, tile], 1), :] += push[:1, :dofs]
    sums_ref[pl.ds(blocks + block_ref[1, tile], 1), :] += push[:1, dofs:]


def first_kernel(
    count_ref, block_ref, jac_ref, start_ref, kept_ref, turned_ref, live_ref, lam_ref, sums_ref,
    block, sems, small_sems,
):
    tiles = start_ref.shape[0]
    small = [
        pltpu.make_async_copy(source, target, small_sems.at[place])
        for place, (source, target) in enumerate(
            [(block_ref, block), (start_ref, lam_ref)]
        )
    ]
    copies = [
        pltpu.make_async_copy(jac_ref.at[tile], kept_ref.at[tile], sems.at[tile])
        for tile in range(tiles)
    ]
    groups = [range(first, min(first + GROUP, tiles)) for first in range(0, tiles, GROUP)]
    for copy in small + copies:
        copy.start()
    sums_ref[...] = jnp.zeros_like(sums_ref)
    for copy in small:
        copy.wait()
    order = lax.broadcasted_iota(jnp.int32, lam_ref.shape, 0)
    live_ref[...] = jnp.where(order < count_ref[0], 1.0, 0.0)
    lam_ref[...] = lam_ref[...] * live_ref[...]
    for group, before in zip(groups + [[]], [[]] + groups):
        for tile in group:
            copies[tile].wait()
        for tile in group:
            turned_ref[tile] = kept_ref[tile].T
        for tile in before:
            push_tile(tile, lam_ref, turned_ref, block, sums_ref)


def sweep_kernel(
    parts, block_ref, live_ref, jac_ref, turned_ref, bias_ref, step_ref, friction_ref, old_ref, *refs
):
    part_refs, (out_ref, sums_ref, vel_ref, rel_ref, *held) = refs[:parts], refs[parts:]
    lam_ref = held[0] if held else out_ref
    tiles = old_ref.shape[0]
    blocks, dofs = vel_ref.shape[0] // 2, vel_ref.shape[1]
    vel_ref[...] = tree([ref[...].astype(jnp.float32) for ref in part_refs])
    sums_ref[...] = jnp.zeros_like(sums_ref)
    for tile in range(tiles):
        own_row = vel_ref[pl.ds(block_ref[0, tile], 1), :]
        next_row = vel_ref[pl.ds(blocks + block_ref[1, tile], 1), :]
        row = jnp.broadcast_to(jnp.concatenate([own_row, next_row], axis=1), (16, 2 * dofs))
        rel = jnp.dot(row.astype(jnp.bfloat16), jac_ref[tile], preferred_element_type=jnp.float32)
        rel_ref[pl.ds(tile, 1), :] = rel[:1]
    trial = old_ref[...] - step_ref[...] * (rel_ref[...] + bias_ref[...])
    lam = project(trial, friction_ref[...], friction_ref.shape[1])
    lam_ref[...] = lam * live_ref[...]
    copies = [pltpu.make_async_copy(lam_ref, out_ref, held[1])] if held else []
    for copy in copies:
        copy.start()
    for tile in range(tiles):
        push_tile(tile, lam_ref, turned_ref, block_ref, sums_ref)
    for copy in copies:
        copy.wait()


GROUP = 4
LIMIT = 24 * 1024 * 1024
SMEM = pl.BlockSpec(memory_space=pltpu.SMEM)
VMEM = pl.BlockSpec(memory_space=pltpu.VMEM)


def result_shapes(lam, blocks, dofs):
    return [
        jax.ShapeDtypeStruct(lam.shape, jnp.float32),
        jax.ShapeDtypeStruct((2 * blocks, dofs), jnp.float32),
    ]


def first_push(jacobian, tile_block, tile_count, start, blocks):
    tiles, rows, cols = jacobian.shape
    lam_shape, sums_shape = result_shapes(start, blocks, rows // 2)
    held = [
        pltpu.with_memory_space_constraint(array, pltpu.HBM)
        for array in (tile_block, jacobian, start)
    ]
    return pl.pallas_call(
        first_kernel,
        out_shape=[
            pltpu.VMEM((tiles, rows, cols), jacobian.dtype),
            pltpu.VMEM((tiles, cols, rows), jacobian.dtype),
            lam_shape, lam_shape, sums_shape,
        ],
        in_specs=[SMEM] + [pl.BlockSpec(memory_space=pltpu.HBM)] * 3,
        out_specs=[VMEM] * 5,
        scratch_shapes=[
            pltpu.SMEM(tile_block.shape, jnp.int32),
            pltpu.SemaphoreType.DMA((tiles,)),
            pltpu.SemaphoreType.DMA((2,)),
        ],
        compiler_params=pltpu.CompilerParams(vmem_limit_bytes=LIMIT),
        cost_estimate=pl.CostEstimate(
            flops=2 * jacobian.size, bytes_accessed=2 * jacobian.size, transcendentals=0
        ),
        name="first_push",
    )(tile_count, *held)


def sweep_step(kept, turned, tile_block, live, bias, step, friction, lam, parts, last):
    rows, dofs = parts[0].shape
    kept = pltpu.with_memory_space_constraint(kept, pltpu.VMEM)
    turned = pltpu.with_memory_space_constraint(turned, pltpu.VMEM)
    return pl.pallas_call(
        functools.partial(sweep_kernel, len(parts)),
        out_shape=result_shapes(lam, rows // 2, dofs),
        in_specs=[SMEM] + [VMEM] * (7 + len(parts)),
        out_specs=[pl.BlockSpec(memory_space=pl.ANY) if last else VMEM, VMEM],
        scratch_shapes=[
            pltpu.VMEM((rows, dofs), jnp.float32),
            pltpu.VMEM(lam.shape, jnp.float32),
        ]
        + ([pltpu.VMEM(lam.shape, jnp.float32), pltpu.SemaphoreType.DMA] if last else []),
        compiler_params=pltpu.CompilerParams(vmem_limit_bytes=LIMIT),
        cost_estimate=pl.CostEstimate(
            flops=4 * kept.size, bytes_accessed=4 * kept.size, transcendentals=0
        ),
        name="sweep_step",
    )(tile_block, live, kept, turned, bias, step, friction, lam, *parts)


def per_device(
    jacobian, tile_block, tile_count, vel_free, inv_mass, bias, step_scale, friction, impulse_start
):
    tiles, sides, dofs, rows = jacobian.shape
    blocks = vel_free.shape[0]
    flat = jacobian.reshape(tiles, sides * dofs, rows)
    even = (lax.axis_index("body") & 1) == 0
    even, tile_block = lax.optimization_barrier((even, tile_block.T))
    kept, turned, live, lam, sums = first_push(
        flat, tile_block, tile_count, impulse_start, blocks
    )
    share, mass_next = vel_free * (1.0 / pair_count()), None
    for sweep in range(ITERS):
        both = pair_sum(sums)
        own, later = both[:blocks], both[blocks:]
        extra = [rounded(inv_mass)] if mass_next is None else []
        from_last, from_next = traded(
            rounded(later), rounded(share + inv_mass * own), even, *extra
        )
        if mass_next is None:
            mass_next = from_next[blocks:].astype(jnp.float32)
        parts = over_pairs(
            jnp.concatenate(
                [share + inv_mass * (own + from_last), from_next[:blocks] + mass_next * later]
            )
        )
        lam, sums = sweep_step(
            kept, turned, tile_block, live, bias, step_scale, friction, lam, parts,
            last=sweep == ITERS - 1,
        )
    both = pair_sum(sums)
    from_last = crossed(rounded(both[blocks:]), ahead_of)
    total = tree([part.astype(jnp.float32) for part in over_pairs(both[:blocks] + from_last)])
    velocity = vel_free + inv_mass * total
    return (lam, velocity)


def solution(mesh):
    placed = (
        P(("contact", "body"), None, None, None),
        P(("contact", "body"), None),
        P(("contact", "body")),
        P("body", None),
        P("body", None),
        P(("contact", "body"), None),
        P(("contact", "body"), None),
        P(("contact", "body"), None),
        P(("contact", "body"), None),
    )
    return jax.shard_map(
        per_device,
        mesh=mesh,
        in_specs=placed,
        out_specs=(P(("contact", "body"), None), P("body", None)),
        check_vma=False,
    )
```

```python
import functools

import jax
import jax.numpy as jnp
from jax import lax
from jax.experimental import pallas as pl
from jax.experimental.pallas import tpu as pltpu
from jax.sharding import PartitionSpec as P

ITERS = 2


def crossed(value, target):
    count, groups = lax.axis_size("body"), lax.axis_size("contact")
    cross = 1 if groups % 2 == 0 else 0
    pairs = [
        (group * count + place, (group ^ cross) * count + target(place) % count)
        for group in range(groups)
        for place in range(count)
    ]
    return lax.ppermute(value, ("contact", "body"), pairs)


def ahead_of(place):
    return place + 1


def traded(ahead, back, even, *extra):
    both = lambda value: jnp.concatenate([value, *extra]) if extra else value
    if lax.axis_size("body") % 2:
        return crossed(ahead, ahead_of), crossed(both(back), lambda place: place - 1)
    far, close = lax.optimization_barrier(
        (both(jnp.where(even, back, ahead)), both(jnp.where(even, ahead, back)))
    )
    wide = crossed(far, lambda place: place + 2 * (place % 2) - 1)
    near = crossed(close, lambda place: place ^ 1)
    rows = ahead.shape[0]
    return jnp.where(even, wide[:rows], near[:rows]), jnp.where(even, near, wide)


def rounded(value):
    return value.astype(jnp.bfloat16)


def tree(values):
    while len(values) > 1:
        values = [left + right for left, right in zip(values[::2], values[1::2])]
    return values[0]


def pair_sum(value):
    count = lax.axis_size("contact")
    if count % 2:
        return value
    return value + lax.ppermute(value, "contact", [(place, place ^ 1) for place in range(count)])


def pair_count():
    count = lax.axis_size("contact")
    return count if count % 2 else count // 2


def over_pairs(value):
    count = lax.axis_size("contact")
    if count & (count - 1):
        mine = (lax.axis_index("contact") & 1) == 0
        return [lax.psum(value if count % 2 else jnp.where(mine, value, 0.0), "contact")]
    stride, parts = 2, [value]
    while stride < count:
        radix = min(count // stride, 4)
        value = rounded(tree([part.astype(jnp.float32) for part in parts]))
        parts = []
        for digit in range(1, radix):
            pairs = [(place, place ^ (digit * stride) ^ 1) for place in range(count)]
            parts.append(lax.ppermute(value, "contact", pairs))
        parts.append(value)
        stride *= radix
    return parts


def project(trial, friction, contacts):
    normal = trial[:, :contacts]
    first = trial[:, contacts : 2 * contacts]
    second = trial[:, 2 * contacts :]
    tangent = jnp.sqrt(first * first + second * second)
    inside = tangent <= friction * normal
    below = friction * tangent <= -normal
    moved = (normal + friction * tangent) / (1.0 + friction * friction)
    safe = jnp.where(inside | below, 1.0, tangent)
    factor = jnp.where(inside, 1.0, jnp.where(below, 0.0, friction * moved / safe))
    new_normal = jnp.where(inside, normal, jnp.where(below, 0.0, moved))
    return jnp.concatenate([new_normal, first * factor, second * factor], axis=1)


def push_tile(tile, lam_ref, turned_ref, block_ref, sums_ref):
    blocks, dofs = sums_ref.shape[0] // 2, sums_ref.shape[1]
    row = jnp.broadcast_to(lam_ref[pl.ds(tile, 1), :], (16, lam_ref.shape[1]))
    push = jnp.dot(
        row.astype(jnp.bfloat16), turned_ref[tile], preferred_element_type=jnp.float32
    )
    sums_ref[pl.ds(block_ref[0, tile], 1), :] += push[:1, :dofs]
    sums_ref[pl.ds(blocks + block_ref[1, tile], 1), :] += push[:1, dofs:]


def first_kernel(
    count_ref, block_ref, jac_ref, start_ref, kept_ref, turned_ref, live_ref, lam_ref, sums_ref,
    block, sems, small_sems,
):
    tiles = start_ref.shape[0]
    small = [
        pltpu.make_async_copy(source, target, small_sems.at[place])
        for place, (source, target) in enumerate(
            [(block_ref, block), (start_ref, lam_ref)]
        )
    ]
    copies = [
        pltpu.make_async_copy(jac_ref.at[tile], kept_ref.at[tile], sems.at[tile])
        for tile in range(tiles)
    ]
    groups = [range(first, min(first + GROUP, tiles)) for first in range(0, tiles, GROUP)]
    started = 3 * GROUP
    for copy in small + copies[:started]:
        copy.start()
    sums_ref[...] = jnp.zeros_like(sums_ref)
    for copy in small:
        copy.wait()
    order = lax.broadcasted_iota(jnp.int32, lam_ref.shape, 0)
    live_ref[...] = jnp.where(order < count_ref[0], 1.0, 0.0)
    lam_ref[...] = lam_ref[...] * live_ref[...]
    for group, before in zip(groups + [[]], [[]] + groups):
        for tile in group:
            copies[tile].wait()
        for copy in copies[started : started + len(group)]:
            copy.start()
        started += len(group)
        for tile in group:
            turned_ref[tile] = kept_ref[tile].T
        for tile in before:
            push_tile(tile, lam_ref, turned_ref, block, sums_ref)


def sweep_kernel(
    parts, block_ref, live_ref, jac_ref, turned_ref, bias_ref, step_ref, friction_ref, old_ref, *refs
):
    part_refs, (out_ref, sums_ref, vel_ref, rel_ref, *held) = refs[:parts], refs[parts:]
    lam_ref = held[0] if held else out_ref
    tiles = old_ref.shape[0]
    blocks, dofs = vel_ref.shape[0] // 2, vel_ref.shape[1]
    vel_ref[...] = tree([ref[...].astype(jnp.float32) for ref in part_refs])
    sums_ref[...] = jnp.zeros_like(sums_ref)
    for tile in range(tiles):
        own_row = vel_ref[pl.ds(block_ref[0, tile], 1), :]
        next_row = vel_ref[pl.ds(blocks + block_ref[1, tile], 1), :]
        row = jnp.broadcast_to(jnp.concatenate([own_row, next_row], axis=1), (16, 2 * dofs))
        rel = jnp.dot(row.astype(jnp.bfloat16), jac_ref[tile], preferred_element_type=jnp.float32)
        rel_ref[pl.ds(tile, 1), :] = rel[:1]
    trial = old_ref[...] - step_ref[...] * (rel_ref[...] + bias_ref[...])
    lam = project(trial, friction_ref[...], friction_ref.shape[1])
    lam_ref[...] = lam * live_ref[...]
    copies = [pltpu.make_async_copy(lam_ref, out_ref, held[1])] if held else []
    for copy in copies:
        copy.start()
    for tile in range(tiles):
        push_tile(tile, lam_ref, turned_ref, block_ref, sums_ref)
    for copy in copies:
        copy.wait()


GROUP = 2
LIMIT = 24 * 1024 * 1024
SMEM = pl.BlockSpec(memory_space=pltpu.SMEM)
VMEM = pl.BlockSpec(memory_space=pltpu.VMEM)


def result_shapes(lam, blocks, dofs):
    return [
        jax.ShapeDtypeStruct(lam.shape, jnp.float32),
        jax.ShapeDtypeStruct((2 * blocks, dofs), jnp.float32),
    ]


def first_push(jacobian, tile_block, tile_count, start, blocks):
    tiles, rows, cols = jacobian.shape
    lam_shape, sums_shape = result_shapes(start, blocks, rows // 2)
    held = [
        pltpu.with_memory_space_constraint(array, pltpu.HBM)
        for array in (tile_block, jacobian, start)
    ]
    return pl.pallas_call(
        first_kernel,
        out_shape=[
            pltpu.VMEM((tiles, rows, cols), jacobian.dtype),
            pltpu.VMEM((tiles, cols, rows), jacobian.dtype),
            lam_shape, lam_shape, sums_shape,
        ],
        in_specs=[SMEM] + [pl.BlockSpec(memory_space=pltpu.HBM)] * 3,
        out_specs=[VMEM] * 5,
        scratch_shapes=[
            pltpu.SMEM(tile_block.shape, jnp.int32),
            pltpu.SemaphoreType.DMA((tiles,)),
            pltpu.SemaphoreType.DMA((2,)),
        ],
        compiler_params=pltpu.CompilerParams(vmem_limit_bytes=LIMIT),
        cost_estimate=pl.CostEstimate(
            flops=2 * jacobian.size, bytes_accessed=2 * jacobian.size, transcendentals=0
        ),
        name="first_push",
    )(tile_count, *held)


def sweep_step(kept, turned, tile_block, live, bias, step, friction, lam, parts, last):
    rows, dofs = parts[0].shape
    kept = pltpu.with_memory_space_constraint(kept, pltpu.VMEM)
    turned = pltpu.with_memory_space_constraint(turned, pltpu.VMEM)
    return pl.pallas_call(
        functools.partial(sweep_kernel, len(parts)),
        out_shape=result_shapes(lam, rows // 2, dofs),
        in_specs=[SMEM] + [VMEM] * (7 + len(parts)),
        out_specs=[pl.BlockSpec(memory_space=pl.ANY) if last else VMEM, VMEM],
        scratch_shapes=[
            pltpu.VMEM((rows, dofs), jnp.float32),
            pltpu.VMEM(lam.shape, jnp.float32),
        ]
        + ([pltpu.VMEM(lam.shape, jnp.float32), pltpu.SemaphoreType.DMA] if last else []),
        compiler_params=pltpu.CompilerParams(vmem_limit_bytes=LIMIT),
        cost_estimate=pl.CostEstimate(
            flops=4 * kept.size, bytes_accessed=4 * kept.size, transcendentals=0
        ),
        name="sweep_step",
    )(tile_block, live, kept, turned, bias, step, friction, lam, *parts)


def per_device(
    jacobian, tile_block, tile_count, vel_free, inv_mass, bias, step_scale, friction, impulse_start
):
    tiles, sides, dofs, rows = jacobian.shape
    blocks = vel_free.shape[0]
    flat = jacobian.reshape(tiles, sides * dofs, rows)
    even = (lax.axis_index("body") & 1) == 0
    even, tile_block = lax.optimization_barrier((even, tile_block.T))
    kept, turned, live, lam, sums = first_push(
        flat, tile_block, tile_count, impulse_start, blocks
    )
    share, mass_next = vel_free * (1.0 / pair_count()), None
    for sweep in range(ITERS):
        both = pair_sum(sums)
        own, later = both[:blocks], both[blocks:]
        extra = [rounded(inv_mass)] if mass_next is None else []
        from_last, from_next = traded(
            rounded(later), rounded(share + inv_mass * own), even, *extra
        )
        if mass_next is None:
            mass_next = from_next[blocks:].astype(jnp.float32)
        parts = over_pairs(
            jnp.concatenate(
                [share + inv_mass * (own + from_last), from_next[:blocks] + mass_next * later]
            )
        )
        lam, sums = sweep_step(
            kept, turned, tile_block, live, bias, step_scale, friction, lam, parts,
            last=sweep == ITERS - 1,
        )
    both = pair_sum(sums)
    from_last = crossed(rounded(both[blocks:]), ahead_of)
    total = tree([part.astype(jnp.float32) for part in over_pairs(both[:blocks] + from_last)])
    velocity = vel_free + inv_mass * total
    return (lam, velocity)


def solution(mesh):
    placed = (
        P(("contact", "body"), None, None, None),
        P(("contact", "body"), None),
        P(("contact", "body")),
        P("body", None),
        P("body", None),
        P(("contact", "body"), None),
        P(("contact", "body"), None),
        P(("contact", "body"), None),
        P(("contact", "body"), None),
    )
    return jax.shard_map(
        per_device,
        mesh=mesh,
        in_specs=placed,
        out_specs=(P(("contact", "body"), None), P("body", None)),
        check_vma=False,
    )
```

```python
import functools

import jax
import jax.numpy as jnp
from jax import lax
from jax.experimental import pallas as pl
from jax.experimental.pallas import tpu as pltpu
from jax.sharding import PartitionSpec as P

ITERS = 2


def crossed(value, target):
    count, groups = lax.axis_size("body"), lax.axis_size("contact")
    cross = 1 if groups % 2 == 0 else 0
    pairs = [
        (group * count + place, (group ^ cross) * count + target(place) % count)
        for group in range(groups)
        for place in range(count)
    ]
    return lax.ppermute(value, ("contact", "body"), pairs)


def ahead_of(place):
    return place + 1


def traded(ahead, back, even, *extra):
    both = lambda value: jnp.concatenate([value, *extra]) if extra else value
    if lax.axis_size("body") % 2:
        return crossed(ahead, ahead_of), crossed(both(back), lambda place: place - 1)
    near = crossed(both(jnp.where(even, ahead, back)), lambda place: place ^ 1)
    wide = crossed(both(jnp.where(even, back, ahead)), lambda place: place + 2 * (place % 2) - 1)
    rows = ahead.shape[0]
    return jnp.where(even, wide[:rows], near[:rows]), jnp.where(even, near, wide)


def rounded(value):
    return value.astype(jnp.bfloat16)


def tree(values):
    while len(values) > 1:
        values = [left + right for left, right in zip(values[::2], values[1::2])]
    return values[0]


def pair_sum(value):
    count = lax.axis_size("contact")
    if count % 2:
        return value
    return value + lax.ppermute(value, "contact", [(place, place ^ 1) for place in range(count)])


def pair_count():
    count = lax.axis_size("contact")
    return count if count % 2 else count // 2


def over_pairs(value):
    count = lax.axis_size("contact")
    if count & (count - 1):
        mine = (lax.axis_index("contact") & 1) == 0
        return [lax.psum(value if count % 2 else jnp.where(mine, value, 0.0), "contact")]
    stride, parts = 2, [value]
    while stride < count:
        radix = min(count // stride, 4)
        value = rounded(tree([part.astype(jnp.float32) for part in parts]))
        parts = []
        for digit in range(1, radix):
            pairs = [(place, place ^ (digit * stride) ^ 1) for place in range(count)]
            parts.append(lax.ppermute(value, "contact", pairs))
        parts.append(value)
        stride *= radix
    return parts


def project(trial, friction, contacts):
    normal = trial[:, :contacts]
    first = trial[:, contacts : 2 * contacts]
    second = trial[:, 2 * contacts :]
    tangent = jnp.sqrt(first * first + second * second)
    inside = tangent <= friction * normal
    below = friction * tangent <= -normal
    moved = (normal + friction * tangent) / (1.0 + friction * friction)
    safe = jnp.where(inside | below, 1.0, tangent)
    factor = jnp.where(inside, 1.0, jnp.where(below, 0.0, friction * moved / safe))
    new_normal = jnp.where(inside, normal, jnp.where(below, 0.0, moved))
    return jnp.concatenate([new_normal, first * factor, second * factor], axis=1)


def push_tile(tile, lam_ref, turned_ref, block_ref, sums_ref):
    blocks, dofs = sums_ref.shape[0] // 2, sums_ref.shape[1]
    row = jnp.broadcast_to(lam_ref[pl.ds(tile, 1), :], (16, lam_ref.shape[1]))
    push = jnp.dot(
        row.astype(jnp.bfloat16), turned_ref[tile], preferred_element_type=jnp.float32
    )
    sums_ref[pl.ds(block_ref[0, tile], 1), :] += push[:1, :dofs]
    sums_ref[pl.ds(blocks + block_ref[1, tile], 1), :] += push[:1, dofs:]


def first_kernel(
    count_ref, block_ref, jac_ref, start_ref, kept_ref, turned_ref, live_ref, lam_ref, sums_ref,
    block, sems, small_sems,
):
    tiles = start_ref.shape[0]
    small = [
        pltpu.make_async_copy(source, target, small_sems.at[place])
        for place, (source, target) in enumerate(
            [(block_ref, block), (start_ref, lam_ref)]
        )
    ]
    copies = [
        pltpu.make_async_copy(jac_ref.at[tile], kept_ref.at[tile], sems.at[tile])
        for tile in range(tiles)
    ]
    groups = [range(first, min(first + GROUP, tiles)) for first in range(0, tiles, GROUP)]
    started = 3 * GROUP
    for copy in small + copies[:started]:
        copy.start()
    sums_ref[...] = jnp.zeros_like(sums_ref)
    for copy in small:
        copy.wait()
    order = lax.broadcasted_iota(jnp.int32, lam_ref.shape, 0)
    live_ref[...] = jnp.where(order < count_ref[0], 1.0, 0.0)
    lam_ref[...] = lam_ref[...] * live_ref[...]
    for group, before in zip(groups + [[]], [[]] + groups):
        for tile in group:
            copies[tile].wait()
        for copy in copies[started : started + len(group)]:
            copy.start()
        started += len(group)
        for tile in group:
            turned_ref[tile] = kept_ref[tile].T
        for tile in before:
            push_tile(tile, lam_ref, turned_ref, block, sums_ref)


def sweep_kernel(
    parts, block_ref, live_ref, jac_ref, turned_ref, bias_ref, step_ref, friction_ref, old_ref, *refs
):
    part_refs, (out_ref, sums_ref, vel_ref, rel_ref, *held) = refs[:parts], refs[parts:]
    lam_ref = held[0] if held else out_ref
    tiles = old_ref.shape[0]
    blocks, dofs = vel_ref.shape[0] // 2, vel_ref.shape[1]
    vel_ref[...] = tree([ref[...].astype(jnp.float32) for ref in part_refs])
    sums_ref[...] = jnp.zeros_like(sums_ref)
    for tile in range(tiles):
        own_row = vel_ref[pl.ds(block_ref[0, tile], 1), :]
        next_row = vel_ref[pl.ds(blocks + block_ref[1, tile], 1), :]
        row = jnp.broadcast_to(jnp.concatenate([own_row, next_row], axis=1), (16, 2 * dofs))
        rel = jnp.dot(row.astype(jnp.bfloat16), jac_ref[tile], preferred_element_type=jnp.float32)
        rel_ref[pl.ds(tile, 1), :] = rel[:1]
    trial = old_ref[...] - step_ref[...] * (rel_ref[...] + bias_ref[...])
    lam = project(trial, friction_ref[...], friction_ref.shape[1])
    lam_ref[...] = lam * live_ref[...]
    copies = [pltpu.make_async_copy(lam_ref, out_ref, held[1])] if held else []
    for copy in copies:
        copy.start()
    for tile in range(tiles):
        push_tile(tile, lam_ref, turned_ref, block_ref, sums_ref)
    for copy in copies:
        copy.wait()


GROUP = 2
LIMIT = 24 * 1024 * 1024
SMEM = pl.BlockSpec(memory_space=pltpu.SMEM)
VMEM = pl.BlockSpec(memory_space=pltpu.VMEM)


def result_shapes(lam, blocks, dofs):
    return [
        jax.ShapeDtypeStruct(lam.shape, jnp.float32),
        jax.ShapeDtypeStruct((2 * blocks, dofs), jnp.float32),
    ]


def first_push(jacobian, tile_block, tile_count, start, blocks):
    tiles, rows, cols = jacobian.shape
    lam_shape, sums_shape = result_shapes(start, blocks, rows // 2)
    held = [
        pltpu.with_memory_space_constraint(array, pltpu.HBM)
        for array in (tile_block, jacobian, start)
    ]
    return pl.pallas_call(
        first_kernel,
        out_shape=[
            pltpu.VMEM((tiles, rows, cols), jacobian.dtype),
            pltpu.VMEM((tiles, cols, rows), jacobian.dtype),
            lam_shape, lam_shape, sums_shape,
        ],
        in_specs=[SMEM] + [pl.BlockSpec(memory_space=pltpu.HBM)] * 3,
        out_specs=[VMEM] * 5,
        scratch_shapes=[
            pltpu.SMEM(tile_block.shape, jnp.int32),
            pltpu.SemaphoreType.DMA((tiles,)),
            pltpu.SemaphoreType.DMA((2,)),
        ],
        compiler_params=pltpu.CompilerParams(vmem_limit_bytes=LIMIT),
        cost_estimate=pl.CostEstimate(
            flops=2 * jacobian.size, bytes_accessed=2 * jacobian.size, transcendentals=0
        ),
        name="first_push",
    )(tile_count, *held)


def sweep_step(kept, turned, tile_block, live, bias, step, friction, lam, parts, last):
    rows, dofs = parts[0].shape
    kept = pltpu.with_memory_space_constraint(kept, pltpu.VMEM)
    turned = pltpu.with_memory_space_constraint(turned, pltpu.VMEM)
    return pl.pallas_call(
        functools.partial(sweep_kernel, len(parts)),
        out_shape=result_shapes(lam, rows // 2, dofs),
        in_specs=[SMEM] + [VMEM] * (7 + len(parts)),
        out_specs=[pl.BlockSpec(memory_space=pl.ANY) if last else VMEM, VMEM],
        scratch_shapes=[
            pltpu.VMEM((rows, dofs), jnp.float32),
            pltpu.VMEM(lam.shape, jnp.float32),
        ]
        + ([pltpu.VMEM(lam.shape, jnp.float32), pltpu.SemaphoreType.DMA] if last else []),
        compiler_params=pltpu.CompilerParams(vmem_limit_bytes=LIMIT),
        cost_estimate=pl.CostEstimate(
            flops=4 * kept.size, bytes_accessed=4 * kept.size, transcendentals=0
        ),
        name="sweep_step",
    )(tile_block, live, kept, turned, bias, step, friction, lam, *parts)


def per_device(
    jacobian, tile_block, tile_count, vel_free, inv_mass, bias, step_scale, friction, impulse_start
):
    tiles, sides, dofs, rows = jacobian.shape
    blocks = vel_free.shape[0]
    flat = jacobian.reshape(tiles, sides * dofs, rows)
    even = (lax.axis_index("body") & 1) == 0
    even, tile_block = lax.optimization_barrier((even, tile_block.T))
    kept, turned, live, lam, sums = first_push(
        flat, tile_block, tile_count, impulse_start, blocks
    )
    share, mass_next = vel_free * (1.0 / pair_count()), None
    for sweep in range(ITERS):
        both = pair_sum(sums)
        own, later = both[:blocks], both[blocks:]
        extra = [rounded(inv_mass)] if mass_next is None else []
        from_last, from_next = traded(
            rounded(later), rounded(share + inv_mass * own), even, *extra
        )
        if mass_next is None:
            mass_next = from_next[blocks:].astype(jnp.float32)
        parts = over_pairs(
            jnp.concatenate(
                [share + inv_mass * (own + from_last), from_next[:blocks] + mass_next * later]
            )
        )
        lam, sums = sweep_step(
            kept, turned, tile_block, live, bias, step_scale, friction, lam, parts,
            last=sweep == ITERS - 1,
        )
    both = pair_sum(sums)
    from_last = crossed(rounded(both[blocks:]), ahead_of)
    total = tree([part.astype(jnp.float32) for part in over_pairs(both[:blocks] + from_last)])
    velocity = vel_free + inv_mass * total
    return (lam, velocity)


def solution(mesh):
    placed = (
        P(("contact", "body"), None, None, None),
        P(("contact", "body"), None),
        P(("contact", "body")),
        P("body", None),
        P("body", None),
        P(("contact", "body"), None),
        P(("contact", "body"), None),
        P(("contact", "body"), None),
        P(("contact", "body"), None),
    )
    return jax.shard_map(
        per_device,
        mesh=mesh,
        in_specs=placed,
        out_specs=(P(("contact", "body"), None), P("body", None)),
        check_vma=False,
    )
```

```python
import functools

import jax
import jax.numpy as jnp
from jax import lax
from jax.experimental import pallas as pl
from jax.experimental.pallas import tpu as pltpu
from jax.sharding import PartitionSpec as P

ITERS = 2


def crossed(value, target):
    count, groups = lax.axis_size("body"), lax.axis_size("contact")
    cross = 1 if groups % 2 == 0 else 0
    pairs = [
        (group * count + place, (group ^ cross) * count + target(place) % count)
        for group in range(groups)
        for place in range(count)
    ]
    return lax.ppermute(value, ("contact", "body"), pairs)


def ahead_of(place):
    return place + 1


def traded(ahead, back, even, *extra):
    both = lambda value: jnp.concatenate([value, *extra]) if extra else value
    if lax.axis_size("body") % 2:
        return crossed(ahead, ahead_of), crossed(both(back), lambda place: place - 1)
    far, close = lax.optimization_barrier(
        (both(jnp.where(even, back, ahead)), both(jnp.where(even, ahead, back)))
    )
    wide = crossed(far, lambda place: place + 2 * (place % 2) - 1)
    near = crossed(close, lambda place: place ^ 1)
    rows = ahead.shape[0]
    return jnp.where(even, wide[:rows], near[:rows]), jnp.where(even, near, wide)


def rounded(value):
    return value.astype(jnp.bfloat16)


def tree(values):
    while len(values) > 1:
        values = [left + right for left, right in zip(values[::2], values[1::2])]
    return values[0]


def pair_sum(value):
    count = lax.axis_size("contact")
    if count % 2:
        return value
    return value + lax.ppermute(value, "contact", [(place, place ^ 1) for place in range(count)])


def pair_count():
    count = lax.axis_size("contact")
    return count if count % 2 else count // 2


def over_pairs(value):
    count = lax.axis_size("contact")
    if count & (count - 1):
        mine = (lax.axis_index("contact") & 1) == 0
        return [lax.psum(value if count % 2 else jnp.where(mine, value, 0.0), "contact")]
    stride, parts = 2, [value]
    while stride < count:
        radix = min(count // stride, 4)
        value = rounded(tree([part.astype(jnp.float32) for part in parts]))
        parts = []
        for digit in range(1, radix):
            pairs = [(place, place ^ (digit * stride) ^ 1) for place in range(count)]
            parts.append(lax.ppermute(value, "contact", pairs))
        parts.append(value)
        stride *= radix
    return parts


def project(trial, friction, contacts):
    normal = trial[:, :contacts]
    first = trial[:, contacts : 2 * contacts]
    second = trial[:, 2 * contacts :]
    tangent = jnp.sqrt(first * first + second * second)
    inside = tangent <= friction * normal
    below = friction * tangent <= -normal
    moved = (normal + friction * tangent) / (1.0 + friction * friction)
    safe = jnp.where(inside | below, 1.0, tangent)
    factor = jnp.where(inside, 1.0, jnp.where(below, 0.0, friction * moved / safe))
    new_normal = jnp.where(inside, normal, jnp.where(below, 0.0, moved))
    return jnp.concatenate([new_normal, first * factor, second * factor], axis=1)


def push_tile(tile, lam_ref, turned_ref, block_ref, sums_ref):
    blocks, dofs = sums_ref.shape[0] // 2, sums_ref.shape[1]
    row = jnp.broadcast_to(lam_ref[pl.ds(tile, 1), :], (16, lam_ref.shape[1]))
    push = jnp.dot(
        row.astype(jnp.bfloat16), turned_ref[tile], preferred_element_type=jnp.float32
    )
    sums_ref[pl.ds(block_ref[0, tile], 1), :] += push[:1, :dofs]
    sums_ref[pl.ds(blocks + block_ref[1, tile], 1), :] += push[:1, dofs:]


def first_kernel(
    count_ref, block_ref, jac_ref, start_ref, kept_ref, turned_ref, live_ref, lam_ref, sums_ref,
    block, sems, small_sems,
):
    tiles = start_ref.shape[0]
    small = [
        pltpu.make_async_copy(source, target, small_sems.at[place])
        for place, (source, target) in enumerate(
            [(block_ref, block), (start_ref, lam_ref)]
        )
    ]
    copies = [
        pltpu.make_async_copy(jac_ref.at[tile], kept_ref.at[tile], sems.at[tile])
        for tile in range(tiles)
    ]
    groups = [range(first, min(first + GROUP, tiles)) for first in range(0, tiles, GROUP)]
    started = 3 * GROUP
    for copy in small + copies[:started]:
        copy.start()
    sums_ref[...] = jnp.zeros_like(sums_ref)
    for copy in small:
        copy.wait()
    order = lax.broadcasted_iota(jnp.int32, lam_ref.shape, 0)
    live_ref[...] = jnp.where(order < count_ref[0], 1.0, 0.0)
    lam_ref[...] = lam_ref[...] * live_ref[...]
    for group, before in zip(groups + [[]], [[]] + groups):
        for tile in group:
            copies[tile].wait()
        for copy in copies[started : started + len(group)]:
            copy.start()
        started += len(group)
        for tile in group:
            turned_ref[tile] = kept_ref[tile].T
        for tile in before:
            push_tile(tile, lam_ref, turned_ref, block, sums_ref)


def sweep_kernel(
    parts, block_ref, live_ref, jac_ref, turned_ref, bias_ref, step_ref, friction_ref, old_ref, *refs
):
    part_refs, (out_ref, sums_ref, vel_ref, rel_ref, *held) = refs[:parts], refs[parts:]
    lam_ref = held[0] if held else out_ref
    tiles = old_ref.shape[0]
    blocks, dofs = vel_ref.shape[0] // 2, vel_ref.shape[1]
    vel_ref[...] = tree([ref[...].astype(jnp.float32) for ref in part_refs])
    sums_ref[...] = jnp.zeros_like(sums_ref)
    step = 8 if tiles % 8 == 0 else tiles
    halves = [range(first, first + step) for first in range(0, tiles, step)]

    def rel_tiles(half):
        for tile in half:
            own_row = vel_ref[pl.ds(block_ref[0, tile], 1), :]
            next_row = vel_ref[pl.ds(blocks + block_ref[1, tile], 1), :]
            row = jnp.broadcast_to(jnp.concatenate([own_row, next_row], axis=1), (16, 2 * dofs))
            rel = jnp.dot(
                row.astype(jnp.bfloat16), jac_ref[tile], preferred_element_type=jnp.float32
            )
            rel_ref[pl.ds(tile, 1), :] = rel[:1]

    def project_tiles(half):
        part = slice(half[0], half[-1] + 1)
        trial = old_ref[part] - step_ref[part] * (rel_ref[part] + bias_ref[part])
        lam = project(trial, friction_ref[part], friction_ref.shape[1])
        lam_ref[part] = lam * live_ref[part]

    rel_tiles(halves[0])
    copies = [pltpu.make_async_copy(lam_ref, out_ref, held[1])] if held else []
    for half, after in zip(halves, halves[1:] + [[]]):
        project_tiles(half)
        rel_tiles(after)
        if not after:
            for copy in copies:
                copy.start()
        for tile in half:
            push_tile(tile, lam_ref, turned_ref, block_ref, sums_ref)
    for copy in copies:
        copy.wait()


GROUP = 2
LIMIT = 24 * 1024 * 1024
SMEM = pl.BlockSpec(memory_space=pltpu.SMEM)
VMEM = pl.BlockSpec(memory_space=pltpu.VMEM)


def result_shapes(lam, blocks, dofs):
    return [
        jax.ShapeDtypeStruct(lam.shape, jnp.float32),
        jax.ShapeDtypeStruct((2 * blocks, dofs), jnp.float32),
    ]


def first_push(jacobian, tile_block, tile_count, start, blocks):
    tiles, rows, cols = jacobian.shape
    lam_shape, sums_shape = result_shapes(start, blocks, rows // 2)
    held = [
        pltpu.with_memory_space_constraint(array, pltpu.HBM)
        for array in (tile_block, jacobian, start)
    ]
    return pl.pallas_call(
        first_kernel,
        out_shape=[
            pltpu.VMEM((tiles, rows, cols), jacobian.dtype),
            pltpu.VMEM((tiles, cols, rows), jacobian.dtype),
            lam_shape, lam_shape, sums_shape,
        ],
        in_specs=[SMEM] + [pl.BlockSpec(memory_space=pltpu.HBM)] * 3,
        out_specs=[VMEM] * 5,
        scratch_shapes=[
            pltpu.SMEM(tile_block.shape, jnp.int32),
            pltpu.SemaphoreType.DMA((tiles,)),
            pltpu.SemaphoreType.DMA((2,)),
        ],
        compiler_params=pltpu.CompilerParams(vmem_limit_bytes=LIMIT),
        cost_estimate=pl.CostEstimate(
            flops=2 * jacobian.size, bytes_accessed=2 * jacobian.size, transcendentals=0
        ),
        name="first_push",
    )(tile_count, *held)


def sweep_step(kept, turned, tile_block, live, bias, step, friction, lam, parts, last):
    rows, dofs = parts[0].shape
    kept = pltpu.with_memory_space_constraint(kept, pltpu.VMEM)
    turned = pltpu.with_memory_space_constraint(turned, pltpu.VMEM)
    return pl.pallas_call(
        functools.partial(sweep_kernel, len(parts)),
        out_shape=result_shapes(lam, rows // 2, dofs),
        in_specs=[SMEM] + [VMEM] * (7 + len(parts)),
        out_specs=[pl.BlockSpec(memory_space=pl.ANY) if last else VMEM, VMEM],
        scratch_shapes=[
            pltpu.VMEM((rows, dofs), jnp.float32),
            pltpu.VMEM(lam.shape, jnp.float32),
        ]
        + ([pltpu.VMEM(lam.shape, jnp.float32), pltpu.SemaphoreType.DMA] if last else []),
        compiler_params=pltpu.CompilerParams(vmem_limit_bytes=LIMIT),
        cost_estimate=pl.CostEstimate(
            flops=4 * kept.size, bytes_accessed=4 * kept.size, transcendentals=0
        ),
        name="sweep_step",
    )(tile_block, live, kept, turned, bias, step, friction, lam, *parts)


def per_device(
    jacobian, tile_block, tile_count, vel_free, inv_mass, bias, step_scale, friction, impulse_start
):
    tiles, sides, dofs, rows = jacobian.shape
    blocks = vel_free.shape[0]
    flat = jacobian.reshape(tiles, sides * dofs, rows)
    even = (lax.axis_index("body") & 1) == 0
    even, tile_block = lax.optimization_barrier((even, tile_block.T))
    kept, turned, live, lam, sums = first_push(
        flat, tile_block, tile_count, impulse_start, blocks
    )
    share, mass_next = vel_free * (1.0 / pair_count()), None
    for sweep in range(ITERS):
        both = pair_sum(sums)
        own, later = both[:blocks], both[blocks:]
        extra = [rounded(inv_mass)] if mass_next is None else []
        from_last, from_next = traded(
            rounded(later), rounded(share + inv_mass * own), even, *extra
        )
        if mass_next is None:
            mass_next = from_next[blocks:].astype(jnp.float32)
        parts = over_pairs(
            jnp.concatenate(
                [share + inv_mass * (own + from_last), from_next[:blocks] + mass_next * later]
            )
        )
        lam, sums = sweep_step(
            kept, turned, tile_block, live, bias, step_scale, friction, lam, parts,
            last=sweep == ITERS - 1,
        )
    both = pair_sum(sums)
    from_last = crossed(rounded(both[blocks:]), ahead_of)
    total = tree([part.astype(jnp.float32) for part in over_pairs(both[:blocks] + from_last)])
    velocity = vel_free + inv_mass * total
    return (lam, velocity)


def solution(mesh):
    placed = (
        P(("contact", "body"), None, None, None),
        P(("contact", "body"), None),
        P(("contact", "body")),
        P("body", None),
        P("body", None),
        P(("contact", "body"), None),
        P(("contact", "body"), None),
        P(("contact", "body"), None),
        P(("contact", "body"), None),
    )
    return jax.shard_map(
        per_device,
        mesh=mesh,
        in_specs=placed,
        out_specs=(P(("contact", "body"), None), P("body", None)),
        check_vma=False,
    )
```

```python
import functools

import jax
import jax.numpy as jnp
from jax import lax
from jax.experimental import pallas as pl
from jax.experimental.pallas import tpu as pltpu
from jax.sharding import PartitionSpec as P

ITERS = 2


def crossed(value, target):
    count, groups = lax.axis_size("body"), lax.axis_size("contact")
    cross = 1 if groups % 2 == 0 else 0
    pairs = [
        (group * count + place, (group ^ cross) * count + target(place) % count)
        for group in range(groups)
        for place in range(count)
    ]
    return lax.ppermute(value, ("contact", "body"), pairs)


def ahead_of(place):
    return place + 1


def traded(ahead, back, even, *extra):
    both = lambda value: jnp.concatenate([value, *extra]) if extra else value
    if lax.axis_size("body") % 2:
        return crossed(ahead, ahead_of), crossed(both(back), lambda place: place - 1)
    far, close = lax.optimization_barrier(
        (both(jnp.where(even, back, ahead)), both(jnp.where(even, ahead, back)))
    )
    wide = crossed(far, lambda place: place + 2 * (place % 2) - 1)
    near = crossed(close, lambda place: place ^ 1)
    rows = ahead.shape[0]
    return jnp.where(even, wide[:rows], near[:rows]), jnp.where(even, near, wide)


def rounded(value):
    return value.astype(jnp.bfloat16)


def tree(values):
    while len(values) > 1:
        values = [left + right for left, right in zip(values[::2], values[1::2])]
    return values[0]


def pair_sum(value):
    count = lax.axis_size("contact")
    if count % 2:
        return value
    return value + lax.ppermute(value, "contact", [(place, place ^ 1) for place in range(count)])


def pair_count():
    count = lax.axis_size("contact")
    return count if count % 2 else count // 2


def over_pairs(value):
    count = lax.axis_size("contact")
    if count & (count - 1):
        mine = (lax.axis_index("contact") & 1) == 0
        return [lax.psum(value if count % 2 else jnp.where(mine, value, 0.0), "contact")]
    stride, parts = 2, [value]
    while stride < count:
        radix = min(count // stride, 4)
        value = rounded(tree([part.astype(jnp.float32) for part in parts]))
        parts = []
        for digit in [1, 3, 2][: radix - 1]:
            pairs = [(place, place ^ (digit * stride) ^ 1) for place in range(count)]
            parts.append(lax.ppermute(value, "contact", pairs))
        parts.append(value)
        stride *= radix
    return parts


def project(trial, friction, contacts):
    normal = trial[:, :contacts]
    first = trial[:, contacts : 2 * contacts]
    second = trial[:, 2 * contacts :]
    tangent = jnp.sqrt(first * first + second * second)
    inside = tangent <= friction * normal
    below = friction * tangent <= -normal
    moved = (normal + friction * tangent) / (1.0 + friction * friction)
    safe = jnp.where(inside | below, 1.0, tangent)
    factor = jnp.where(inside, 1.0, jnp.where(below, 0.0, friction * moved / safe))
    new_normal = jnp.where(inside, normal, jnp.where(below, 0.0, moved))
    return jnp.concatenate([new_normal, first * factor, second * factor], axis=1)


def push_tile(tile, lam_ref, turned_ref, block_ref, sums_ref):
    blocks, dofs = sums_ref.shape[0] // 2, sums_ref.shape[1]
    row = jnp.broadcast_to(lam_ref[pl.ds(tile, 1), :], (16, lam_ref.shape[1]))
    push = jnp.dot(
        row.astype(jnp.bfloat16), turned_ref[tile], preferred_element_type=jnp.float32
    )
    sums_ref[pl.ds(block_ref[0, tile], 1), :] += push[:1, :dofs]
    sums_ref[pl.ds(blocks + block_ref[1, tile], 1), :] += push[:1, dofs:]


def first_kernel(
    count_ref, block_ref, jac_ref, start_ref, kept_ref, turned_ref, live_ref, lam_ref, sums_ref,
    block, sems, small_sems,
):
    tiles = start_ref.shape[0]
    small = [
        pltpu.make_async_copy(source, target, small_sems.at[place])
        for place, (source, target) in enumerate(
            [(block_ref, block), (start_ref, lam_ref)]
        )
    ]
    copies = [
        pltpu.make_async_copy(jac_ref.at[tile], kept_ref.at[tile], sems.at[tile])
        for tile in range(tiles)
    ]
    groups = [range(first, min(first + GROUP, tiles)) for first in range(0, tiles, GROUP)]
    started = 3 * GROUP
    for copy in small + copies[:started]:
        copy.start()
    sums_ref[...] = jnp.zeros_like(sums_ref)
    for copy in small:
        copy.wait()
    order = lax.broadcasted_iota(jnp.int32, lam_ref.shape, 0)
    live_ref[...] = jnp.where(order < count_ref[0], 1.0, 0.0)
    lam_ref[...] = lam_ref[...] * live_ref[...]
    for group, before in zip(groups + [[]], [[]] + groups):
        for tile in group:
            copies[tile].wait()
        for copy in copies[started : started + len(group)]:
            copy.start()
        started += len(group)
        for tile in group:
            turned_ref[tile] = kept_ref[tile].T
        for tile in before:
            push_tile(tile, lam_ref, turned_ref, block, sums_ref)


def sweep_kernel(
    parts, block_ref, live_ref, jac_ref, turned_ref, bias_ref, step_ref, friction_ref, old_ref, *refs
):
    part_refs, (out_ref, sums_ref, vel_ref, rel_ref, *held) = refs[:parts], refs[parts:]
    lam_ref = held[0] if held else out_ref
    tiles = old_ref.shape[0]
    blocks, dofs = vel_ref.shape[0] // 2, vel_ref.shape[1]
    vel_ref[...] = tree([ref[...].astype(jnp.float32) for ref in part_refs])
    sums_ref[...] = jnp.zeros_like(sums_ref)
    step = 8 if tiles % 8 == 0 else tiles
    halves = [range(first, first + step) for first in range(0, tiles, step)]

    def rel_tiles(half):
        for tile in half:
            own_row = vel_ref[pl.ds(block_ref[0, tile], 1), :]
            next_row = vel_ref[pl.ds(blocks + block_ref[1, tile], 1), :]
            row = jnp.broadcast_to(jnp.concatenate([own_row, next_row], axis=1), (16, 2 * dofs))
            rel = jnp.dot(
                row.astype(jnp.bfloat16), jac_ref[tile], preferred_element_type=jnp.float32
            )
            rel_ref[pl.ds(tile, 1), :] = rel[:1]

    def project_tiles(half):
        part = slice(half[0], half[-1] + 1)
        trial = old_ref[part] - step_ref[part] * (rel_ref[part] + bias_ref[part])
        lam = project(trial, friction_ref[part], friction_ref.shape[1])
        lam_ref[part] = lam * live_ref[part]

    rel_tiles(halves[0])
    copies = [pltpu.make_async_copy(lam_ref, out_ref, held[1])] if held else []
    for half, after in zip(halves, halves[1:] + [[]]):
        project_tiles(half)
        rel_tiles(after)
        if not after:
            for copy in copies:
                copy.start()
        for tile in half:
            push_tile(tile, lam_ref, turned_ref, block_ref, sums_ref)
    for copy in copies:
        copy.wait()


GROUP = 2
LIMIT = 24 * 1024 * 1024
SMEM = pl.BlockSpec(memory_space=pltpu.SMEM)
VMEM = pl.BlockSpec(memory_space=pltpu.VMEM)


def result_shapes(lam, blocks, dofs):
    return [
        jax.ShapeDtypeStruct(lam.shape, jnp.float32),
        jax.ShapeDtypeStruct((2 * blocks, dofs), jnp.float32),
    ]


def first_push(jacobian, tile_block, tile_count, start, blocks):
    tiles, rows, cols = jacobian.shape
    lam_shape, sums_shape = result_shapes(start, blocks, rows // 2)
    held = [
        pltpu.with_memory_space_constraint(array, pltpu.HBM)
        for array in (tile_block, jacobian, start)
    ]
    return pl.pallas_call(
        first_kernel,
        out_shape=[
            pltpu.VMEM((tiles, rows, cols), jacobian.dtype),
            pltpu.VMEM((tiles, cols, rows), jacobian.dtype),
            lam_shape, lam_shape, sums_shape,
        ],
        in_specs=[SMEM] + [pl.BlockSpec(memory_space=pltpu.HBM)] * 3,
        out_specs=[VMEM] * 5,
        scratch_shapes=[
            pltpu.SMEM(tile_block.shape, jnp.int32),
            pltpu.SemaphoreType.DMA((tiles,)),
            pltpu.SemaphoreType.DMA((2,)),
        ],
        compiler_params=pltpu.CompilerParams(vmem_limit_bytes=LIMIT),
        cost_estimate=pl.CostEstimate(
            flops=2 * jacobian.size, bytes_accessed=2 * jacobian.size, transcendentals=0
        ),
        name="first_push",
    )(tile_count, *held)


def sweep_step(kept, turned, tile_block, live, bias, step, friction, lam, parts, last):
    rows, dofs = parts[0].shape
    kept = pltpu.with_memory_space_constraint(kept, pltpu.VMEM)
    turned = pltpu.with_memory_space_constraint(turned, pltpu.VMEM)
    return pl.pallas_call(
        functools.partial(sweep_kernel, len(parts)),
        out_shape=result_shapes(lam, rows // 2, dofs),
        in_specs=[SMEM] + [VMEM] * (7 + len(parts)),
        out_specs=[pl.BlockSpec(memory_space=pl.ANY) if last else VMEM, VMEM],
        scratch_shapes=[
            pltpu.VMEM((rows, dofs), jnp.float32),
            pltpu.VMEM(lam.shape, jnp.float32),
        ]
        + ([pltpu.VMEM(lam.shape, jnp.float32), pltpu.SemaphoreType.DMA] if last else []),
        compiler_params=pltpu.CompilerParams(vmem_limit_bytes=LIMIT),
        cost_estimate=pl.CostEstimate(
            flops=4 * kept.size, bytes_accessed=4 * kept.size, transcendentals=0
        ),
        name="sweep_step",
    )(tile_block, live, kept, turned, bias, step, friction, lam, *parts)


def per_device(
    jacobian, tile_block, tile_count, vel_free, inv_mass, bias, step_scale, friction, impulse_start
):
    tiles, sides, dofs, rows = jacobian.shape
    blocks = vel_free.shape[0]
    flat = jacobian.reshape(tiles, sides * dofs, rows)
    even = (lax.axis_index("body") & 1) == 0
    even, tile_block = lax.optimization_barrier((even, tile_block.T))
    kept, turned, live, lam, sums = first_push(
        flat, tile_block, tile_count, impulse_start, blocks
    )
    share, mass_next = vel_free * (1.0 / pair_count()), None
    for sweep in range(ITERS):
        both = pair_sum(sums)
        own, later = both[:blocks], both[blocks:]
        extra = [rounded(inv_mass)] if mass_next is None else []
        from_last, from_next = traded(
            rounded(later), rounded(share + inv_mass * own), even, *extra
        )
        if mass_next is None:
            mass_next = from_next[blocks:].astype(jnp.float32)
        parts = over_pairs(
            jnp.concatenate(
                [share + inv_mass * (own + from_last), from_next[:blocks] + mass_next * later]
            )
        )
        lam, sums = sweep_step(
            kept, turned, tile_block, live, bias, step_scale, friction, lam, parts,
            last=sweep == ITERS - 1,
        )
    both = pair_sum(sums)
    from_last = crossed(rounded(both[blocks:]), ahead_of)
    total = tree([part.astype(jnp.float32) for part in over_pairs(both[:blocks] + from_last)])
    velocity = vel_free + inv_mass * total
    return (lam, velocity)


def solution(mesh):
    placed = (
        P(("contact", "body"), None, None, None),
        P(("contact", "body"), None),
        P(("contact", "body")),
        P("body", None),
        P("body", None),
        P(("contact", "body"), None),
        P(("contact", "body"), None),
        P(("contact", "body"), None),
        P(("contact", "body"), None),
    )
    return jax.shard_map(
        per_device,
        mesh=mesh,
        in_specs=placed,
        out_specs=(P(("contact", "body"), None), P("body", None)),
        check_vma=False,
    )
```

```python
import functools

import jax
import jax.numpy as jnp
from jax import lax
from jax.experimental import pallas as pl
from jax.experimental.pallas import tpu as pltpu
from jax.sharding import PartitionSpec as P

ITERS = 2


def crossed(value, target):
    count, groups = lax.axis_size("body"), lax.axis_size("contact")
    cross = 1 if groups % 2 == 0 else 0
    pairs = [
        (group * count + place, (group ^ cross) * count + target(place) % count)
        for group in range(groups)
        for place in range(count)
    ]
    return lax.ppermute(value, ("contact", "body"), pairs)


def ahead_of(place):
    return place + 1


def traded(ahead, back, even, *extra):
    both = lambda value: jnp.concatenate([value, *extra]) if extra else value
    if lax.axis_size("body") % 2:
        return crossed(ahead, ahead_of), crossed(both(back), lambda place: place - 1)
    far, close = lax.optimization_barrier(
        (both(jnp.where(even, back, ahead)), both(jnp.where(even, ahead, back)))
    )
    wide = crossed(far, lambda place: place + 2 * (place % 2) - 1)
    near = crossed(close, lambda place: place ^ 1)
    rows = ahead.shape[0]
    return jnp.where(even, wide[:rows], near[:rows]), jnp.where(even, near, wide)


def rounded(value):
    return value.astype(jnp.bfloat16)


def tree(values):
    while len(values) > 1:
        values = [left + right for left, right in zip(values[::2], values[1::2])]
    return values[0]


def pair_sum(value):
    count = lax.axis_size("contact")
    if count % 2:
        return value
    return value + lax.ppermute(value, "contact", [(place, place ^ 1) for place in range(count)])


def pair_count():
    count = lax.axis_size("contact")
    return count if count % 2 else count // 2


def over_pairs(value):
    count = lax.axis_size("contact")
    if count & (count - 1):
        mine = (lax.axis_index("contact") & 1) == 0
        return [lax.psum(value if count % 2 else jnp.where(mine, value, 0.0), "contact")]
    stride, parts = 2, [value]
    while stride < count:
        radix = min(count // stride, 4)
        value = rounded(tree([part.astype(jnp.float32) for part in parts]))
        parts = []
        for digit in range(1, radix):
            pairs = [(place, place ^ (digit * stride) ^ 1) for place in range(count)]
            parts.append(lax.ppermute(value, "contact", pairs))
        parts.append(value)
        stride *= radix
    return parts


def project(trial, friction, contacts):
    normal = trial[:, :contacts]
    first = trial[:, contacts : 2 * contacts]
    second = trial[:, 2 * contacts :]
    tangent = jnp.sqrt(first * first + second * second)
    inside = tangent <= friction * normal
    below = friction * tangent <= -normal
    moved = (normal + friction * tangent) / (1.0 + friction * friction)
    safe = jnp.where(inside | below, 1.0, tangent)
    factor = jnp.where(inside, 1.0, jnp.where(below, 0.0, friction * moved / safe))
    new_normal = jnp.where(inside, normal, jnp.where(below, 0.0, moved))
    return jnp.concatenate([new_normal, first * factor, second * factor], axis=1)


def push_tile(tile, lam_ref, turned_ref, block_ref, sums_ref):
    blocks, dofs = sums_ref.shape[0] // 2, sums_ref.shape[1]
    row = jnp.broadcast_to(lam_ref[pl.ds(tile, 1), :], (16, lam_ref.shape[1]))
    push = jnp.dot(
        row.astype(jnp.bfloat16), turned_ref[tile], preferred_element_type=jnp.float32
    )
    sums_ref[pl.ds(block_ref[0, tile], 1), :] += push[:1, :dofs]
    sums_ref[pl.ds(blocks + block_ref[1, tile], 1), :] += push[:1, dofs:]


def first_kernel(
    count_ref, block_ref, jac_ref, start_ref, kept_ref, turned_ref, live_ref, lam_ref, sums_ref,
    block, sems, small_sems,
):
    tiles = start_ref.shape[0]
    small = [
        pltpu.make_async_copy(source, target, small_sems.at[place])
        for place, (source, target) in enumerate(
            [(block_ref, block), (start_ref, lam_ref)]
        )
    ]
    groups = [range(first, min(first + GROUP, tiles)) for first in range(0, tiles, GROUP)]
    copies = [
        pltpu.make_async_copy(
            jac_ref.at[pl.ds(group[0], len(group))],
            kept_ref.at[pl.ds(group[0], len(group))],
            sems.at[place],
        )
        for place, group in enumerate(groups)
    ]
    for copy in small + copies[:AHEAD]:
        copy.start()
    sums_ref[...] = jnp.zeros_like(sums_ref)
    for copy in small:
        copy.wait()
    order = lax.broadcasted_iota(jnp.int32, lam_ref.shape, 0)
    live_ref[...] = jnp.where(order < count_ref[0], 1.0, 0.0)
    lam_ref[...] = lam_ref[...] * live_ref[...]
    for place, (group, before) in enumerate(zip(groups + [[]], [[]] + groups)):
        if group:
            copies[place].wait()
        for copy in copies[place + AHEAD : place + AHEAD + 1]:
            copy.start()
        for tile in group:
            turned_ref[tile] = kept_ref[tile].T
        for tile in before:
            push_tile(tile, lam_ref, turned_ref, block, sums_ref)


def sweep_kernel(
    parts, block_ref, live_ref, jac_ref, turned_ref, bias_ref, step_ref, friction_ref, old_ref, *refs
):
    part_refs, (out_ref, sums_ref, vel_ref, rel_ref, *held) = refs[:parts], refs[parts:]
    lam_ref = held[0] if held else out_ref
    tiles = old_ref.shape[0]
    blocks, dofs = vel_ref.shape[0] // 2, vel_ref.shape[1]
    vel_ref[...] = tree([ref[...].astype(jnp.float32) for ref in part_refs])
    sums_ref[...] = jnp.zeros_like(sums_ref)
    step = 8 if tiles % 8 == 0 else tiles
    halves = [range(first, first + step) for first in range(0, tiles, step)]

    def rel_tiles(half):
        for tile in half:
            own_row = vel_ref[pl.ds(block_ref[0, tile], 1), :]
            next_row = vel_ref[pl.ds(blocks + block_ref[1, tile], 1), :]
            row = jnp.broadcast_to(jnp.concatenate([own_row, next_row], axis=1), (16, 2 * dofs))
            rel = jnp.dot(
                row.astype(jnp.bfloat16), jac_ref[tile], preferred_element_type=jnp.float32
            )
            rel_ref[pl.ds(tile, 1), :] = rel[:1]

    def project_tiles(half):
        part = slice(half[0], half[-1] + 1)
        trial = old_ref[part] - step_ref[part] * (rel_ref[part] + bias_ref[part])
        lam = project(trial, friction_ref[part], friction_ref.shape[1])
        lam_ref[part] = lam * live_ref[part]

    rel_tiles(halves[0])
    copies = [pltpu.make_async_copy(lam_ref, out_ref, held[1])] if held else []
    for half, after in zip(halves, halves[1:] + [[]]):
        project_tiles(half)
        rel_tiles(after)
        if not after:
            for copy in copies:
                copy.start()
        for tile in half:
            push_tile(tile, lam_ref, turned_ref, block_ref, sums_ref)
    for copy in copies:
        copy.wait()


GROUP = 2
AHEAD = 3
LIMIT = 24 * 1024 * 1024
SMEM = pl.BlockSpec(memory_space=pltpu.SMEM)
VMEM = pl.BlockSpec(memory_space=pltpu.VMEM)


def result_shapes(lam, blocks, dofs):
    return [
        jax.ShapeDtypeStruct(lam.shape, jnp.float32),
        jax.ShapeDtypeStruct((2 * blocks, dofs), jnp.float32),
    ]


def first_push(jacobian, tile_block, tile_count, start, blocks):
    tiles, rows, cols = jacobian.shape
    lam_shape, sums_shape = result_shapes(start, blocks, rows // 2)
    held = [
        pltpu.with_memory_space_constraint(array, pltpu.HBM)
        for array in (tile_block, jacobian, start)
    ]
    return pl.pallas_call(
        first_kernel,
        out_shape=[
            pltpu.VMEM((tiles, rows, cols), jacobian.dtype),
            pltpu.VMEM((tiles, cols, rows), jacobian.dtype),
            lam_shape, lam_shape, sums_shape,
        ],
        in_specs=[SMEM] + [pl.BlockSpec(memory_space=pltpu.HBM)] * 3,
        out_specs=[VMEM] * 5,
        scratch_shapes=[
            pltpu.SMEM(tile_block.shape, jnp.int32),
            pltpu.SemaphoreType.DMA((tiles,)),
            pltpu.SemaphoreType.DMA((2,)),
        ],
        compiler_params=pltpu.CompilerParams(vmem_limit_bytes=LIMIT),
        cost_estimate=pl.CostEstimate(
            flops=2 * jacobian.size, bytes_accessed=2 * jacobian.size, transcendentals=0
        ),
        name="first_push",
    )(tile_count, *held)


def sweep_step(kept, turned, tile_block, live, bias, step, friction, lam, parts, last):
    rows, dofs = parts[0].shape
    kept = pltpu.with_memory_space_constraint(kept, pltpu.VMEM)
    turned = pltpu.with_memory_space_constraint(turned, pltpu.VMEM)
    return pl.pallas_call(
        functools.partial(sweep_kernel, len(parts)),
        out_shape=result_shapes(lam, rows // 2, dofs),
        in_specs=[SMEM] + [VMEM] * (7 + len(parts)),
        out_specs=[pl.BlockSpec(memory_space=pl.ANY) if last else VMEM, VMEM],
        scratch_shapes=[
            pltpu.VMEM((rows, dofs), jnp.float32),
            pltpu.VMEM(lam.shape, jnp.float32),
        ]
        + ([pltpu.VMEM(lam.shape, jnp.float32), pltpu.SemaphoreType.DMA] if last else []),
        compiler_params=pltpu.CompilerParams(vmem_limit_bytes=LIMIT),
        cost_estimate=pl.CostEstimate(
            flops=4 * kept.size, bytes_accessed=4 * kept.size, transcendentals=0
        ),
        name="sweep_step",
    )(tile_block, live, kept, turned, bias, step, friction, lam, *parts)


def per_device(
    jacobian, tile_block, tile_count, vel_free, inv_mass, bias, step_scale, friction, impulse_start
):
    tiles, sides, dofs, rows = jacobian.shape
    blocks = vel_free.shape[0]
    flat = jacobian.reshape(tiles, sides * dofs, rows)
    even = (lax.axis_index("body") & 1) == 0
    even, tile_block = lax.optimization_barrier((even, tile_block.T))
    kept, turned, live, lam, sums = first_push(
        flat, tile_block, tile_count, impulse_start, blocks
    )
    share, mass_next = vel_free * (1.0 / pair_count()), None
    for sweep in range(ITERS):
        both = pair_sum(sums)
        own, later = both[:blocks], both[blocks:]
        extra = [rounded(inv_mass)] if mass_next is None else []
        from_last, from_next = traded(
            rounded(later), rounded(share + inv_mass * own), even, *extra
        )
        if mass_next is None:
            mass_next = from_next[blocks:].astype(jnp.float32)
        parts = over_pairs(
            jnp.concatenate(
                [share + inv_mass * (own + from_last), from_next[:blocks] + mass_next * later]
            )
        )
        lam, sums = sweep_step(
            kept, turned, tile_block, live, bias, step_scale, friction, lam, parts,
            last=sweep == ITERS - 1,
        )
    both = pair_sum(sums)
    from_last = crossed(rounded(both[blocks:]), ahead_of)
    total = tree([part.astype(jnp.float32) for part in over_pairs(both[:blocks] + from_last)])
    velocity = vel_free + inv_mass * total
    return (lam, velocity)


def solution(mesh):
    placed = (
        P(("contact", "body"), None, None, None),
        P(("contact", "body"), None),
        P(("contact", "body")),
        P("body", None),
        P("body", None),
        P(("contact", "body"), None),
        P(("contact", "body"), None),
        P(("contact", "body"), None),
        P(("contact", "body"), None),
    )
    return jax.shard_map(
        per_device,
        mesh=mesh,
        in_specs=placed,
        out_specs=(P(("contact", "body"), None), P("body", None)),
        check_vma=False,
    )
```

```python
import functools

import jax
import jax.numpy as jnp
from jax import lax
from jax.experimental import pallas as pl
from jax.experimental.pallas import tpu as pltpu
from jax.sharding import PartitionSpec as P

ITERS = 2


def crossed(value, target):
    count, groups = lax.axis_size("body"), lax.axis_size("contact")
    cross = 1 if groups % 2 == 0 else 0
    pairs = [
        (group * count + place, (group ^ cross) * count + target(place) % count)
        for group in range(groups)
        for place in range(count)
    ]
    return lax.ppermute(value, ("contact", "body"), pairs)


def ahead_of(place):
    return place + 1


def traded(ahead, back, even, *extra):
    both = lambda value: jnp.concatenate([value, *extra]) if extra else value
    if lax.axis_size("body") % 2:
        return crossed(ahead, ahead_of), crossed(both(back), lambda place: place - 1)
    far, close = lax.optimization_barrier(
        (both(jnp.where(even, back, ahead)), both(jnp.where(even, ahead, back)))
    )
    wide = crossed(far, lambda place: place + 2 * (place % 2) - 1)
    near = crossed(close, lambda place: place ^ 1)
    rows = ahead.shape[0]
    return jnp.where(even, wide[:rows], near[:rows]), jnp.where(even, near, wide)


def rounded(value):
    return value.astype(jnp.bfloat16)


def tree(values):
    while len(values) > 1:
        values = [left + right for left, right in zip(values[::2], values[1::2])]
    return values[0]


def pair_sum(value):
    count = lax.axis_size("contact")
    if count % 2:
        return value
    return value + lax.ppermute(value, "contact", [(place, place ^ 1) for place in range(count)])


def pair_count():
    count = lax.axis_size("contact")
    return count if count % 2 else count // 2


def over_pairs(value):
    count = lax.axis_size("contact")
    if count & (count - 1):
        mine = (lax.axis_index("contact") & 1) == 0
        return [lax.psum(value if count % 2 else jnp.where(mine, value, 0.0), "contact")]
    stride, parts = 2, [value]
    while stride < count:
        radix = min(count // stride, 4)
        value = rounded(tree([part.astype(jnp.float32) for part in parts]))
        parts = []
        for digit in range(1, radix):
            pairs = [(place, place ^ (digit * stride) ^ 1) for place in range(count)]
            parts.append(lax.ppermute(value, "contact", pairs))
        parts.append(value)
        stride *= radix
    return parts


def project(trial, friction, contacts):
    normal = trial[:, :contacts]
    first = trial[:, contacts : 2 * contacts]
    second = trial[:, 2 * contacts :]
    tangent = jnp.sqrt(first * first + second * second)
    inside = tangent <= friction * normal
    below = friction * tangent <= -normal
    moved = (normal + friction * tangent) / (1.0 + friction * friction)
    safe = jnp.where(inside | below, 1.0, tangent)
    factor = jnp.where(inside, 1.0, jnp.where(below, 0.0, friction * moved / safe))
    new_normal = jnp.where(inside, normal, jnp.where(below, 0.0, moved))
    return jnp.concatenate([new_normal, first * factor, second * factor], axis=1)


def push_tile(tile, lam_ref, turned_ref, block_ref, sums_ref):
    blocks, dofs = sums_ref.shape[0] // 2, sums_ref.shape[1]
    row = jnp.broadcast_to(lam_ref[pl.ds(tile, 1), :], (16, lam_ref.shape[1]))
    push = jnp.dot(
        row.astype(jnp.bfloat16), turned_ref[tile], preferred_element_type=jnp.float32
    )
    sums_ref[pl.ds(block_ref[0, tile], 1), :] += push[:1, :dofs]
    sums_ref[pl.ds(blocks + block_ref[1, tile], 1), :] += push[:1, dofs:]


def first_kernel(
    count_ref, block_ref, jac_ref, start_ref, kept_ref, turned_ref, live_ref, lam_ref, sums_ref,
    block, sems, small_sems,
):
    tiles = start_ref.shape[0]
    small = [
        pltpu.make_async_copy(source, target, small_sems.at[place])
        for place, (source, target) in enumerate(
            [(block_ref, block), (start_ref, lam_ref)]
        )
    ]
    groups = [range(first, min(first + GROUP, tiles)) for first in range(0, tiles, GROUP)]
    copies = [
        pltpu.make_async_copy(
            jac_ref.at[pl.ds(group[0], len(group))],
            kept_ref.at[pl.ds(group[0], len(group))],
            sems.at[place],
        )
        for place, group in enumerate(groups)
    ]
    for copy in small + copies[:AHEAD]:
        copy.start()
    sums_ref[...] = jnp.zeros_like(sums_ref)
    for copy in small:
        copy.wait()
    order = lax.broadcasted_iota(jnp.int32, lam_ref.shape, 0)
    live_ref[...] = jnp.where(order < count_ref[0], 1.0, 0.0)
    lam_ref[...] = lam_ref[...] * live_ref[...]
    for place, (group, before) in enumerate(zip(groups + [[]], [[]] + groups)):
        if group:
            copies[place].wait()
        for copy in copies[place + AHEAD : place + AHEAD + 1]:
            copy.start()
        for tile in group:
            turned_ref[tile] = kept_ref[tile].T
        for tile in before:
            push_tile(tile, lam_ref, turned_ref, block, sums_ref)


def sweep_kernel(
    parts, block_ref, live_ref, jac_ref, turned_ref, bias_ref, step_ref, friction_ref, old_ref, *refs
):
    part_refs, (out_ref, sums_ref, vel_ref, rel_ref, *held) = refs[:parts], refs[parts:]
    lam_ref = held[0] if held else out_ref
    tiles = old_ref.shape[0]
    blocks, dofs = vel_ref.shape[0] // 2, vel_ref.shape[1]
    vel_ref[...] = tree([ref[...].astype(jnp.float32) for ref in part_refs])
    sums_ref[...] = jnp.zeros_like(sums_ref)
    step = 8 if tiles % 8 == 0 else tiles
    halves = [range(first, first + step) for first in range(0, tiles, step)]

    def rel_tiles(half):
        for tile in half:
            own_row = vel_ref[pl.ds(block_ref[0, tile], 1), :]
            next_row = vel_ref[pl.ds(blocks + block_ref[1, tile], 1), :]
            row = jnp.broadcast_to(jnp.concatenate([own_row, next_row], axis=1), (16, 2 * dofs))
            rel = jnp.dot(
                row.astype(jnp.bfloat16), jac_ref[tile], preferred_element_type=jnp.float32
            )
            rel_ref[pl.ds(tile, 1), :] = rel[:1]

    def project_tiles(half):
        part = slice(half[0], half[-1] + 1)
        trial = old_ref[part] - step_ref[part] * (rel_ref[part] + bias_ref[part])
        lam = project(trial, friction_ref[part], friction_ref.shape[1])
        lam_ref[part] = lam * live_ref[part]

    rel_tiles(halves[0])
    copies = [pltpu.make_async_copy(lam_ref, out_ref, held[1])] if held else []
    for half, after in zip(halves, halves[1:] + [[]]):
        project_tiles(half)
        rel_tiles(after)
        if not after:
            for copy in copies:
                copy.start()
        for tile in half:
            push_tile(tile, lam_ref, turned_ref, block_ref, sums_ref)
    for copy in copies:
        copy.wait()


GROUP = 2
AHEAD = 4
LIMIT = 24 * 1024 * 1024
SMEM = pl.BlockSpec(memory_space=pltpu.SMEM)
VMEM = pl.BlockSpec(memory_space=pltpu.VMEM)


def result_shapes(lam, blocks, dofs):
    return [
        jax.ShapeDtypeStruct(lam.shape, jnp.float32),
        jax.ShapeDtypeStruct((2 * blocks, dofs), jnp.float32),
    ]


def first_push(jacobian, tile_block, tile_count, start, blocks):
    tiles, rows, cols = jacobian.shape
    lam_shape, sums_shape = result_shapes(start, blocks, rows // 2)
    held = [
        pltpu.with_memory_space_constraint(array, pltpu.HBM)
        for array in (tile_block, jacobian, start)
    ]
    return pl.pallas_call(
        first_kernel,
        out_shape=[
            pltpu.VMEM((tiles, rows, cols), jacobian.dtype),
            pltpu.VMEM((tiles, cols, rows), jacobian.dtype),
            lam_shape, lam_shape, sums_shape,
        ],
        in_specs=[SMEM] + [pl.BlockSpec(memory_space=pltpu.HBM)] * 3,
        out_specs=[VMEM] * 5,
        scratch_shapes=[
            pltpu.SMEM(tile_block.shape, jnp.int32),
            pltpu.SemaphoreType.DMA((tiles,)),
            pltpu.SemaphoreType.DMA((2,)),
        ],
        compiler_params=pltpu.CompilerParams(vmem_limit_bytes=LIMIT),
        cost_estimate=pl.CostEstimate(
            flops=2 * jacobian.size, bytes_accessed=2 * jacobian.size, transcendentals=0
        ),
        name="first_push",
    )(tile_count, *held)


def sweep_step(kept, turned, tile_block, live, bias, step, friction, lam, parts, last):
    rows, dofs = parts[0].shape
    kept = pltpu.with_memory_space_constraint(kept, pltpu.VMEM)
    turned = pltpu.with_memory_space_constraint(turned, pltpu.VMEM)
    return pl.pallas_call(
        functools.partial(sweep_kernel, len(parts)),
        out_shape=result_shapes(lam, rows // 2, dofs),
        in_specs=[SMEM] + [VMEM] * (7 + len(parts)),
        out_specs=[pl.BlockSpec(memory_space=pl.ANY) if last else VMEM, VMEM],
        scratch_shapes=[
            pltpu.VMEM((rows, dofs), jnp.float32),
            pltpu.VMEM(lam.shape, jnp.float32),
        ]
        + ([pltpu.VMEM(lam.shape, jnp.float32), pltpu.SemaphoreType.DMA] if last else []),
        compiler_params=pltpu.CompilerParams(vmem_limit_bytes=LIMIT),
        cost_estimate=pl.CostEstimate(
            flops=4 * kept.size, bytes_accessed=4 * kept.size, transcendentals=0
        ),
        name="sweep_step",
    )(tile_block, live, kept, turned, bias, step, friction, lam, *parts)


def per_device(
    jacobian, tile_block, tile_count, vel_free, inv_mass, bias, step_scale, friction, impulse_start
):
    tiles, sides, dofs, rows = jacobian.shape
    blocks = vel_free.shape[0]
    flat = jacobian.reshape(tiles, sides * dofs, rows)
    even = (lax.axis_index("body") & 1) == 0
    even, tile_block = lax.optimization_barrier((even, tile_block.T))
    kept, turned, live, lam, sums = first_push(
        flat, tile_block, tile_count, impulse_start, blocks
    )
    share, mass_next = vel_free * (1.0 / pair_count()), None
    for sweep in range(ITERS):
        both = pair_sum(sums)
        own, later = both[:blocks], both[blocks:]
        extra = [rounded(inv_mass)] if mass_next is None else []
        from_last, from_next = traded(
            rounded(later), rounded(share + inv_mass * own), even, *extra
        )
        if mass_next is None:
            mass_next = from_next[blocks:].astype(jnp.float32)
        parts = over_pairs(
            jnp.concatenate(
                [share + inv_mass * (own + from_last), from_next[:blocks] + mass_next * later]
            )
        )
        lam, sums = sweep_step(
            kept, turned, tile_block, live, bias, step_scale, friction, lam, parts,
            last=sweep == ITERS - 1,
        )
    both = pair_sum(sums)
    from_last = crossed(rounded(both[blocks:]), ahead_of)
    total = tree([part.astype(jnp.float32) for part in over_pairs(both[:blocks] + from_last)])
    velocity = vel_free + inv_mass * total
    return (lam, velocity)


def solution(mesh):
    placed = (
        P(("contact", "body"), None, None, None),
        P(("contact", "body"), None),
        P(("contact", "body")),
        P("body", None),
        P("body", None),
        P(("contact", "body"), None),
        P(("contact", "body"), None),
        P(("contact", "body"), None),
        P(("contact", "body"), None),
    )
    return jax.shard_map(
        per_device,
        mesh=mesh,
        in_specs=placed,
        out_specs=(P(("contact", "body"), None), P("body", None)),
        check_vma=False,
    )
```
